128 devices in a mesh: row: 8 (over x, core), col: 16 (over z, y).
Axes of the slice: x: 4, y: 4, z: 4, core: 2. Of those that a mesh axis runs over, the one named last changes fastest.
Arguments:
- right_side: float32 [4, 128, 512, 128], P(None, 'row', 'col'), may hold values from -8 to 8
- material: int32 [128, 512, 128], P('row', 'col'), may hold values 0 or 1
- reaction: float32 [4, 2], replicated, may hold values from 0.05 to 1
- coarse_inverse: float32 [4, 1024, 1024], P(None, ('row', 'col')), may hold values from -0.000100708008 to 0.02
Outputs:
- corrected: float32 [4, 128, 512, 128], P(None, 'row', 'col')
The draws below stay inside these ranges and needn't reach their ends.
All inputs are finite; a program needn't handle non-finite values. No bound on the sum of `material` on one device may be relied on, other than what follows from the above.
Results may differ from the reference program's by a relative error of at most 0.00007.
Values sent between devices are 32-bit elements; how exact they have to be, the bound alone decides.
No kernel may reach another device: no remote copies, remote signals or barrier semaphores. Data moves between devices by JAX's collectives and lax.ppermute only.
A program may use at most 128 MiB of HBM per device.

```python
import math
from functools import partial
import jax
import jax.numpy as jnp
from jax import lax

CX = 16
CY = 32
CZ = 128
FIELDS = 4
SWEEPS_FINE = 4
SWEEPS_COARSE = 4
ZC = 8
NX = 128
NY = 512
NZ = 128
COARSE = 1024
N_ROW = 8
N_COL = 16


def draw_coarse_inverse(key, part):
    key = jax.random.fold_in(key, 11)
    first_key, second_key = jax.random.split(key)
    scale = 0.4 / math.sqrt(CX * CY * CZ / (8.0 * ZC))
    leading = jax.random.uniform(first_key, (FIELDS, COARSE), jnp.float32, 0.5, 1.5)
    spread = jax.random.uniform(second_key, (FIELDS, COARSE, COARSE), jnp.float32, -1.0, 1.0) * (8.0 / COARSE)
    identity = jnp.eye(COARSE, dtype=jnp.float32)[None]
    return ((spread + identity * leading[:, :, None]) * scale).astype(jnp.float32)


def with_ends(array, stream_key, smallest, high):
    extent = array.shape
    place = [jax.random.randint(jax.random.fold_in(stream_key, axis), (), 0, extent[axis]) for axis in range(len(extent))]
    array = array.at[tuple(place)].set(smallest)
    longest = extent.index(max(extent))
    place[longest] = (place[longest] + 1) % extent[longest]
    return array.at[tuple(place)].set(high)


def level_of(rng, dims, cuts, least, largest):
    def one(axis_at, blocks):
        steps = jax.random.uniform(jax.random.fold_in(jax.random.fold_in(rng, 6), axis_at), (blocks,), jnp.float32, least / len(cuts), largest / len(cuts))
        return jnp.repeat(jnp.exp(steps), dims[axis_at] // blocks).reshape((-1,) + (1,) * (len(dims) - axis_at - 1))

    gain = one(*cuts[0])
    for cut in cuts[1:]:
        gain = gain * one(*cut)
    return gain


def bell_draw(rng, extent, width, bound, pieces=(), kind=jnp.bfloat16):
    values = jax.random.normal(rng, extent, jnp.float32) * width
    if len(pieces) > 0:
        values = level_of(rng, extent, pieces, -0.22, 0.18) * values
    return jnp.clip(values, min=-bound, max=bound).astype(kind)


def setup_inputs(seed: int = 0) -> dict:
    seeds = jax.random.split(jax.random.key(seed), 5)
    right_side = bell_draw(seeds[0], (FIELDS, NX, NY, NZ), 1.0, 8.0, ((1, 8), (2, 16)), jnp.float32)
    material = with_ends((jax.random.randint(seeds[1], (NX, NY, NZ), 0, 3) < 1).astype(jnp.int32), jax.random.fold_in(seeds[1], 1), 0, 1)
    reaction = jnp.clip(jnp.exp(jax.random.uniform(seeds[2], (FIELDS, 2), jnp.float32, math.log(0.05), math.log(1.0))), 0.05, 1.0)
    coarse_inverse = draw_coarse_inverse(jax.random.fold_in(seeds[4], 71), 0)
    return {"right_side": right_side, "material": material, "reaction": reaction, "coarse_inverse": coarse_inverse}


LOW_BOUND = 0.25
HIGH_BOUND = 2.0
THETA = (HIGH_BOUND + LOW_BOUND) / 2.0
DELTA = (HIGH_BOUND - LOW_BOUND) / 2.0


def cell_diagonal(reaction, material):
    base = reaction[:, 0][:, None, None, None]
    jump = (reaction[:, 1] - reaction[:, 0])[:, None, None, None]
    return 6.0 + base + jump * material.astype(jnp.float32)[None]


def operate(field, diagonal):
    padded = jnp.pad(field, ((0, 0), (1, 1), (1, 1), (1, 1)))
    beside = padded[:, 2:, 1:-1, 1:-1] + padded[:, :-2, 1:-1, 1:-1]
    beside = beside + padded[:, 1:-1, 2:, 1:-1] + padded[:, 1:-1, :-2, 1:-1]
    beside = beside + padded[:, 1:-1, 1:-1, 2:] + padded[:, 1:-1, 1:-1, :-2]
    return diagonal * field - beside


def restrict_sum(field):
    f, a, b, z = field.shape
    return field.reshape(f, a // 2, 2, b // 2, 2, z // 2, 2).sum(axis=(2, 4, 6))


def prolong(field):
    f, a, b, z = field.shape
    wide = jnp.broadcast_to(field[:, :, None, :, None, :, None], (f, a, 2, b, 2, z, 2))
    return wide.reshape(f, 2 * a, 2 * b, 2 * z)


def chebyshev(operator, diagonal, source, initial, sweeps):
    inverse = 1.0 / diagonal
    if initial is None:
        solution = jnp.zeros_like(source)
        residue = source
    else:
        solution = initial
        residue = source - operator(initial)
    update = inverse * residue / THETA
    damping = DELTA / THETA
    for sweep in range(sweeps):
        solution = solution + update
        if sweep + 1 < sweeps:
            residue = residue - operator(update)
            following = 1.0 / (2.0 * THETA / DELTA - damping)
            update = following * damping * update + (2.0 * following / DELTA) * inverse * residue
            damping = following
    return solution


def reference(right_side, material, reaction, coarse_inverse):
    diagonal = cell_diagonal(reaction, material)
    fine_operator = partial(operate, diagonal=diagonal)
    first = chebyshev(fine_operator, diagonal, right_side, None, SWEEPS_FINE)
    fine_residue = right_side - operate(first, diagonal)
    coarse_source = 0.5 * restrict_sum(fine_residue)
    coarse_diagonal = 6.0 + 0.5 * restrict_sum(diagonal - 6.0)
    coarse_operator = partial(operate, diagonal=coarse_diagonal)
    coarse_first = chebyshev(coarse_operator, coarse_diagonal, coarse_source, None, SWEEPS_COARSE)
    coarse_residue = coarse_source - operate(coarse_first, coarse_diagonal)
    fields, half_x, half_y, half_z = coarse_residue.shape
    grouped = (fields, N_ROW, half_x // N_ROW, N_COL, half_y // N_COL, ZC, half_z // ZC)
    coarsest = coarse_residue.reshape(grouped).sum(axis=(2, 4, 6)).reshape(fields, N_ROW * N_COL * ZC)
    correction = jnp.einsum("fic,fc->fi", coarse_inverse, coarsest, precision=lax.Precision.HIGHEST)
    spread = correction.reshape(fields, N_ROW, 1, N_COL, 1, ZC, 1)
    coarse_second = (coarse_first.reshape(grouped) + spread).reshape(coarse_first.shape)
    coarse_final = chebyshev(coarse_operator, coarse_diagonal, coarse_source, coarse_second, SWEEPS_COARSE)
    second = first + prolong(coarse_final)
    return chebyshev(fine_operator, diagonal, right_side, second, SWEEPS_FINE)
```

```python
import functools

import jax
import jax.numpy as jnp
from jax import lax
from jax.experimental import pallas as pl
from jax.experimental.pallas import tpu as pltpu
from jax.sharding import PartitionSpec as P

FIELDS = 4
CX, CY, CZ = 16, 32, 128
HX, HY = CX // 2, CY // 2
GROUPS = 8
SWEEPS = 4
LOW_BOUND = 0.25
HIGH_BOUND = 2.0
THETA = (HIGH_BOUND + LOW_BOUND) / 2.0
DELTA = (HIGH_BOUND - LOW_BOUND) / 2.0

FX, FY, FO = CX + 8, CY + 32, 16
QX, QY, QO = HX + 18, HY + 32, 16
EX = HX + 12
CORNER_AT = {1: 0, 2: 8, 3: 16, 9: 23, 4: 24, 8: 30, 5: 32, 7: 37, 6: 40}
CORNER_LINES = 48


def corner_size(j):
    return min(HX, 10 - j)


def coefficients():
    rho = DELTA / THETA
    pairs = []
    for _ in range(SWEEPS - 1):
        following = 1.0 / (2.0 * THETA / DELTA - rho)
        pairs.append((following * rho, 2.0 * following / DELTA))
        rho = following
    return pairs


def lanes():
    return lax.broadcasted_iota(jnp.int32, (1, CZ), 1)


def beside(ref, f, x, low, count, width):
    here = ref[f, x, low : low + count, :]
    lane = lanes()
    total = ref[f, x + 1, low : low + count, :] + ref[f, x - 1, low : low + count, :]
    total = total + ref[f, x, low + 1 : low + 1 + count, :]
    total = total + ref[f, x, low - 1 : low - 1 + count, :]
    total = total + jnp.where(lane < CZ - width, pltpu.roll(here, CZ - width, 1), 0.0)
    total = total + jnp.where(lane >= width, pltpu.roll(here, width, 1), 0.0)
    return here, total


def diagonal_values(reaction, f):
    low = reaction[f, 0]
    jump = reaction[f, 1] - low
    return 6.0 + low, 6.0 + low + jump


def inverse_of(code, reaction, f):
    fluid, solid = diagonal_values(reaction, f)
    ones = jnp.ones((8, CZ), jnp.float32)
    fluid, solid = (ones / (ones * fluid))[:1], (ones / (ones * solid))[:1]
    return jnp.where(code == 0.0, fluid, jnp.where(code == 1.0, solid, 0.0))


def place():
    return lax.axis_index("row"), lax.axis_index("col")


def pack_layers(b, material, up, down, right, left):
    for f in range(FIELDS + 1):
        if f < FIELDS:
            take = lambda start, size, step: b[f, pl.ds(start, size, stride=step), :]
        else:
            take = lambda start, size, step: material[pl.ds(start, size, stride=step), :].astype(
                jnp.float32
            )
        for i in range(4):
            up[f, i] = take((CX - 4 + i) * CY, CY, 1)
            down[f, i] = take(i * CY, CY, 1)
            right[f, i] = take(CY - 4 + i, CX, CY)
            left[f, i] = take(i, CX, CY)


def pack_corners(low, high, up, down):
    for f in range(FIELDS + 1):
        for side, (ref, rows) in enumerate(((low, (3, 2, 1)), (high, (0, 1, 2)))):
            at = 8 * side
            for j, row in enumerate(rows):
                size = 3 - j
                up[f, at : at + size, :] = ref[f, row, CX - size : CX, :]
                down[f, at : at + size, :] = ref[f, row, 0:size, :]
                at += size
            up[f, at : at + 2, :] = jnp.zeros((2, CZ), jnp.float32)
            down[f, at : at + 2, :] = jnp.zeros((2, CZ), jnp.float32)


def smooth_first(
    nrow, ncol, reaction, b, material, above, below, low, high, kabove, kbelow,
    first, scaled, code, coarse, up, down, right, left,
    s, inv, p0, p1, p2, p3, pair,
):
    row, col = place()
    parts = (p0, p1, p2, p3)
    zeros = jnp.zeros((FY, CZ), jnp.float32)
    for x in (*range(4), *range(FX - 4, FX)):
        for f in range(FIELDS):
            s[f, x] = zeros
        code[x] = zeros + 2.0

    def own(i, carry):
        x = i + 4
        for f in range(FIELDS):
            s[f, x, 8:16, :] = zeros[:8]
            s[f, x, 16:48, :] = b[f, pl.ds(pl.multiple_of(i * CY, CY), CY), :]
            s[f, x, 48:56, :] = zeros[:8]
        code[x, 0:16, :] = zeros[:16] + 2.0
        code[x, 16:48, :] = material[pl.ds(pl.multiple_of(i * CY, CY), CY), :].astype(jnp.float32)
        code[x, 48:64, :] = zeros[:16] + 2.0
        return carry

    lax.fori_loop(0, CX, own, 0, unroll=2)
    sflat = s.reshape(FIELDS, FX * FY, CZ)
    cflat = code.reshape(FX * FY, CZ)

    def put(f, start, size, value):
        if f < FIELDS:
            sflat[f, pl.ds(start, size, stride=FY), :] = value
        else:
            cflat[pl.ds(start, size, stride=FY), :] = value

    def rows(first_x, ref):
        for i in range(4):
            for f in range(FIELDS):
                s[f, first_x + i, 16:48, :] = ref[f, i]
            code[first_x + i, 16:48, :] = ref[FIELDS, i]

    @pl.when(row > 0)
    def _():
        rows(0, above)

    @pl.when(row < nrow - 1)
    def _():
        rows(FX - 4, below)

    @pl.when(col > 0)
    def _():
        for f in range(FIELDS + 1):
            for i in range(4):
                put(f, 4 * FY + FO - 4 + i, CX, low[f, i])

    @pl.when(col < ncol - 1)
    def _():
        for f in range(FIELDS + 1):
            for i in range(4):
                put(f, 4 * FY + FO + CY + i, CX, high[f, i])

    def corners(ref, is_above, is_high):
        for f in range(FIELDS + 1):
            at = 8 * is_high
            for j in range(3):
                size = 3 - j
                x = 4 - size if is_above else 4 + CX
                y = FO + CY + j if is_high else FO - 1 - j
                put(f, x * FY + y, size, ref[f, at : at + size, :])
                at += size

    for ref, is_above, in_x in ((kabove, 1, row > 0), (kbelow, 0, row < nrow - 1)):
        for is_high, in_y in ((0, col > 0), (1, col < ncol - 1)):
            pl.when(in_x & in_y)(functools.partial(corners, ref, is_above, is_high))

    def scale(x, carry):
        kind = code[x, 8:56, :]
        for f in range(FIELDS):
            inverse = inverse_of(kind, reaction, f)
            value = inverse * s[f, x, 8:56, :]
            inv[f, x, 8:56, :] = inverse
            s[f, x, 8:56, :] = value
            p0[f, x, 8:56, :] = value * (1.0 / THETA)
        return carry

    lax.fori_loop(0, FX, scale, 0)

    for k, (keep, gain) in enumerate(coefficients()):
        def sweep(x, carry):
            for f in range(FIELDS):
                here, total = beside(parts[k], f, x, 8, 48, 1)
                value = s[f, x, 8:56, :] - here + inv[f, x, 8:56, :] * total
                s[f, x, 8:56, :] = value
                parts[k + 1][f, x, 8:56, :] = keep * here + gain * value
            return carry

        lax.fori_loop(k + 1, FX - k - 1, sweep, 0)

    parity = lanes() % 2 == 0

    def finish(i, carry):
        at_y = pl.multiple_of(i * 2 * CY, 2 * CY)
        sums = []
        for f in range(FIELDS):
            fluid, solid = diagonal_values(reaction, f)
            residue = jnp.zeros((CY, CZ), jnp.float32)
            for h in range(2):
                x = i * 2 + h + 4
                here, total = beside(p3, f, x, 16, CY, 1)
                value = s[f, x, 16:48, :] - here + inv[f, x, 16:48, :] * total
                out = pl.ds(at_y + h * CY, CY)
                scaled[f, out, :] = value
                first[f, out, :] = (
                    p0[f, x, 16:48, :] + p1[f, x, 16:48, :] + p2[f, x, 16:48, :] + here
                )
                residue = residue + jnp.where(code[x, 16:48, :] == 1.0, solid, fluid) * value
            sums.append(residue)
        sums.append(code[i * 2 + 4, 16:48, :] + code[i * 2 + 5, 16:48, :])
        halves = []
        for f, value in enumerate(sums):
            pair[f] = value
            halves.append(pair[f, pl.ds(0, HY, stride=2), :] + pair[f, pl.ds(1, HY, stride=2), :])
        halves.append(halves[4])
        out = pl.ds(pl.multiple_of(i * HY, HY), HY)
        for plane in range(3):
            even, odd = halves[2 * plane], halves[2 * plane + 1]
            merged = jnp.where(
                parity, even + pltpu.roll(even, CZ - 1, 1), odd + pltpu.roll(odd, 1, 1)
            )
            coarse[plane, out, :] = merged * 0.5 if plane < 2 else merged
        return carry

    lax.fori_loop(0, HX, finish, 0)

    for f in range(FIELDS):
        for i in range(3):
            up[f, i] = scaled[f, pl.ds((CX - 3 + i) * CY, CY), :]
            down[f, i] = scaled[f, pl.ds(i * CY, CY), :]
            at = 27 * HX + (f * 3 + i) * CX
            right[at : at + CX, :] = scaled[f, pl.ds(CY - 3 + i, CX, stride=CY), :]
            left[at : at + CX, :] = scaled[f, pl.ds(i, CX, stride=CY), :]
    for plane in range(3):
        for i in range(9):
            at = (plane * 9 + i) * HX
            right[at : at + HX, :] = coarse[plane, pl.ds(HY - 9 + i, HX, stride=HY), :]
            left[at : at + HX, :] = coarse[plane, pl.ds(i, HX, stride=HY), :]


SIDE_LINES = 27 * HX + 12 * CX
KNOT_LINES = 6 * CORNER_LINES + FIELDS * 8
EDGE_LINES = 3 * 24


def pack_knots(coarse, low, high, up, down, far_up, far_down):
    for plane in range(3):
        base = plane * 24
        far_up[base : base + HY, :] = coarse[plane, (HX - 1) * HY : HX * HY, :]
        far_down[base : base + HY, :] = coarse[plane, 0:HY, :]
        far_up[base + HY : base + 24, :] = jnp.zeros((8, CZ), jnp.float32)
        far_down[base + HY : base + 24, :] = jnp.zeros((8, CZ), jnp.float32)
        for side, ref in enumerate((low, high)):
            line = (plane * 9 + (0 if side else 8)) * HX
            at = base + HY + side
            far_up[at : at + 1, :] = ref[line + HX - 1 : line + HX, :]
            far_down[at : at + 1, :] = ref[line : line + 1, :]
            base_at = (plane * 2 + side) * CORNER_LINES
            up[base_at + 40 : base_at + 48, :] = jnp.zeros((8, CZ), jnp.float32)
            down[base_at + 40 : base_at + 48, :] = jnp.zeros((8, CZ), jnp.float32)
            for j, offset in CORNER_AT.items():
                size = corner_size(j)
                line = (plane * 9 + (j - 1 if side else 9 - j)) * HX
                at = base_at + offset
                up[at : at + size, :] = ref[line + HX - size : line + HX, :]
                down[at : at + size, :] = ref[line : line + size, :]
    for f in range(FIELDS):
        base = 6 * CORNER_LINES + f * 8
        up[base : base + 8, :] = jnp.zeros((8, CZ), jnp.float32)
        down[base : base + 8, :] = jnp.zeros((8, CZ), jnp.float32)
        for side, ref in enumerate((low, high)):
            for j in range(2):
                size = 2 - j
                line = 27 * HX + (f * 3 + (j if side else 2 - j)) * CX
                at = base + side * 4 + 2 * j
                up[at : at + size, :] = ref[line + CX - size : line + CX, :]
                down[at : at + size, :] = ref[line : line + size, :]


def coarse_constants(reaction, plane):
    parity = lanes() % 2 == 0
    low = jnp.where(parity, reaction[2 * plane, 0], reaction[2 * plane + 1, 0])
    jump = jnp.where(
        parity,
        reaction[2 * plane, 1] - reaction[2 * plane, 0],
        reaction[2 * plane + 1, 1] - reaction[2 * plane + 1, 0],
    )
    return 8.0 * low, jump


def smooth_coarse(
    nrow, ncol, reaction, coarse, above, below, low, high, kabove, kbelow, far_above, far_below,
    start, scaled, inverse_out, sums,
    s, inv, count, p0, p1, p2, p3,
):
    row, col = place()
    parts = (p0, p1, p2, p3)
    zeros = jnp.zeros((QY, CZ), jnp.float32)

    def clear(x, carry):
        for plane in range(2):
            s[plane, x] = zeros
        count[x] = zeros - 1.0
        return carry

    lax.fori_loop(0, QX, clear, 0)
    sflat = s.reshape(2, QX * QY, CZ)
    cflat = count.reshape(QX * QY, CZ)

    def put(plane, start_row, size, value):
        if plane < 2:
            sflat[plane, pl.ds(start_row, size, stride=QY), :] = value
        else:
            cflat[pl.ds(start_row, size, stride=QY), :] = value

    def block(plane, x, value):
        if plane < 2:
            s[plane, x, QO : QO + HY, :] = value
        else:
            count[x, QO : QO + HY, :] = value

    def rows(first_x, ref):
        for plane in range(3):
            for i in range(HX):
                block(plane, first_x + i, ref[plane, i * HY : (i + 1) * HY, :])

    rows(9, coarse)

    @pl.when(row > 0)
    def _():
        rows(1, above)

    @pl.when(row < nrow - 1)
    def _():
        rows(9 + HX, below)

    def edge(ref, x):
        for plane in range(3):
            base = plane * 24
            block(plane, x, ref[base : base + HY, :])
            for is_high, in_y in ((0, col > 0), (1, col < ncol - 1)):
                @pl.when(in_y)
                def _():
                    y = QO + HY if is_high else QO - 1
                    at = base + HY + is_high
                    put(plane, x * QY + y, 1, ref[at : at + 1, :])

    pl.when(row > 1)(functools.partial(edge, far_above, 0))
    pl.when(row < nrow - 2)(functools.partial(edge, far_below, QX - 1))

    def side(ref, first_y):
        for plane in range(3):
            for i in range(9):
                line = (plane * 9 + i) * HX
                put(plane, 9 * QY + first_y + i, HX, ref[line : line + HX, :])

    pl.when(col > 0)(functools.partial(side, low, QO - 9))
    pl.when(col < ncol - 1)(functools.partial(side, high, QO + HY))

    def corners(ref, is_above, is_high):
        for plane in range(3):
            base = (plane * 2 + is_high) * CORNER_LINES
            for j, at in CORNER_AT.items():
                size = corner_size(j)
                x = 9 - size if is_above else 9 + HX
                y = QO + HY - 1 + j if is_high else QO - j
                put(plane, x * QY + y, size, ref[base + at : base + at + size, :])

    for ref, is_above, in_x in ((kabove, 1, row > 0), (kbelow, 0, row < nrow - 1)):
        for is_high, in_y in ((0, col > 0), (1, col < ncol - 1)):
            pl.when(in_x & in_y)(functools.partial(corners, ref, is_above, is_high))

    def scale(x, carry):
        number = count[x]
        for plane in range(2):
            low8, jump = coarse_constants(reaction, plane)
            inverse = jnp.where(number < 0.0, 0.0, 1.0 / (6.0 + 0.5 * (low8 + jump * number)))
            value = inverse * s[plane, x]
            inv[plane, x] = inverse
            s[plane, x] = value
            p0[plane, x] = value * (1.0 / THETA)
        return carry

    lax.fori_loop(0, QX, scale, 0)

    for k, (keep, gain) in enumerate(coefficients()):
        def sweep(x, carry):
            for plane in range(2):
                here, total = beside(parts[k], plane, x, 8, 32, 2)
                value = s[plane, x, 8:40, :] - here + inv[plane, x, 8:40, :] * total
                s[plane, x, 8:40, :] = value
                parts[k + 1][plane, x, 8:40, :] = keep * here + gain * value
            return carry

        lax.fori_loop(k + 1, QX - k - 1, sweep, 0)

    def finish(x, carry):
        for plane in range(2):
            here, total = beside(p3, plane, x, 8, 32, 2)
            value = s[plane, x, 8:40, :] - here + inv[plane, x, 8:40, :] * total
            scaled[plane, x - 4] = value
            inverse_out[plane, x - 4] = inv[plane, x, 8:40, :]
        return carry

    lax.fori_loop(4, QX - 4, finish, 0)

    def add(x, carry):
        for plane in range(2):
            start[plane, x - 7] = (
                p0[plane, x, 8:40, :] + p1[plane, x, 8:40, :]
                + p2[plane, x, 8:40, :] + p3[plane, x, 8:40, :]
            )
        return carry

    lax.fori_loop(7, QX - 7, add, 0)

    lane = lanes()
    message = jnp.zeros((8, CZ), jnp.float32)
    for plane in range(2):
        low8, jump = coarse_constants(reaction, plane)
        total = jnp.zeros((HY, CZ), jnp.float32)
        for x in range(9, 9 + HX):
            diagonal = 6.0 + 0.5 * (low8 + jump * count[x, QO : QO + HY, :])
            total = total + diagonal * scaled[plane, x - 4, 8 : 8 + HY, :]
        total = total[:8] + total[8:]
        for shift in (4, 2, 1):
            total = total + pltpu.roll(total, shift, 0)
        for shift in (2, 4, 8):
            total = total + pltpu.roll(total, CZ - shift, 1)
        for odd in range(2):
            for g in range(GROUPS):
                to = (2 * plane + odd) * GROUPS + g
                moved = pltpu.roll(total, (to - 16 * g - odd) % CZ, 1)
                message = jnp.where(lane == to, moved, message)
    sums[...] = jnp.broadcast_to(message[:1], sums.shape)


def smooth_second(
    nrow, ncol, reaction, gathered, mine, kin_above, kin_below, kin_low, kin_high,
    start, qscaled, qinverse, first, scaled, code, above, below, low, high, kabove, kbelow,
    out,
    wide, spread, e, q0, q1, q2, q3, qs, fs, inv, f0, p0, p1, p2, p3,
):
    row, col = place()
    lane = lanes()
    width = ncol * GROUPS
    fields = [jnp.zeros((nrow, CZ), jnp.float32) for _ in range(FIELDS)]
    for c in range(ncol):
        some = gathered[pl.ds(c, nrow, stride=ncol), :]
        for f in range(FIELDS):
            moved = pltpu.roll(some, (c * GROUPS - f * GROUPS) % CZ, 1)
            here = (lane >= c * GROUPS) & (lane < (c + 1) * GROUPS)
            fields[f] = jnp.where(here, moved, fields[f])
    for f in range(FIELDS):
        wide[f] = fields[f]

    group = lax.broadcasted_iota(jnp.int32, (GROUPS, CZ), 0)
    spot = lax.broadcasted_iota(jnp.int32, (GROUPS, CZ), 1)
    mask = [(spot // 16 == group) & (spot % 2 == odd) for odd in range(2)]
    e[...] = jnp.zeros_like(e)

    def product(rows_of, f):
        total = jnp.zeros((GROUPS, width), jnp.float32)
        for k in range(nrow):
            total = total + rows_of(f, k) * wide[f, k : k + 1, 0:width]
        return jnp.sum(total, axis=1, keepdims=True)

    def neighbour(rows_of, dx, dy):
        for plane in range(2):
            even = product(rows_of, 2 * plane)
            odd = product(rows_of, 2 * plane + 1)
            full = jnp.where(mask[0], even, jnp.where(mask[1], odd, 0.0))
            line = jnp.sum(full, axis=0, keepdims=True)
            x_from, x_to = {-1: (0, 6), 0: (6, 6 + HX), 1: (6 + HX, EX)}[dx]
            y_from, y_to = {-1: (8, QO), 0: (QO, QO + HY), 1: (QO + HY, QO + HY + 8)}[dy]
            for x in range(x_from, x_to):
                e[plane, x, y_from:y_to, :] = jnp.broadcast_to(line, (y_to - y_from, CZ))

    def slab(ref, part):
        if part is None:
            return lambda f, k: ref[f, :, k * width : (k + 1) * width]
        return lambda f, k: ref[part, f, :, k * width : (k + 1) * width]

    neighbour(slab(mine, None), 0, 0)
    in_x = {-1: row > 0, 1: row < nrow - 1}
    in_y = {-1: col > 0, 1: col < ncol - 1}
    pl.when(in_x[-1])(functools.partial(neighbour, slab(kin_above, None), -1, 0))
    pl.when(in_x[1])(functools.partial(neighbour, slab(kin_below, None), 1, 0))
    for dy, ref in ((-1, kin_low), (1, kin_high)):
        pl.when(in_y[dy])(functools.partial(neighbour, slab(ref, 0), 0, dy))
        for part, dx in ((1, -1), (2, 1)):
            pl.when(in_y[dy] & in_x[dx])(
                functools.partial(neighbour, slab(ref, part), dx, dy)
            )

    parts = (q0, q1, q2, q3)

    def begin(x, carry):
        for plane in range(2):
            here, total = beside(e, plane, x, 8, 32, 2)
            value = qscaled[plane, x - 1] - here + qinverse[plane, x - 1] * total
            qs[plane, x] = value
            q0[plane, x, 8:40, :] = value * (1.0 / THETA)
        return carry

    lax.fori_loop(1, EX - 1, begin, 0)
    for k, (keep, gain) in enumerate(coefficients()):
        def sweep(x, carry):
            for plane in range(2):
                here, total = beside(parts[k], plane, x, 8, 32, 2)
                value = qs[plane, x] - here + qinverse[plane, x - 1] * total
                qs[plane, x] = value
                parts[k + 1][plane, x, 8:40, :] = keep * here + gain * value
            return carry

        lax.fori_loop(k + 2, EX - k - 2, sweep, 0)

    parity = lane % 2 == 0

    def lift(i, carry):
        for plane in range(2):
            total = start[plane, i] + e[plane, i + 4, 8:40, :]
            total = total + q0[plane, i + 4, 8:40, :] + q1[plane, i + 4, 8:40, :]
            total = total + q2[plane, i + 4, 8:40, :] + q3[plane, i + 4, 8:40, :]
            for odd in range(2):
                if odd:
                    value = jnp.where(parity, pltpu.roll(total, CZ - 1, 1), total)
                else:
                    value = jnp.where(parity, total, pltpu.roll(total, 1, 1))
                spread[...] = value
                some = spread[4:28, :]
                for h in range(2):
                    for y in range(2):
                        f0[2 * plane + odd, i * 2 + h, pl.ds(8 + y, 24, stride=2), :] = some
        return carry

    lax.fori_loop(0, HX + 4, lift, 0)

    zeros = jnp.zeros((FY, CZ), jnp.float32)
    for x in (*range(4), *range(FX - 4, FX)):
        for f in range(FIELDS):
            fs[f, x] = zeros

    def own(i, carry):
        for f in range(FIELDS):
            fs[f, i + 4, 8:16, :] = zeros[:8]
            fs[f, i + 4, 16:48, :] = scaled[f, pl.ds(pl.multiple_of(i * CY, CY), CY), :]
            fs[f, i + 4, 48:56, :] = zeros[:8]
        return carry

    lax.fori_loop(0, CX, own, 0, unroll=2)
    sflat = fs.reshape(FIELDS, FX * FY, CZ)

    def rows(first_x, ref):
        for f in range(FIELDS):
            for i in range(3):
                fs[f, first_x + i, 16:48, :] = ref[f, i]

    pl.when(in_x[-1])(functools.partial(rows, 1, above))
    pl.when(in_x[1])(functools.partial(rows, 4 + CX, below))

    def side(ref, first_y):
        for f in range(FIELDS):
            for i in range(3):
                line = 27 * HX + (f * 3 + i) * CX
                sflat[f, pl.ds(4 * FY + first_y + i, CX, stride=FY), :] = ref[line : line + CX, :]

    pl.when(in_y[-1])(functools.partial(side, low, FO - 3))
    pl.when(in_y[1])(functools.partial(side, high, FO + CY))

    def corners(ref, is_above, is_high):
        for f in range(FIELDS):
            base = 6 * CORNER_LINES + f * 8 + is_high * 4
            for j in range(2):
                size = 2 - j
                x = 4 - size if is_above else 4 + CX
                y = FO + CY + j if is_high else FO - 1 - j
                at = base + 2 * j
                sflat[f, pl.ds(x * FY + y, size, stride=FY), :] = ref[at : at + size, :]

    for ref, is_above, dx in ((kabove, 1, -1), (kbelow, 0, 1)):
        for is_high, dy in ((0, -1), (1, 1)):
            pl.when(in_x[dx] & in_y[dy])(functools.partial(corners, ref, is_above, is_high))

    parts = (p0, p1, p2, p3)

    def open_fine(x, carry):
        kind = code[x, 8:56, :]
        for f in range(FIELDS):
            here, total = beside(f0, f, x, 8, 48, 1)
            inverse = inverse_of(kind, reaction, f)
            inv[f, x, 8:56, :] = inverse
            value = fs[f, x, 8:56, :] - here + inverse * total
            fs[f, x, 8:56, :] = value
            p0[f, x, 8:56, :] = value * (1.0 / THETA)
        return carry

    lax.fori_loop(1, FX - 1, open_fine, 0)
    for k, (keep, gain) in enumerate(coefficients()[:2]):
        def sweep(x, carry):
            for f in range(FIELDS):
                here, total = beside(parts[k], f, x, 8, 48, 1)
                value = fs[f, x, 8:56, :] - here + inv[f, x, 8:56, :] * total
                fs[f, x, 8:56, :] = value
                parts[k + 1][f, x, 8:56, :] = keep * here + gain * value
            return carry

        lax.fori_loop(k + 2, FX - k - 2, sweep, 0)

    keep, gain = coefficients()[2]

    def close(i, carry):
        x = i + 4
        at = pl.ds(pl.multiple_of(i * CY, CY), CY)
        for f in range(FIELDS):
            here, total = beside(p2, f, x, 16, CY, 1)
            value = fs[f, x, 16:48, :] - here + inv[f, x, 16:48, :] * total
            result = first[f, at, :] + f0[f, x, 16:48, :] + p0[f, x, 16:48, :]
            result = result + p1[f, x, 16:48, :] + here
            out[f, at, :] = result + (keep * here + gain * value)
        return carry

    lax.fori_loop(0, CX, close, 0)


def call(kernel, out_shapes, scratch, *args, smem=0, limit=40):
    vmem = pl.BlockSpec(memory_space=pltpu.VMEM)
    specs = [pl.BlockSpec(memory_space=pltpu.SMEM)] * smem + [vmem] * (len(args) - smem)
    return pl.pallas_call(
        kernel,
        out_shape=[jax.ShapeDtypeStruct(shape, jnp.float32) for shape in out_shapes],
        in_specs=specs,
        out_specs=[vmem] * len(out_shapes),
        scratch_shapes=[pltpu.VMEM(shape, jnp.float32) for shape in scratch],
        compiler_params=pltpu.CompilerParams(vmem_limit_bytes=limit * 1024 * 1024),
    )(*args)


def ahead(value, axis, steps=1):
    count = lax.axis_size(axis)
    return lax.ppermute(value, axis, [(i, (i + steps) % count) for i in range(count)])


def back(value, axis, steps=1):
    count = lax.axis_size(axis)
    return lax.ppermute(value, axis, [((i + steps) % count, i) for i in range(count)])


def body(right_side, material, reaction, coarse_inverse):
    nrow, ncol = lax.axis_size("row"), lax.axis_size("col")
    b = right_side.reshape(FIELDS, CX * CY, CZ)
    material = material.reshape(CX * CY, CZ)

    x_layer, y_layer = (FIELDS + 1, 4, CY, CZ), (FIELDS + 1, 4, CX, CZ)
    up, down, right, left = call(
        pack_layers, [x_layer, x_layer, y_layer, y_layer], [], b, material
    )
    above, below = ahead(up, "row"), back(down, "row")
    low, high = ahead(right, "col"), back(left, "col")
    up, down = call(pack_corners, [(FIELDS + 1, 16, CZ)] * 2, [], low, high)
    kabove, kbelow = ahead(up, "row"), back(down, "row")

    kin_above, kin_below = ahead(coarse_inverse, "row"), back(coarse_inverse, "row")
    kin = jnp.stack([coarse_inverse, kin_above, kin_below])
    kin_low, kin_high = ahead(kin, "col"), back(kin, "col")

    fine = (FIELDS, CX * CY, CZ)
    padded = (FIELDS, FX, FY, CZ)
    x_layer = (FIELDS, 3, CY, CZ)
    first, scaled, code, coarse, up, down, right, left = call(
        functools.partial(smooth_first, nrow, ncol),
        [fine, fine, padded[1:], (3, HX * HY, CZ), x_layer, x_layer]
        + [(SIDE_LINES, CZ)] * 2,
        [padded] * 6 + [(FIELDS + 1, CY, CZ)],
        reaction, b, material, above, below, low, high, kabove, kbelow,
        smem=1,
    )

    qabove, qbelow = ahead(coarse, "row"), back(coarse, "row")
    low, high = ahead(right, "col"), back(left, "col")
    above, below = ahead(up, "row"), back(down, "row")
    up, down, far_up, far_down = call(
        pack_knots, [(KNOT_LINES, CZ)] * 2 + [(EDGE_LINES, CZ)] * 2, [], coarse, low, high
    )
    kabove, kbelow = ahead(up, "row"), back(down, "row")
    far_above, far_below = ahead(far_up, "row", 2), back(far_down, "row", 2)

    qpadded = (2, QX, QY, CZ)
    start, qscaled, qinverse, sums = call(
        functools.partial(smooth_coarse, nrow, ncol),
        [(2, HX + 4, 32, CZ), (2, HX + 10, 32, CZ), (2, HX + 10, 32, CZ), (nrow * ncol, CZ)],
        [qpadded, qpadded, qpadded[1:]] + [qpadded] * 4,
        reaction, coarse, qabove, qbelow, low, high, kabove, kbelow, far_above, far_below,
        smem=1,
    )

    gathered = lax.all_to_all(sums, ("row", "col"), 0, 0)

    epadded = (2, EX, QY, CZ)
    (out,) = call(
        functools.partial(smooth_second, nrow, ncol),
        [fine],
        [(FIELDS, nrow, CZ), (32, CZ)] + [epadded] * 5 + [(2, EX, 32, CZ)] + [padded] * 7,
        reaction, gathered, coarse_inverse, kin_above, kin_below, kin_low, kin_high,
        start, qscaled, qinverse, first, scaled, code, above, below, low, high, kabove, kbelow,
        smem=1, limit=48,
    )
    return out.reshape(right_side.shape)


def solution(mesh):
    placed = (
        P(None, "row", "col", None),
        P("row", "col", None),
        P(),
        P(None, ("row", "col"), None),
    )
    return jax.shard_map(
        body, mesh=mesh, in_specs=placed, out_specs=P(None, "row", "col", None), check_vma=False
    )
```

```python
import functools

import jax
import jax.numpy as jnp
from jax import lax
from jax.experimental import pallas as pl
from jax.experimental.pallas import tpu as pltpu
from jax.sharding import PartitionSpec as P

FIELDS = 4
CX, CY, CZ = 16, 32, 128
HX, HY = CX // 2, CY // 2
GROUPS = 8
SWEEPS = 4
LOW_BOUND = 0.25
HIGH_BOUND = 2.0
THETA = (HIGH_BOUND + LOW_BOUND) / 2.0
DELTA = (HIGH_BOUND - LOW_BOUND) / 2.0

WX = CX + 4
GX, FY, FO = CX + 12, CY + 32, 16
FX = CX + 8
VX = HX + 2
QX, QY, QO = HX + 18, HY + 32, 16
EX = HX + 12
CORNER_AT = {1: 0, 2: 9, 3: 17, 4: 24, 5: 30, 6: 35, 7: 39, 8: 42, 9: 44}
CORNER_LINES = 48
FINE_CORNER_AT = {1: 0, 2: 5, 3: 9, 4: 12}

LAYER_LINES = (FIELDS + 1) * 6 * CY
BAND_LINES = (FIELDS + 1) * 4 * CX
KIN_LINES = FIELDS * GROUPS * 8
COARSE_LINES = 3 * (HX + 1) * HY
FACE_LINES = COARSE_LINES + FIELDS * CY
STRIP_LINES = 272
STRIP_AT = {1: 0, 2: WX, 3: 2 * WX - 2}
SIDE_LINES = STRIP_LINES + FIELDS * (3 * WX - 6)
KNOT_LINES = 6 * CORNER_LINES


def coefficients():
    rho = DELTA / THETA
    pairs = []
    for _ in range(SWEEPS - 1):
        following = 1.0 / (2.0 * THETA / DELTA - rho)
        pairs.append((following * rho, 2.0 * following / DELTA))
        rho = following
    return pairs


def every(low, high, step):
    for i in range(low, high):
        step(i)


def lanes():
    return lax.broadcasted_iota(jnp.int32, (1, CZ), 1)


def beside(ref, f, x, low, count, width):
    here = ref[f, x, low : low + count, :]
    lane = lanes()
    total = ref[f, x + 1, low : low + count, :] + ref[f, x - 1, low : low + count, :]
    total = total + ref[f, x, low + 1 : low + 1 + count, :]
    total = total + ref[f, x, low - 1 : low - 1 + count, :]
    total = total + jnp.where(lane < CZ - width, pltpu.roll(here, CZ - width, 1), 0.0)
    total = total + jnp.where(lane >= width, pltpu.roll(here, width, 1), 0.0)
    return here, total


def diagonal_values(reaction, f):
    low = reaction[2 * f : 2 * f + 1, :]
    jump = reaction[2 * f + 1 : 2 * f + 2, :] - low
    return 6.0 + low, 6.0 + low + jump


def inverse_of(code, reaction, f):
    fluid, solid = diagonal_values(reaction, f)
    fluid, solid = 1.0 / fluid, 1.0 / solid
    return jnp.where(code == 0.0, fluid, jnp.where(code == 1.0, solid, 0.0))


def place():
    return lax.axis_index("row"), lax.axis_index("col")


def by_parity(step, first, second):
    even = lax.rem(lax.axis_index("col"), 2) == 0
    pl.when(even)(functools.partial(step, second, first))
    pl.when(jnp.logical_not(even))(functools.partial(step, first, second))


def pack_layers(
    b, material, inverse, up, down, first, second, b_here, material_here, inverse_here, sems,
):
    copies = [pltpu.make_async_copy(b.at[f], b_here.at[f], sems.at[f]) for f in range(FIELDS)]
    copies.append(pltpu.make_async_copy(material, material_here, sems.at[FIELDS]))
    copies.append(pltpu.make_async_copy(inverse, inverse_here, sems.at[FIELDS + 1]))
    for copy in copies:
        copy.start()
    for f in range(FIELDS + 1):
        copies[f].wait()
        if f < FIELDS:
            take = lambda start, size, step: b_here[f, pl.ds(start, size, stride=step), :]
        else:
            take = lambda start, size, step: material_here[
                pl.ds(start, size, stride=step), :
            ].astype(jnp.float32)
        at = f * 6 * CY
        up[at : at + 6 * CY, :] = take((CX - 6) * CY, 6 * CY, 1)
        down[at : at + 6 * CY, :] = take(0, 6 * CY, 1)

        def bands(left, right):
            for i in range(4):
                at = (f * 4 + i) * CX
                right[at : at + CX, :] = take(CY - 4 + i, CX, CY)
                left[at : at + CX, :] = take(i, CX, CY)

        by_parity(bands, first, second)
    copies[FIELDS + 1].wait()
    for f in range(FIELDS):
        for k in range(inverse.shape[2] // CZ):
            at = BAND_LINES + (f * GROUPS + k) * GROUPS
            value = inverse_here[f, :, k * CZ : (k + 1) * CZ]
            first[at : at + GROUPS, :] = value
            second[at : at + GROUPS, :] = value


def pack_corners(mine, first, second, reaction, up, down, kin, constants):
    for f in range(FIELDS):
        for i in range(2):
            constants[2 * f + i : 2 * f + i + 1, :] = jnp.broadcast_to(
                reaction[i : i + 1, f : f + 1], (1, CZ)
            )
    for f in range(FIELDS):
        for k in range(mine.shape[2] // CZ):
            at = (f * GROUPS + k) * GROUPS
            kin[0, at : at + GROUPS, :] = mine[f, :, k * CZ : (k + 1) * CZ]

    def pack(low, high):
        for side, ref in enumerate((low, high)):
            kin[1 + side] = ref[BAND_LINES : BAND_LINES + KIN_LINES, :]
            for f in range(FIELDS + 1):
                for j, offset in FINE_CORNER_AT.items():
                    size = 6 - j
                    line = (f * 4 + (j - 1 if side else 4 - j)) * CX
                    at = (f * 2 + side) * 16 + offset
                    up[at : at + size, :] = ref[line + CX - size : line + CX, :]
                    down[at : at + size, :] = ref[line : line + size, :]
                at = (f * 2 + side) * 16 + 14
                up[at : at + 2, :] = jnp.zeros((2, CZ), jnp.float32)
                down[at : at + 2, :] = jnp.zeros((2, CZ), jnp.float32)

    by_parity(pack, first, second)


def smooth_first(
    nrow, ncol, reaction, b, material, above, below, even, odd, kabove, kbelow,
    first, scaled, code, coarse, up, down, side_even, side_odd,
    s, inv, p0, p1, p2, p3, pair,
):
    row, col = place()
    parts = (p0, p1, p2, p3)
    zeros = jnp.zeros((FY, CZ), jnp.float32)
    for x in (*range(6), *range(GX - 6, GX)):
        for f in range(FIELDS):
            s[f, x, 8:56, :] = zeros[:48]
        code[x] = zeros + 2.0

    def own(i):
        x = i + 6
        for f in range(FIELDS):
            s[f, x, 8:16, :] = zeros[:8]
            s[f, x, 16:48, :] = b[f, i * CY : i * CY + CY, :]
            s[f, x, 48:56, :] = zeros[:8]
        code[x, 0:16, :] = zeros[:16] + 2.0
        code[x, 16:48, :] = material[i * CY : i * CY + CY, :].astype(jnp.float32)
        code[x, 48:64, :] = zeros[:16] + 2.0

    every(0, CX, own)
    sflat = s.reshape(FIELDS, GX * FY, CZ)
    cflat = code.reshape(GX * FY, CZ)

    def put(f, start, size, value):
        if f < FIELDS:
            sflat[f, pl.ds(start, size, stride=FY), :] = value
        else:
            cflat[pl.ds(start, size, stride=FY), :] = value

    def rows(first_x, ref):
        for i in range(6):
            for f in range(FIELDS):
                at = (f * 6 + i) * CY
                s[f, first_x + i, 16:48, :] = ref[at : at + CY, :]
            at = (FIELDS * 6 + i) * CY
            code[first_x + i, 16:48, :] = ref[at : at + CY, :]

    pl.when(row > 0)(functools.partial(rows, 0, above))
    pl.when(row < nrow - 1)(functools.partial(rows, GX - 6, below))

    def bands(ref, first_y):
        for f in range(FIELDS + 1):
            for i in range(4):
                at = (f * 4 + i) * CX
                put(f, 6 * FY + first_y + i, CX, ref[at : at + CX, :])

    def sides(low, high):
        pl.when(col > 0)(functools.partial(bands, low, FO - 4))
        pl.when(col < ncol - 1)(functools.partial(bands, high, FO + CY))

    by_parity(sides, even, odd)

    def corners(ref, is_above, is_high):
        for f in range(FIELDS + 1):
            for j, offset in FINE_CORNER_AT.items():
                size = 6 - j
                at = (f * 2 + is_high) * 16 + offset
                x = 6 - size if is_above else 6 + CX
                y = FO + CY - 1 + j if is_high else FO - j
                put(f, x * FY + y, size, ref[at : at + size, :])

    for ref, is_above, in_x in ((kabove, 1, row > 0), (kbelow, 0, row < nrow - 1)):
        for is_high, in_y in ((0, col > 0), (1, col < ncol - 1)):
            pl.when(in_x & in_y)(functools.partial(corners, ref, is_above, is_high))

    def scale(x):
        kind = code[x, 8:56, :]
        for f in range(FIELDS):
            inverse = inverse_of(kind, reaction, f)
            value = inverse * s[f, x, 8:56, :]
            inv[f, x, 8:56, :] = inverse
            s[f, x, 8:56, :] = value
            p0[f, x, 8:56, :] = value * (1.0 / THETA)

    every(0, GX, scale)

    for k, (keep, gain) in enumerate(coefficients()):
        def sweep(x):
            for f in range(FIELDS):
                here, total = beside(parts[k], f, x, 8, 48, 1)
                value = s[f, x, 8:56, :] - here + inv[f, x, 8:56, :] * total
                s[f, x, 8:56, :] = value
                parts[k + 1][f, x, 8:56, :] = keep * here + gain * value

        every(k + 1, GX - k - 1, sweep)

    parity = lanes() % 2 == 0

    def finish(i):
        at_y = i * 2 * CY
        inside = 1 <= i <= HX
        sums = []
        for f in range(FIELDS):
            fluid, solid = diagonal_values(reaction, f)
            residue = jnp.zeros((CY, CZ), jnp.float32)
            for h in range(2):
                x = i * 2 + h + 4
                row_at = (i * 2 + h - 2) * CY
                here, total = beside(p3, f, x, 16, CY, 1)
                value = s[f, x, 16:48, :] - here + inv[f, x, 16:48, :] * total
                out = pl.ds(at_y + h * CY, CY)
                scaled[f, out, :] = value
                if inside:
                    first[f, row_at : row_at + CY, :] = (
                        p0[f, x, 16:48, :] + p1[f, x, 16:48, :] + p2[f, x, 16:48, :] + here
                    )
                residue = residue + jnp.where(code[x, 16:48, :] == 1.0, solid, fluid) * value
            sums.append(residue)
        sums.append(code[i * 2 + 4, 16:48, :] + code[i * 2 + 5, 16:48, :])
        halves = []
        for f, value in enumerate(sums):
            here = pair.at[i % 2, f]
            here[...] = value
            halves.append(here[pl.ds(0, HY, stride=2), :] + here[pl.ds(1, HY, stride=2), :])
        halves.append(halves[4])
        out = pl.ds(i * HY, HY)
        for plane in range(3):
            even, odd = halves[2 * plane], halves[2 * plane + 1]
            merged = jnp.where(
                parity, even + pltpu.roll(even, CZ - 1, 1), odd + pltpu.roll(odd, 1, 1)
            )
            if plane < 2:
                coarse[plane, out, :] = merged * 0.5
            else:
                coarse[plane, out, :] = jnp.where(merged > 8.5, -1.0, merged)

    every(0, VX, finish)

    for f in range(FIELDS):
        at = COARSE_LINES + f * CY
        up[at : at + CY, :] = scaled[f, (CX - 1) * CY : CX * CY, :]
        down[at : at + CY, :] = scaled[f, 4 * CY : 5 * CY, :]
    for plane in range(3):
        at, size = plane * (HX + 1) * HY, (HX + 1) * HY
        up[at : at + size, :] = coarse[plane, 0:size, :]
        down[at : at + size, :] = coarse[plane, HY : HY + size, :]

    def strips(left, right):
        for plane in range(3):
            for i in range(9):
                at = (plane * 9 + i) * VX
                right[at : at + VX, :] = coarse[plane, pl.ds(HY - 9 + i, VX, stride=HY), :]
                left[at : at + VX, :] = coarse[plane, pl.ds(i, VX, stride=HY), :]
        for f in range(FIELDS):
            for j, offset in STRIP_AT.items():
                size = WX + 2 - 2 * j
                at = STRIP_LINES + f * (3 * WX - 6) + offset
                x = (j - 1) * CY
                right[at : at + size, :] = scaled[f, pl.ds(x + CY - j, size, stride=CY), :]
                left[at : at + size, :] = scaled[f, pl.ds(x + j - 1, size, stride=CY), :]

    by_parity(strips, side_even, side_odd)


def pack_knots(first, second, up, down):
    def pack(low, high):
        for plane in range(3):
            for side, ref in enumerate((low, high)):
                base = (plane * 2 + side) * CORNER_LINES
                up[base + 40 : base + 48, :] = jnp.zeros((8, CZ), jnp.float32)
                down[base + 40 : base + 48, :] = jnp.zeros((8, CZ), jnp.float32)
                for j, offset in CORNER_AT.items():
                    size = 10 - j
                    line = (plane * 9 + (j - 1 if side else 9 - j)) * VX
                    at = base + offset
                    up[at : at + size, :] = ref[line + VX - 1 - size : line + VX - 1, :]
                    down[at : at + size, :] = ref[line + 1 : line + 1 + size, :]

    by_parity(pack, first, second)


def coarse_constants(reaction, plane):
    parity = lanes() % 2 == 0
    even, odd = (
        [reaction[2 * f + i : 2 * f + i + 1, :] for i in range(2)]
        for f in (2 * plane, 2 * plane + 1)
    )
    low = jnp.where(parity, even[0], odd[0])
    return 8.0 * low, jnp.where(parity, even[1] - even[0], odd[1] - odd[0])


def smooth_coarse(
    nrow, ncol, reaction, coarse, above, below, even, odd, kabove, kbelow,
    start, scaled, inverse_out, sums,
    s, inv, count, p0, p1, p2, p3,
):
    row, col = place()
    parts = (p0, p1, p2, p3)
    zeros = jnp.zeros((QY, CZ), jnp.float32)

    def clear(x):
        for plane in range(2):
            s[plane, x] = zeros
        count[x] = zeros - 1.0

    every(0, QX, clear)
    sflat = s.reshape(2, QX * QY, CZ)
    cflat = count.reshape(QX * QY, CZ)

    def put(plane, start_row, size, value):
        if plane < 2:
            sflat[plane, pl.ds(start_row, size, stride=QY), :] = value
        else:
            cflat[pl.ds(start_row, size, stride=QY), :] = value

    def block(plane, x, value):
        if plane < 2:
            s[plane, x, QO : QO + HY, :] = value
        else:
            count[x, QO : QO + HY, :] = value

    def rows(first_x, ref):
        for plane in range(3):
            for i in range(HX + 1):
                at = (plane * (HX + 1) + i) * HY
                block(plane, first_x + i, ref[at : at + HY, :])

    for plane in range(3):
        for i in range(HX):
            block(plane, 9 + i, coarse[plane, (i + 1) * HY : (i + 2) * HY, :])
    pl.when(row > 0)(functools.partial(rows, 0, above))
    pl.when(row < nrow - 1)(functools.partial(rows, 9 + HX, below))

    def strips(ref, first_y):
        for plane in range(3):
            for i in range(9):
                line = (plane * 9 + i) * VX
                put(plane, 9 * QY + first_y + i, HX, ref[line + 1 : line + 1 + HX, :])

    def sides(low, high):
        pl.when(col > 0)(functools.partial(strips, low, QO - 9))
        pl.when(col < ncol - 1)(functools.partial(strips, high, QO + HY))

    by_parity(sides, even, odd)

    def corners(ref, is_above, is_high):
        for plane in range(3):
            base = (plane * 2 + is_high) * CORNER_LINES
            for j, at in CORNER_AT.items():
                size = 10 - j
                x = 9 - size if is_above else 9 + HX
                y = QO + HY - 1 + j if is_high else QO - j
                put(plane, x * QY + y, size, ref[base + at : base + at + size, :])

    for ref, is_above, in_x in ((kabove, 1, row > 0), (kbelow, 0, row < nrow - 1)):
        for is_high, in_y in ((0, col > 0), (1, col < ncol - 1)):
            pl.when(in_x & in_y)(functools.partial(corners, ref, is_above, is_high))

    def scale(x):
        number = count[x]
        for plane in range(2):
            low8, jump = coarse_constants(reaction, plane)
            inverse = jnp.where(number < 0.0, 0.0, 1.0 / (6.0 + 0.5 * (low8 + jump * number)))
            value = inverse * s[plane, x]
            inv[plane, x] = inverse
            s[plane, x] = value
            p0[plane, x] = value * (1.0 / THETA)

    every(0, QX, scale)

    for k, (keep, gain) in enumerate(coefficients()):
        def sweep(x):
            for plane in range(2):
                here, total = beside(parts[k], plane, x, 8, 32, 2)
                value = s[plane, x, 8:40, :] - here + inv[plane, x, 8:40, :] * total
                s[plane, x, 8:40, :] = value
                parts[k + 1][plane, x, 8:40, :] = keep * here + gain * value

        every(k + 1, QX - k - 1, sweep)

    def finish(x):
        for plane in range(2):
            here, total = beside(p3, plane, x, 8, 32, 2)
            value = s[plane, x, 8:40, :] - here + inv[plane, x, 8:40, :] * total
            scaled[plane, x - 4] = value
            inverse_out[plane, x - 4] = inv[plane, x, 8:40, :]

    every(4, QX - 4, finish)

    def add(x):
        for plane in range(2):
            start[plane, x - 7] = (
                p0[plane, x, 8:40, :] + p1[plane, x, 8:40, :]
                + p2[plane, x, 8:40, :] + p3[plane, x, 8:40, :]
            )

    every(7, QX - 7, add)

    lane = lanes()
    message = jnp.zeros((8, CZ), jnp.float32)
    for plane in range(2):
        low8, jump = coarse_constants(reaction, plane)
        total = jnp.zeros((HY, CZ), jnp.float32)
        for x in range(9, 9 + HX):
            diagonal = 6.0 + 0.5 * (low8 + jump * count[x, QO : QO + HY, :])
            total = total + diagonal * scaled[plane, x - 4, 8 : 8 + HY, :]
        total = total[:8] + total[8:]
        for shift in (4, 2, 1):
            total = total + pltpu.roll(total, shift, 0)
        for shift in (2, 4, 8):
            total = total + pltpu.roll(total, CZ - shift, 1)
        for odd in range(2):
            for g in range(GROUPS):
                to = (2 * plane + odd) * GROUPS + g
                moved = pltpu.roll(total, (to - 16 * g - odd) % CZ, 1)
                message = jnp.where(lane == to, moved, message)
    sums[...] = jnp.broadcast_to(message[:1], sums.shape)


def smooth_second(
    nrow, ncol, reaction, gathered, kin, kin_above, kin_below,
    start, qscaled, qinverse, first, scaled, code, above, below, even, odd,
    out,
    wide, spread, e, q0, q1, q2, q3, qs, fs, inv, f0, p0, p1, p2,
):
    row, col = place()
    lane = lanes()
    width = ncol * GROUPS
    fields = [jnp.zeros((nrow, CZ), jnp.float32) for _ in range(FIELDS)]
    for c in range(ncol):
        some = gathered[pl.ds(c, nrow, stride=ncol), :]
        for f in range(FIELDS):
            moved = pltpu.roll(some, (c * GROUPS - f * GROUPS) % CZ, 1)
            here = (lane >= c * GROUPS) & (lane < (c + 1) * GROUPS)
            fields[f] = jnp.where(here, moved, fields[f])
    for f in range(FIELDS):
        wide[f] = fields[f]

    group = lax.broadcasted_iota(jnp.int32, (GROUPS, CZ), 0)
    spot = lax.broadcasted_iota(jnp.int32, (GROUPS, CZ), 1)
    mask = [(spot // 16 == group) & (spot % 2 == odd) for odd in range(2)]
    e[...] = jnp.zeros_like(e)

    def product(rows_of, f):
        total = jnp.zeros((GROUPS, width), jnp.float32)
        for k in range(nrow):
            total = total + rows_of(f, k) * wide[f, k : k + 1, 0:width]
        return jnp.sum(total, axis=1, keepdims=True)

    def neighbour(rows_of, dx, dy):
        for plane in range(2):
            even = product(rows_of, 2 * plane)
            odd = product(rows_of, 2 * plane + 1)
            full = jnp.where(mask[0], even, jnp.where(mask[1], odd, 0.0))
            line = jnp.sum(full, axis=0, keepdims=True)
            x_from, x_to = {-1: (0, 6), 0: (6, 6 + HX), 1: (6 + HX, EX)}[dx]
            y_from, y_to = {-1: (8, QO), 0: (QO, QO + HY), 1: (QO + HY, QO + HY + 8)}[dy]
            for x in range(x_from, x_to):
                e[plane, x, y_from:y_to, :] = jnp.broadcast_to(line, (y_to - y_from, CZ))

    def slab(ref, part):
        def rows_of(f, k):
            at = (f * GROUPS + k) * GROUPS
            return ref[part, at : at + GROUPS, :]

        return rows_of

    in_x = {-1: row > 0, 0: True, 1: row < nrow - 1}
    in_y = {-1: col > 0, 0: True, 1: col < ncol - 1}
    for dx, ref in ((0, kin), (-1, kin_above), (1, kin_below)):
        for part, dy in enumerate((0, -1, 1)):
            step = functools.partial(neighbour, slab(ref, part), dx, dy)
            if dx == 0 and dy == 0:
                step()
            else:
                pl.when(in_x[dx] & in_y[dy])(step)

    parts = (q0, q1, q2, q3)

    def begin(x):
        for plane in range(2):
            here, total = beside(e, plane, x, 8, 32, 2)
            value = qscaled[plane, x - 1] - here + qinverse[plane, x - 1] * total
            qs[plane, x] = value
            q0[plane, x, 8:40, :] = value * (1.0 / THETA)

    every(1, EX - 1, begin)
    for k, (keep, gain) in enumerate(coefficients()):
        def sweep(x):
            for plane in range(2):
                here, total = beside(parts[k], plane, x, 8, 32, 2)
                value = qs[plane, x] - here + qinverse[plane, x - 1] * total
                qs[plane, x] = value
                parts[k + 1][plane, x, 8:40, :] = keep * here + gain * value

        every(k + 2, EX - k - 2, sweep)

    parity = lane % 2 == 0

    def lift(i):
        for plane in range(2):
            total = start[plane, i] + e[plane, i + 4, 8:40, :]
            total = total + q0[plane, i + 4, 8:40, :] + q1[plane, i + 4, 8:40, :]
            total = total + q2[plane, i + 4, 8:40, :] + q3[plane, i + 4, 8:40, :]
            for odd in range(2):
                if odd:
                    value = jnp.where(parity, pltpu.roll(total, CZ - 1, 1), total)
                else:
                    value = jnp.where(parity, total, pltpu.roll(total, 1, 1))
                spread[...] = value
                some = spread[4:28, :]
                for h in range(2):
                    for y in range(2):
                        f0[2 * plane + odd, i * 2 + h, pl.ds(8 + y, 24, stride=2), :] = some

    every(0, HX + 4, lift)

    zeros = jnp.zeros((48, CZ), jnp.float32)
    for f in range(FIELDS):
        for x in (1, FX - 2):
            fs[f, x, 8:56, :] = zeros
        for x in range(2, FX - 2):
            fs[f, x, 8:16, :] = zeros[:8]
            fs[f, x, 16:48, :] = scaled[f, (x - 2) * CY : (x - 1) * CY, :]
            fs[f, x, 48:56, :] = zeros[:8]
    sflat = fs.reshape(FIELDS, FX * FY, CZ)

    def face(x, ref):
        for f in range(FIELDS):
            at = COARSE_LINES + f * CY
            fs[f, x, 16:48, :] = ref[at : at + CY, :]

    pl.when(in_x[-1])(functools.partial(face, 1, above))
    pl.when(in_x[1])(functools.partial(face, FX - 2, below))

    def strips(ref, is_high):
        for f in range(FIELDS):
            for j, offset in STRIP_AT.items():
                size = WX + 2 - 2 * j
                at = STRIP_LINES + f * (3 * WX - 6) + offset
                y = FO + CY - 1 + j if is_high else FO - j
                start = (1 + j) * FY + y
                sflat[f, pl.ds(start, size, stride=FY), :] = ref[at : at + size, :]

    def sides(low, high):
        pl.when(in_y[-1])(functools.partial(strips, low, 0))
        pl.when(in_y[1])(functools.partial(strips, high, 1))

    by_parity(sides, even, odd)

    parts = (p0, p1, p2)

    def open_fine(x):
        kind = code[x + 2, 8:56, :]
        for f in range(FIELDS):
            here, total = beside(f0, f, x, 8, 48, 1)
            inverse = inverse_of(kind, reaction, f)
            inv[f, x, 8:56, :] = inverse
            value = fs[f, x, 8:56, :] - here + inverse * total
            fs[f, x, 8:56, :] = value
            p0[f, x, 8:56, :] = value * (1.0 / THETA)

    every(1, FX - 1, open_fine)
    for k, (keep, gain) in enumerate(coefficients()[:2]):
        def sweep(x):
            for f in range(FIELDS):
                here, total = beside(parts[k], f, x, 8, 48, 1)
                value = fs[f, x, 8:56, :] - here + inv[f, x, 8:56, :] * total
                fs[f, x, 8:56, :] = value
                parts[k + 1][f, x, 8:56, :] = keep * here + gain * value

        every(k + 2, FX - k - 2, sweep)

    keep, gain = coefficients()[2]

    def close(i):
        x = i + 4
        at = pl.ds(i * CY, CY)
        for f in range(FIELDS):
            here, total = beside(p2, f, x, 16, CY, 1)
            value = fs[f, x, 16:48, :] - here + inv[f, x, 16:48, :] * total
            result = first[f, at, :] + f0[f, x, 16:48, :] + p0[f, x, 16:48, :]
            result = result + p1[f, x, 16:48, :] + here
            out[f, at, :] = result + (keep * here + gain * value)

    every(0, CX, close)


def call(kernel, out_shapes, scratch, *args, limit=16, in_hbm=False):
    vmem = pl.BlockSpec(memory_space=pltpu.VMEM)
    given = pl.BlockSpec(memory_space=pltpu.HBM) if in_hbm else vmem
    return pl.pallas_call(
        kernel,
        out_shape=[jax.ShapeDtypeStruct(shape, jnp.float32) for shape in out_shapes],
        in_specs=[given] * len(args),
        out_specs=[vmem] * len(out_shapes),
        scratch_shapes=[
            pltpu.VMEM(shape, jnp.float32) if isinstance(shape, tuple) else shape
            for shape in scratch
        ],
        compiler_params=pltpu.CompilerParams(vmem_limit_bytes=int(limit * 1024 * 1024)),
    )(*args)


def ahead(value):
    count = lax.axis_size("row")
    return lax.ppermute(value, "row", [(i, (i + 1) % count) for i in range(count)])


def back(value):
    count = lax.axis_size("row")
    return lax.ppermute(value, "row", [((i + 1) % count, i) for i in range(count)])


def pairs(value, odd):
    nrow, ncol = lax.axis_size("row"), lax.axis_size("col")
    moves = []
    for r in range(nrow):
        for c in range(ncol):
            if not odd:
                to = (r, c ^ 1)
            elif c in (0, ncol - 1):
                to = (r ^ 1, c)
            else:
                to = (r, c + 1 if c % 2 else c - 1)
            moves.append((r * ncol + c, to[0] * ncol + to[1]))
    return lax.ppermute(value, ("row", "col"), moves)


def body(right_side, material, reaction, coarse_inverse):
    nrow, ncol = lax.axis_size("row"), lax.axis_size("col")
    b = right_side.reshape(FIELDS, CX * CY, CZ)
    material = material.reshape(CX * CY, CZ)

    fine = (FIELDS, CX * CY, CZ)
    up, down, even, odd = call(
        pack_layers,
        [(LAYER_LINES, CZ)] * 2 + [(BAND_LINES + KIN_LINES, CZ)] * 2,
        [fine, pltpu.VMEM(fine[1:], jnp.int32), coarse_inverse.shape,
         pltpu.SemaphoreType.DMA((FIELDS + 2,))],
        b, material, coarse_inverse,
        in_hbm=True, limit=59.27,
    )
    odd, even = pairs(odd, True), pairs(even, False)
    above, below = ahead(up), back(down)
    up, down, kin, reaction = call(
        pack_corners,
        [((FIELDS + 1) * 32, CZ)] * 2 + [(3, KIN_LINES, CZ), (2 * FIELDS, CZ)], [],
        coarse_inverse, even, odd, reaction.T,
    )
    kabove, kbelow = ahead(up), back(down)
    kin, kabove, kbelow = lax.optimization_barrier((kin, kabove, kbelow))
    kin_above, kin_below = ahead(kin), back(kin)

    wide = (FIELDS, WX * CY, CZ)
    padded = (FIELDS, GX, FY, CZ)
    first, scaled, code, coarse, up, down, side_even, side_odd = call(
        functools.partial(smooth_first, nrow, ncol),
        [fine, wide, padded[1:], (3, VX * HY, CZ)]
        + [(FACE_LINES, CZ)] * 2 + [(SIDE_LINES, CZ)] * 2,
        [padded] * 6 + [(2, FIELDS + 1, CY, CZ)],
        reaction, b, material, above, below, even, odd, kabove, kbelow,
        limit=30,
    )
    up, down, side_even, side_odd, kin_above, kin_below = lax.optimization_barrier(
        (up, down, side_even, side_odd, kin_above, kin_below)
    )

    odd, even = pairs(side_odd, True), pairs(side_even, False)
    above, below = ahead(up), back(down)
    up, down = call(pack_knots, [(KNOT_LINES, CZ)] * 2, [], even, odd)
    kabove, kbelow = ahead(up), back(down)

    qpadded = (2, QX, QY, CZ)
    start, qscaled, qinverse, sums = call(
        functools.partial(smooth_coarse, nrow, ncol),
        [(2, HX + 4, 32, CZ), (2, HX + 10, 32, CZ), (2, HX + 10, 32, CZ), (nrow * ncol, CZ)],
        [qpadded, qpadded, qpadded[1:]] + [qpadded] * 4,
        reaction, coarse, above, below, even, odd, kabove, kbelow,
        limit=14,
    )

    gathered = lax.all_to_all(sums, ("row", "col"), 0, 0)

    epadded = (2, EX, QY, CZ)
    padded = (FIELDS, FX, FY, CZ)
    (out,) = call(
        functools.partial(smooth_second, nrow, ncol),
        [fine],
        [(FIELDS, nrow, CZ), (32, CZ)] + [epadded] * 5 + [(2, EX, 32, CZ)] + [padded] * 6,
        reaction, gathered, kin, kin_above, kin_below,
        start, qscaled, qinverse, first, scaled, code, above, below, even, odd,
        limit=32,
    )
    return out.reshape(right_side.shape)


def solution(mesh):
    placed = (
        P(None, "row", "col", None),
        P("row", "col", None),
        P(),
        P(None, ("row", "col"), None),
    )
    return jax.shard_map(
        body, mesh=mesh, in_specs=placed, out_specs=P(None, "row", "col", None), check_vma=False
    )
```

```python
import functools

import jax
import jax.numpy as jnp
from jax import lax
from jax.experimental import pallas as pl
from jax.experimental.pallas import tpu as pltpu
from jax.sharding import PartitionSpec as P

FIELDS = 4
CX, CY, CZ = 16, 32, 128
HX, HY = CX // 2, CY // 2
GROUPS = 8
SWEEPS = 4
LOW_BOUND = 0.25
HIGH_BOUND = 2.0
THETA = (HIGH_BOUND + LOW_BOUND) / 2.0
DELTA = (HIGH_BOUND - LOW_BOUND) / 2.0

WX = CX + 4
GX, FY, FO, FN = CX + 12, CY + 24, 8, CY + 8
OWN = slice(FO, FO + CY)
ALL = slice(FO, FO + FN)
FX = CX + 8
MID = (4, CX - 4)
VX = HX + 2
QX, QY, QO = HX + 18, HY + 32, 16
EX = HX + 12
CORNER_AT = {1: 0, 2: 9, 3: 17, 4: 24, 5: 30, 6: 35, 7: 39, 8: 42, 9: 44}
CORNER_LINES = 48
FINE_CORNER_AT = {1: 0, 2: 5, 3: 9, 4: 12}
FINE_CORNER_LINES = (FIELDS + 1) * 32

LAYER_LINES = (FIELDS + 1) * 6 * CY
BAND_LINES = (FIELDS + 1) * 4 * CX
KIN_LINES = FIELDS * GROUPS * 8
COARSE_LINES = 3 * (HX + 1) * HY
FACE_KIN = COARSE_LINES + FIELDS * CY
FACE_LINES = FACE_KIN + 2 * KIN_LINES
STRIP_LINES = 272
STRIP_AT = {1: 0, 2: WX, 3: 2 * WX - 2}
SIDE_LINES = STRIP_LINES + FIELDS * (3 * WX - 6)
KNOT_LINES = 6 * CORNER_LINES


def coefficients():
    rho = DELTA / THETA
    pairs = []
    for _ in range(SWEEPS - 1):
        following = 1.0 / (2.0 * THETA / DELTA - rho)
        pairs.append((following * rho, 2.0 * following / DELTA))
        rho = following
    return pairs


def every(low, high, step):
    for i in range(low, high):
        step(i)


def lanes():
    return lax.broadcasted_iota(jnp.int32, (1, CZ), 1)


def beside(ref, f, x, low, count, width):
    here = ref[f, x, low : low + count, :]
    lane = lanes()
    total = ref[f, x + 1, low : low + count, :] + ref[f, x - 1, low : low + count, :]
    total = total + ref[f, x, low + 1 : low + 1 + count, :]
    total = total + ref[f, x, low - 1 : low - 1 + count, :]
    total = total + jnp.where(lane < CZ - width, pltpu.roll(here, CZ - width, 1), 0.0)
    total = total + jnp.where(lane >= width, pltpu.roll(here, width, 1), 0.0)
    return here, total


def diagonal_values(reaction, f):
    low = reaction[2 * f : 2 * f + 1, :]
    jump = reaction[2 * f + 1 : 2 * f + 2, :] - low
    return 6.0 + low, 6.0 + low + jump


def inverse_of(code, reaction, f):
    fluid, solid = diagonal_values(reaction, f)
    fluid, solid = 1.0 / fluid, 1.0 / solid
    return jnp.where(code == 0.0, fluid, jnp.where(code == 1.0, solid, 0.0))


def place():
    return lax.axis_index("row"), lax.axis_index("col")


def by_parity(step, first, second):
    even = lax.rem(lax.axis_index("col"), 2) == 0
    pl.when(even)(functools.partial(step, second, first))
    pl.when(jnp.logical_not(even))(functools.partial(step, first, second))


def pack_layers(
    b, material, inverse, up, down, first, second, b_here, material_here, inverse_here, sems,
):
    copies = [pltpu.make_async_copy(b.at[f], b_here.at[f], sems.at[f]) for f in range(FIELDS)]
    copies.append(pltpu.make_async_copy(material, material_here, sems.at[FIELDS]))
    copies.append(pltpu.make_async_copy(inverse, inverse_here, sems.at[FIELDS + 1]))
    for copy in copies:
        copy.start()
    for f in range(FIELDS + 1):
        copies[f].wait()
        if f < FIELDS:
            take = lambda start, size, step: b_here[f, pl.ds(start, size, stride=step), :]
        else:
            take = lambda start, size, step: material_here[
                pl.ds(start, size, stride=step), :
            ].astype(jnp.float32)
        at = f * 6 * CY
        up[at : at + 6 * CY, :] = take((CX - 6) * CY, 6 * CY, 1)
        down[at : at + 6 * CY, :] = take(0, 6 * CY, 1)

        def bands(left, right):
            for i in range(4):
                at = (f * 4 + i) * CX
                right[at : at + CX, :] = take(CY - 4 + i, CX, CY)
                left[at : at + CX, :] = take(i, CX, CY)

        by_parity(bands, first, second)
    copies[FIELDS + 1].wait()
    for f in range(FIELDS):
        for k in range(inverse.shape[2] // CZ):
            at = BAND_LINES + (f * GROUPS + k) * GROUPS
            value = inverse_here[f, :, k * CZ : (k + 1) * CZ]
            first[at : at + GROUPS, :] = value
            second[at : at + GROUPS, :] = value


def pack_corners(first, second, reaction, inverse, up, down, constants):
    for f in range(FIELDS):
        for k in range(inverse.shape[2] // CZ):
            at = FINE_CORNER_LINES + (f * GROUPS + k) * GROUPS
            value = inverse[f, :, k * CZ : (k + 1) * CZ]
            up[at : at + GROUPS, :] = value
            down[at : at + GROUPS, :] = value
    for f in range(FIELDS):
        for i in range(2):
            constants[2 * f + i : 2 * f + i + 1, :] = jnp.broadcast_to(
                reaction[i : i + 1, f : f + 1], (1, CZ)
            )
    def pack(low, high):
        for side, ref in enumerate((low, high)):
            for f in range(FIELDS + 1):
                for j, offset in FINE_CORNER_AT.items():
                    size = 6 - j
                    line = (f * 4 + (j - 1 if side else 4 - j)) * CX
                    at = (f * 2 + side) * 16 + offset
                    up[at : at + size, :] = ref[line + CX - size : line + CX, :]
                    down[at : at + size, :] = ref[line : line + size, :]
                at = (f * 2 + side) * 16 + 14
                up[at : at + 2, :] = jnp.zeros((2, CZ), jnp.float32)
                down[at : at + 2, :] = jnp.zeros((2, CZ), jnp.float32)

    by_parity(pack, first, second)


def halo_row(j, is_high):
    return FO + CY - 1 + j if is_high else FO + FN - j


def go_round(ref, f, x, value):
    ref[f, x, ALL, :] = value
    ref[f, x, FO - 1 : FO, :] = value[FN - 1 : FN]
    ref[f, x, FO + FN : FO + FN + 1, :] = value[0:1]


def fine_scale(x, reaction, code, s, inv, p0):
    kind = code[x, ALL, :]
    for f in range(FIELDS):
        inverse = inverse_of(kind, reaction, f)
        inv[f, x, ALL, :] = inverse
        if p0 is not None:
            value = inverse * s[f, x, ALL, :]
            s[f, x, ALL, :] = value
            go_round(p0, f, x, value * (1.0 / THETA))


def fine_sweep(x, k, s, inv, parts):
    keep, gain = coefficients()[k]
    for f in range(FIELDS):
        here, total = beside(parts[k], f, x, FO, FN, 1)
        value = s[f, x, ALL, :] - here + inv[f, x, ALL, :] * total
        s[f, x, ALL, :] = value
        go_round(parts[k + 1], f, x, keep * here + gain * value)


def fine_last(x, reaction, code, s, inv, p3, scaled, line):
    residues = []
    for f in range(FIELDS):
        fluid, solid = diagonal_values(reaction, f)
        here, total = beside(p3, f, x, FO, CY, 1)
        value = s[f, x, OWN, :] - here + inv[f, x, OWN, :] * total
        scaled[f, line : line + CY, :] = value
        residues.append(jnp.where(code[x, OWN, :] == 1.0, solid, fluid) * value)
    return residues


def restrict(x, residues, code, pair, coarse, line):
    parity = lanes() % 2 == 0
    sums = [one + other for one, other in zip(*residues)]
    sums.append(code[x, OWN, :] + code[x + 1, OWN, :])
    halves = []
    for f, value in enumerate(sums):
        here = pair.at[x // 2 % 2, f]
        here[...] = value
        halves.append(here[pl.ds(0, HY, stride=2), :] + here[pl.ds(1, HY, stride=2), :])
    halves.append(halves[4])
    for plane in range(3):
        even, odd = halves[2 * plane], halves[2 * plane + 1]
        merged = jnp.where(
            parity, even + pltpu.roll(even, CZ - 1, 1), odd + pltpu.roll(odd, 1, 1)
        )
        merged = merged * 0.5 if plane < 2 else jnp.where(merged > 8.5, -1.0, merged)
        coarse[plane, line : line + HY, :] = merged


def lay_own(x_at, xs, b, material, s, code):
    zeros = jnp.zeros((8, CZ), jnp.float32)
    for x in xs:
        for f in range(FIELDS):
            s[f, x + x_at, OWN, :] = b[f, x * CY : x * CY + CY, :]
            s[f, x + x_at, FO + CY : FO + FN, :] = zeros
        code[x + x_at, OWN, :] = material[x * CY : x * CY + CY, :].astype(jnp.float32)
        code[x + x_at, FO + CY : FO + FN, :] = zeros + 2.0


def putter(s, code):
    sflat = s.reshape(FIELDS, s.shape[1] * FY, CZ)
    cflat = code.reshape(s.shape[1] * FY, CZ)

    def put(f, x, y_row, size, value):
        to = pl.ds(x * FY + y_row, size, stride=FY)
        if f < FIELDS:
            sflat[f, to, :] = value
        else:
            cflat[to, :] = value

    return put


def lay_bands(x_at, spans, ncol, put, even, odd):
    _, col = place()

    def bands(ref, is_high):
        for f in range(FIELDS + 1):
            for i in range(4):
                at = (f * 4 + i) * CX
                row = halo_row(i + 1 if is_high else 4 - i, is_high)
                for x, size in spans:
                    put(f, x + x_at, row, size, ref[at + x : at + x + size, :])

    def sides(low, high):
        pl.when(col > 0)(functools.partial(bands, low, 0))
        pl.when(col < ncol - 1)(functools.partial(bands, high, 1))

    by_parity(sides, even, odd)


def kept_lines():
    for side in range(2):
        for k in range(1, SWEEPS):
            flip = lambda x: CX - 1 - x if side else x
            yield side, k, (flip(k), flip(k + 1)), flip(k)


def smooth_middle(
    nrow, ncol, reaction, b, material, even, odd,
    first, scaled, coarse, keep_p, keep_s, keep_sum,
    s, inv, p0, p1, p2, p3, code, pair,
):
    parts = (p0, p1, p2, p3)
    lay_own(0, range(CX), b, material, s, code)
    lay_bands(0, ((0, CX),), ncol, putter(s, code), even, odd)
    every(0, CX, lambda x: fine_scale(x, reaction, code, s, inv, p0))
    for k in range(SWEEPS - 1):
        every(k + 1, CX - k - 1, lambda x: fine_sweep(x, k, s, inv, parts))
        for side, step, lines, line in kept_lines():
            if step == k + 1:
                for f in range(FIELDS):
                    for i, x in enumerate(lines):
                        keep_p[side, k, i, f] = parts[step][f, x]
                    keep_s[side, k, f] = s[f, line, ALL, :]
    for x in range(*MID, 2):
        residues = []
        for h in range(2):
            line = (x + h - MID[0]) * CY
            residues.append(fine_last(x + h, reaction, code, s, inv, p3, scaled, line))
            for f in range(FIELDS):
                first[f, line : line + CY, :] = sum(p[f, x + h, OWN, :] for p in parts)
        restrict(x, residues, code, pair, coarse, (x - MID[0]) // 2 * HY)
    for side in range(2):
        for i in range(1, SWEEPS):
            x = CX - 1 - i if side else i
            for f in range(FIELDS):
                keep_sum[side, i - 1, f] = sum(p[f, x, OWN, :] for p in parts[: i + 1])


def smooth_outer(
    nrow, ncol, reaction, b, material, above, below, even, odd, kabove, kbelow,
    mid_first, mid_scaled, mid_coarse, keep_p, keep_s, keep_sum,
    first, scaled, code, coarse, up, down, side_even, side_odd,
    s, inv, p0, p1, p2, p3, pair,
):
    row, col = place()
    parts = (p0, p1, p2, p3)
    at_x = 6
    zeros = jnp.zeros((FN, CZ), jnp.float32)
    for x in (*range(6), *range(GX - 6, GX)):
        for f in range(FIELDS):
            s[f, x, ALL, :] = zeros
        code[x, ALL, :] = zeros + 2.0
    outer = (*range(4), *range(CX - 4, CX))
    lay_own(at_x, outer, b, material, s, code)
    for x in range(4, CX - 4):
        code[x + at_x, OWN, :] = material[x * CY : x * CY + CY, :].astype(jnp.float32)
        code[x + at_x, FO + CY : FO + FN, :] = zeros[:8] + 2.0
    put = putter(s, code)

    def rows(first_x, ref):
        for i in range(6):
            for f in range(FIELDS):
                at = (f * 6 + i) * CY
                s[f, first_x + i, OWN, :] = ref[at : at + CY, :]
            at = (FIELDS * 6 + i) * CY
            code[first_x + i, OWN, :] = ref[at : at + CY, :]

    pl.when(row > 0)(functools.partial(rows, 0, above))
    pl.when(row < nrow - 1)(functools.partial(rows, GX - 6, below))
    lay_bands(at_x, ((0, CX),), ncol, put, even, odd)

    def corners(ref, is_above, is_high):
        for f in range(FIELDS + 1):
            for j, offset in FINE_CORNER_AT.items():
                size = 6 - j
                at = (f * 2 + is_high) * 16 + offset
                x = 6 - size if is_above else 6 + CX
                put(f, x, halo_row(j, is_high), size, ref[at : at + size, :])

    for ref, is_above, in_x in ((kabove, 1, row > 0), (kbelow, 0, row < nrow - 1)):
        for is_high, in_y in ((0, col > 0), (1, col < ncol - 1)):
            pl.when(in_x & in_y)(functools.partial(corners, ref, is_above, is_high))

    def both(low, high, step):
        for x in range(low, high):
            step(x + at_x)
            step(CX - 1 - x + at_x)

    both(-6, 2, lambda x: fine_scale(x, reaction, code, s, inv, p0))
    both(2, 4, lambda x: fine_scale(x, reaction, code, s, inv, None))
    for side, k, lines, line in kept_lines():
        for f in range(FIELDS):
            for i, x in enumerate(lines):
                parts[k][f, x + at_x] = keep_p[side, k - 1, i, f]
    for k in range(SWEEPS - 1):
        if k > 0:
            for side, step, lines, line in kept_lines():
                if step == k:
                    for f in range(FIELDS):
                        s[f, line + at_x, ALL, :] = keep_s[side, k - 1, f]
        both(k - 5, k + 1, lambda x: fine_sweep(x, k, s, inv, parts))
    for side, step, lines, line in kept_lines():
        if step == SWEEPS - 1:
            for f in range(FIELDS):
                s[f, line + at_x, ALL, :] = keep_s[side, step - 1, f]
    for x in (*range(-2, 4, 2), *range(CX - 4, CX + 2, 2)):
        residues = []
        for h in range(2):
            line = (x + h + 2) * CY
            residues.append(
                fine_last(x + h + at_x, reaction, code, s, inv, p3, scaled, line)
            )
        restrict(x + at_x, residues, code, pair, coarse, (x // 2 + 1) * HY)
    for f in range(FIELDS):
        for x in range(CX):
            out = slice(x * CY, x * CY + CY)
            side = x >= CX // 2
            i = CX - 1 - x if side else x
            if i < 4:
                some = [p[f, x + at_x, OWN, :] for p in (parts if i == 0 else parts[i + 1 :])]
                if i > 0:
                    some.append(keep_sum[int(side), i - 1, f])
                first[f, out, :] = sum(some)
            else:
                mid = slice((x - MID[0]) * CY, (x - MID[0] + 1) * CY)
                first[f, out, :] = mid_first[f, mid, :]
                scaled[f, (x + 2) * CY : (x + 3) * CY, :] = mid_scaled[f, mid, :]
    for plane in range(3):
        size = (MID[1] - MID[0]) // 2 * HY
        at = (MID[0] // 2 + 1) * HY
        coarse[plane, at : at + size, :] = mid_coarse[plane]

    for f in range(FIELDS):
        at = COARSE_LINES + f * CY
        up[at : at + CY, :] = scaled[f, (CX - 1) * CY : CX * CY, :]
        down[at : at + CY, :] = scaled[f, 4 * CY : 5 * CY, :]
    for plane in range(3):
        at, size = plane * (HX + 1) * HY, (HX + 1) * HY
        up[at : at + size, :] = coarse[plane, 0:size, :]
        down[at : at + size, :] = coarse[plane, HY : HY + size, :]

    def kin(low, high):
        for part, ref in enumerate((low, high)):
            value = ref[BAND_LINES : BAND_LINES + KIN_LINES, :]
            at = FACE_KIN + part * KIN_LINES
            up[at : at + KIN_LINES, :] = value
            down[at : at + KIN_LINES, :] = value

    by_parity(kin, even, odd)

    def strips(left, right):
        for plane in range(3):
            for i in range(9):
                at = (plane * 9 + i) * VX
                right[at : at + VX, :] = coarse[plane, pl.ds(HY - 9 + i, VX, stride=HY), :]
                left[at : at + VX, :] = coarse[plane, pl.ds(i, VX, stride=HY), :]
        for f in range(FIELDS):
            for j, offset in STRIP_AT.items():
                size = WX + 2 - 2 * j
                at = STRIP_LINES + f * (3 * WX - 6) + offset
                x = (j - 1) * CY
                right[at : at + size, :] = scaled[f, pl.ds(x + CY - j, size, stride=CY), :]
                left[at : at + size, :] = scaled[f, pl.ds(x + j - 1, size, stride=CY), :]

    by_parity(strips, side_even, side_odd)


def pack_knots(first, second, up, down):
    def pack(low, high):
        for plane in range(3):
            for side, ref in enumerate((low, high)):
                base = (plane * 2 + side) * CORNER_LINES
                up[base + 40 : base + 48, :] = jnp.zeros((8, CZ), jnp.float32)
                down[base + 40 : base + 48, :] = jnp.zeros((8, CZ), jnp.float32)
                for j, offset in CORNER_AT.items():
                    size = 10 - j
                    line = (plane * 9 + (j - 1 if side else 9 - j)) * VX
                    at = base + offset
                    up[at : at + size, :] = ref[line + VX - 1 - size : line + VX - 1, :]
                    down[at : at + size, :] = ref[line + 1 : line + 1 + size, :]

    by_parity(pack, first, second)


def coarse_constants(reaction, plane):
    parity = lanes() % 2 == 0
    even, odd = (
        [reaction[2 * f + i : 2 * f + i + 1, :] for i in range(2)]
        for f in (2 * plane, 2 * plane + 1)
    )
    low = jnp.where(parity, even[0], odd[0])
    return 8.0 * low, jnp.where(parity, even[1] - even[0], odd[1] - odd[0])


def smooth_coarse(
    nrow, ncol, reaction, coarse, above, below, even, odd, kabove, kbelow,
    start, scaled, inverse_out, sums,
    s, inv, count, p0, p1, p2, p3,
):
    row, col = place()
    parts = (p0, p1, p2, p3)
    zeros = jnp.zeros((QY, CZ), jnp.float32)

    def clear(x):
        for plane in range(2):
            s[plane, x] = zeros
        count[x] = zeros - 1.0

    every(0, QX, clear)
    sflat = s.reshape(2, QX * QY, CZ)
    cflat = count.reshape(QX * QY, CZ)

    def put(plane, start_row, size, value):
        if plane < 2:
            sflat[plane, pl.ds(start_row, size, stride=QY), :] = value
        else:
            cflat[pl.ds(start_row, size, stride=QY), :] = value

    def block(plane, x, value):
        if plane < 2:
            s[plane, x, QO : QO + HY, :] = value
        else:
            count[x, QO : QO + HY, :] = value

    def rows(first_x, ref):
        for plane in range(3):
            for i in range(HX + 1):
                at = (plane * (HX + 1) + i) * HY
                block(plane, first_x + i, ref[at : at + HY, :])

    for plane in range(3):
        for i in range(HX):
            block(plane, 9 + i, coarse[plane, (i + 1) * HY : (i + 2) * HY, :])
    pl.when(row > 0)(functools.partial(rows, 0, above))
    pl.when(row < nrow - 1)(functools.partial(rows, 9 + HX, below))

    def strips(ref, first_y):
        for plane in range(3):
            for i in range(9):
                line = (plane * 9 + i) * VX
                put(plane, 9 * QY + first_y + i, HX, ref[line + 1 : line + 1 + HX, :])

    def sides(low, high):
        pl.when(col > 0)(functools.partial(strips, low, QO - 9))
        pl.when(col < ncol - 1)(functools.partial(strips, high, QO + HY))

    by_parity(sides, even, odd)

    def corners(ref, is_above, is_high):
        for plane in range(3):
            base = (plane * 2 + is_high) * CORNER_LINES
            for j, at in CORNER_AT.items():
                size = 10 - j
                x = 9 - size if is_above else 9 + HX
                y = QO + HY - 1 + j if is_high else QO - j
                put(plane, x * QY + y, size, ref[base + at : base + at + size, :])

    for ref, is_above, in_x in ((kabove, 1, row > 0), (kbelow, 0, row < nrow - 1)):
        for is_high, in_y in ((0, col > 0), (1, col < ncol - 1)):
            pl.when(in_x & in_y)(functools.partial(corners, ref, is_above, is_high))

    def scale(x):
        number = count[x]
        for plane in range(2):
            low8, jump = coarse_constants(reaction, plane)
            inverse = jnp.where(number < 0.0, 0.0, 1.0 / (6.0 + 0.5 * (low8 + jump * number)))
            value = inverse * s[plane, x]
            inv[plane, x] = inverse
            s[plane, x] = value
            p0[plane, x] = value * (1.0 / THETA)

    every(0, QX, scale)

    for k, (keep, gain) in enumerate(coefficients()):
        def sweep(x):
            for plane in range(2):
                here, total = beside(parts[k], plane, x, 8, 32, 2)
                value = s[plane, x, 8:40, :] - here + inv[plane, x, 8:40, :] * total
                s[plane, x, 8:40, :] = value
                parts[k + 1][plane, x, 8:40, :] = keep * here + gain * value

        every(k + 1, QX - k - 1, sweep)

    def finish(x):
        for plane in range(2):
            here, total = beside(p3, plane, x, 8, 32, 2)
            value = s[plane, x, 8:40, :] - here + inv[plane, x, 8:40, :] * total
            scaled[plane, x - 4] = value
            inverse_out[plane, x - 4] = inv[plane, x, 8:40, :]

    every(4, QX - 4, finish)

    def add(x):
        for plane in range(2):
            start[plane, x - 7] = (
                p0[plane, x, 8:40, :] + p1[plane, x, 8:40, :]
                + p2[plane, x, 8:40, :] + p3[plane, x, 8:40, :]
            )

    every(7, QX - 7, add)

    lane = lanes()
    message = jnp.zeros((8, CZ), jnp.float32)
    for plane in range(2):
        low8, jump = coarse_constants(reaction, plane)
        total = jnp.zeros((HY, CZ), jnp.float32)
        for x in range(9, 9 + HX):
            diagonal = 6.0 + 0.5 * (low8 + jump * count[x, QO : QO + HY, :])
            total = total + diagonal * scaled[plane, x - 4, 8 : 8 + HY, :]
        total = total[:8] + total[8:]
        for shift in (4, 2, 1):
            total = total + pltpu.roll(total, shift, 0)
        for shift in (2, 4, 8):
            total = total + pltpu.roll(total, CZ - shift, 1)
        for odd in range(2):
            for g in range(GROUPS):
                to = (2 * plane + odd) * GROUPS + g
                moved = pltpu.roll(total, (to - 16 * g - odd) % CZ, 1)
                message = jnp.where(lane == to, moved, message)
    sums[...] = jnp.broadcast_to(message[:1], sums.shape)


def smooth_second(
    nrow, ncol, reaction, gathered, kin_mine, kin_up, kin_down, mine,
    start, qscaled, qinverse, first, scaled, code, above, below, even, odd,
    out,
    wide, spread, e, q0, q1, q2, q3, qs, fs, inv, f0, p0, p1, p2,
):
    row, col = place()
    lane = lanes()
    width = ncol * GROUPS
    fields = [jnp.zeros((nrow, CZ), jnp.float32) for _ in range(FIELDS)]
    for c in range(ncol):
        some = gathered[pl.ds(c, nrow, stride=ncol), :]
        for f in range(FIELDS):
            moved = pltpu.roll(some, (c * GROUPS - f * GROUPS) % CZ, 1)
            here = (lane >= c * GROUPS) & (lane < (c + 1) * GROUPS)
            fields[f] = jnp.where(here, moved, fields[f])
    for f in range(FIELDS):
        wide[f] = fields[f]

    group = lax.broadcasted_iota(jnp.int32, (GROUPS, CZ), 0)
    spot = lax.broadcasted_iota(jnp.int32, (GROUPS, CZ), 1)
    mask = [(spot // 16 == group) & (spot % 2 == odd) for odd in range(2)]
    e[...] = jnp.zeros_like(e)

    def product(rows_of, f):
        total = jnp.zeros((GROUPS, width), jnp.float32)
        for k in range(nrow):
            total = total + rows_of(f, k) * wide[f, k : k + 1, 0:width]
        return jnp.sum(total, axis=1, keepdims=True)

    def neighbour(rows_of, dx, dy):
        for plane in range(2):
            even = product(rows_of, 2 * plane)
            odd = product(rows_of, 2 * plane + 1)
            full = jnp.where(mask[0], even, jnp.where(mask[1], odd, 0.0))
            line = jnp.sum(full, axis=0, keepdims=True)
            x_from, x_to = {-1: (0, 6), 0: (6, 6 + HX), 1: (6 + HX, EX)}[dx]
            y_from, y_to = {-1: (8, QO), 0: (QO, QO + HY), 1: (QO + HY, QO + HY + 8)}[dy]
            for x in range(x_from, x_to):
                e[plane, x, y_from:y_to, :] = jnp.broadcast_to(line, (y_to - y_from, CZ))

    def slab(ref, part):
        def rows_of(f, k):
            at = (f * GROUPS + k) * GROUPS
            if part is None:
                return ref[FINE_CORNER_LINES + at : FINE_CORNER_LINES + at + GROUPS, :]
            at += FACE_KIN + part * KIN_LINES
            return ref[at : at + GROUPS, :]

        return rows_of

    in_x = {-1: row > 0, 0: True, 1: row < nrow - 1}
    in_y = {-1: col > 0, 0: True, 1: col < ncol - 1}
    for dx, row_ref, ref in ((0, kin_mine, mine), (-1, kin_up, above), (1, kin_down, below)):
        for part, dy in ((None, 0), (0, -1), (1, 1)):
            given = row_ref if part is None else ref
            step = functools.partial(neighbour, slab(given, part), dx, dy)
            if dx == 0 and dy == 0:
                step()
            else:
                pl.when(in_x[dx] & in_y[dy])(step)

    parts = (q0, q1, q2, q3)

    def begin(x):
        for plane in range(2):
            here, total = beside(e, plane, x, 8, 32, 2)
            value = qscaled[plane, x - 1] - here + qinverse[plane, x - 1] * total
            qs[plane, x] = value
            q0[plane, x, 8:40, :] = value * (1.0 / THETA)

    every(1, EX - 1, begin)
    for k, (keep, gain) in enumerate(coefficients()):
        def sweep(x):
            for plane in range(2):
                here, total = beside(parts[k], plane, x, 8, 32, 2)
                value = qs[plane, x] - here + qinverse[plane, x - 1] * total
                qs[plane, x] = value
                parts[k + 1][plane, x, 8:40, :] = keep * here + gain * value

        every(k + 2, EX - k - 2, sweep)

    parity = lane % 2 == 0

    def lift(i):
        for plane in range(2):
            total = start[plane, i] + e[plane, i + 4, 8:40, :]
            total = total + q0[plane, i + 4, 8:40, :] + q1[plane, i + 4, 8:40, :]
            total = total + q2[plane, i + 4, 8:40, :] + q3[plane, i + 4, 8:40, :]
            for odd in range(2):
                if odd:
                    value = jnp.where(parity, pltpu.roll(total, CZ - 1, 1), total)
                else:
                    value = jnp.where(parity, total, pltpu.roll(total, 1, 1))
                spread[...] = value
                high, low = spread[8:26, :], spread[6:8, :]
                for h in range(2):
                    to = f0.at[2 * plane + odd, i * 2 + h]
                    for y in range(2):
                        to[pl.ds(FO + y, 18, stride=2), :] = high
                        to[pl.ds(FO + FN - 4 + y, 2, stride=2), :] = low
                    to[FO - 1 : FO, :] = low[1:2]
                    to[FO + FN : FO + FN + 1, :] = high[0:1]

    every(0, HX + 4, lift)

    zeros = jnp.zeros((FN, CZ), jnp.float32)
    for f in range(FIELDS):
        for x in (1, FX - 2):
            fs[f, x, ALL, :] = zeros
        for x in range(2, FX - 2):
            fs[f, x, OWN, :] = scaled[f, (x - 2) * CY : (x - 1) * CY, :]
            fs[f, x, FO + CY : FO + FN, :] = zeros[:8]
    sflat = fs.reshape(FIELDS, FX * FY, CZ)

    def face(x, ref):
        for f in range(FIELDS):
            at = COARSE_LINES + f * CY
            fs[f, x, OWN, :] = ref[at : at + CY, :]

    pl.when(in_x[-1])(functools.partial(face, 1, above))
    pl.when(in_x[1])(functools.partial(face, FX - 2, below))

    def strips(ref, is_high):
        for f in range(FIELDS):
            for j, offset in STRIP_AT.items():
                size = WX + 2 - 2 * j
                at = STRIP_LINES + f * (3 * WX - 6) + offset
                start = (1 + j) * FY + halo_row(j, is_high)
                sflat[f, pl.ds(start, size, stride=FY), :] = ref[at : at + size, :]

    def sides(low, high):
        pl.when(in_y[-1])(functools.partial(strips, low, 0))
        pl.when(in_y[1])(functools.partial(strips, high, 1))

    by_parity(sides, even, odd)

    parts = (p0, p1, p2)

    def open_fine(x):
        kind = code[x + 2, ALL, :]
        for f in range(FIELDS):
            here, total = beside(f0, f, x, FO, FN, 1)
            inverse = inverse_of(kind, reaction, f)
            inv[f, x, ALL, :] = inverse
            value = fs[f, x, ALL, :] - here + inverse * total
            fs[f, x, ALL, :] = value
            go_round(p0, f, x, value * (1.0 / THETA))

    every(1, FX - 1, open_fine)
    for k in range(2):
        every(k + 2, FX - k - 2, lambda x: fine_sweep(x, k, fs, inv, parts))

    keep, gain = coefficients()[2]

    def close(i):
        x = i + 4
        at = pl.ds(i * CY, CY)
        for f in range(FIELDS):
            here, total = beside(p2, f, x, FO, CY, 1)
            value = fs[f, x, OWN, :] - here + inv[f, x, OWN, :] * total
            result = first[f, at, :] + f0[f, x, OWN, :] + p0[f, x, OWN, :]
            result = result + p1[f, x, OWN, :] + here
            out[f, at, :] = result + (keep * here + gain * value)

    every(0, CX, close)


def call(kernel, out_shapes, scratch, *args, limit=16, in_hbm=False, microseconds=0.1):
    vmem = pl.BlockSpec(memory_space=pltpu.VMEM)
    given = pl.BlockSpec(memory_space=pltpu.HBM) if in_hbm else vmem
    return pl.pallas_call(
        kernel,
        out_shape=[jax.ShapeDtypeStruct(shape, jnp.float32) for shape in out_shapes],
        in_specs=[given] * len(args),
        out_specs=[vmem] * len(out_shapes),
        scratch_shapes=[
            pltpu.VMEM(shape, jnp.float32) if isinstance(shape, tuple) else shape
            for shape in scratch
        ],
        cost_estimate=pl.CostEstimate(
            flops=int(microseconds * 1e6), bytes_accessed=int(microseconds * 3.5e6), transcendentals=0
        ),
        compiler_params=pltpu.CompilerParams(vmem_limit_bytes=int(limit * 1024 * 1024)),
    )(*args)


def ahead(value):
    count = lax.axis_size("row")
    return lax.ppermute(value, "row", [(i, (i + 1) % count) for i in range(count)])


def back(value):
    count = lax.axis_size("row")
    return lax.ppermute(value, "row", [((i + 1) % count, i) for i in range(count)])


def pairs(value, odd):
    nrow, ncol = lax.axis_size("row"), lax.axis_size("col")
    moves = []
    for r in range(nrow):
        for c in range(ncol):
            if not odd:
                to = (r, c ^ 1)
            elif c in (0, ncol - 1):
                to = (r ^ 1, c)
            else:
                to = (r, c + 1 if c % 2 else c - 1)
            moves.append((r * ncol + c, to[0] * ncol + to[1]))
    return lax.ppermute(value, ("row", "col"), moves)


def body(right_side, material, reaction, coarse_inverse):
    nrow, ncol = lax.axis_size("row"), lax.axis_size("col")
    b = right_side.reshape(FIELDS, CX * CY, CZ)
    material = material.reshape(CX * CY, CZ)

    fine = (FIELDS, CX * CY, CZ)
    up, down, even, odd = call(
        pack_layers,
        [(LAYER_LINES, CZ)] * 2 + [(BAND_LINES + KIN_LINES, CZ)] * 2,
        [fine, pltpu.VMEM(fine[1:], jnp.int32), coarse_inverse.shape,
         pltpu.SemaphoreType.DMA((FIELDS + 2,))],
        b, material, coarse_inverse,
        in_hbm=True, limit=59.27,
    )
    odd, even = pairs(odd, True), pairs(even, False)
    above, below = ahead(up), back(down)
    up, down, reaction = call(
        pack_corners,
        [(FINE_CORNER_LINES + KIN_LINES, CZ)] * 2 + [(2 * FIELDS, CZ)], [],
        even, odd, reaction.T, coarse_inverse,
    )
    mine = up
    kabove, kbelow = ahead(up), back(down)
    wide = (FIELDS, WX * CY, CZ)
    middle = MID[1] - MID[0]
    padded = (FIELDS, CX, FY, CZ)
    mids = call(
        functools.partial(smooth_middle, nrow, ncol),
        [(FIELDS, middle * CY, CZ)] * 2 + [(3, middle // 2 * HY, CZ),
         (2, 3, 2, FIELDS, FY, CZ), (2, 3, FIELDS, FN, CZ), (2, 3, FIELDS, CY, CZ)],
        [padded] * 6 + [padded[1:], (2, FIELDS + 1, CY, CZ)],
        reaction, b, material, even, odd,
        limit=16, microseconds=3,
    )
    padded = (FIELDS, GX, FY, CZ)
    first, scaled, code, coarse, up, down, side_even, side_odd = call(
        functools.partial(smooth_outer, nrow, ncol),
        [fine, wide, padded[1:], (3, VX * HY, CZ)]
        + [(FACE_LINES, CZ)] * 2 + [(SIDE_LINES, CZ)] * 2,
        [padded] * 6 + [(2, FIELDS + 1, CY, CZ)],
        reaction, b, material, above, below, even, odd, kabove, kbelow, *mids,
        limit=26, microseconds=3.5,
    )
    kin_row = (mine, kabove, kbelow)
    mine = up
    odd, even = pairs(side_odd, True), pairs(side_even, False)
    above, below = ahead(up), back(down)
    up, down = call(pack_knots, [(KNOT_LINES, CZ)] * 2, [], even, odd)
    kabove, kbelow = ahead(up), back(down)

    qpadded = (2, QX, QY, CZ)
    start, qscaled, qinverse, sums = call(
        functools.partial(smooth_coarse, nrow, ncol),
        [(2, HX + 4, 32, CZ), (2, HX + 10, 32, CZ), (2, HX + 10, 32, CZ), (nrow * ncol, CZ)],
        [qpadded, qpadded, qpadded[1:]] + [qpadded] * 4,
        reaction, coarse, above, below, even, odd, kabove, kbelow,
        limit=14, microseconds=2.5,
    )

    gathered = lax.all_to_all(sums, ("row", "col"), 0, 0)

    epadded = (2, EX, QY, CZ)
    padded = (FIELDS, FX, FY, CZ)
    (out,) = call(
        functools.partial(smooth_second, nrow, ncol),
        [fine],
        [(FIELDS, nrow, CZ), (32, CZ)] + [epadded] * 5 + [(2, EX, 32, CZ)] + [padded] * 6,
        reaction, gathered, *kin_row, mine,
        start, qscaled, qinverse, first, scaled, code, above, below, even, odd,
        limit=32, microseconds=7,
    )
    return out.reshape(right_side.shape)


def solution(mesh):
    placed = (
        P(None, "row", "col", None),
        P("row", "col", None),
        P(),
        P(None, ("row", "col"), None),
    )
    return jax.shard_map(
        body, mesh=mesh, in_specs=placed, out_specs=P(None, "row", "col", None), check_vma=False
    )
```

```python
import functools

import jax
import jax.numpy as jnp
from jax import lax
from jax.experimental import pallas as pl
from jax.experimental.pallas import tpu as pltpu
from jax.sharding import PartitionSpec as P

FIELDS = 4
CX, CY, CZ = 16, 32, 128
HX, HY = CX // 2, CY // 2
GROUPS = 8
SWEEPS = 4
LOW_BOUND = 0.25
HIGH_BOUND = 2.0
THETA = (HIGH_BOUND + LOW_BOUND) / 2.0
DELTA = (HIGH_BOUND - LOW_BOUND) / 2.0

WX = CX + 4
GX, FY, FO, FN = CX + 12, CY + 24, 8, CY + 8
OWN = slice(FO, FO + CY)
ALL = slice(FO, FO + FN)
FX = CX + 8
MID = (4, CX - 4)
VX = HX + 2
QX, QY, QO = HX + 18, HY + 32, 16
EX = HX + 12
CORNER_AT = {1: 0, 2: 9, 3: 17, 4: 24, 5: 30, 6: 35, 7: 39, 8: 42, 9: 44}
CORNER_LINES = 48
FINE_CORNER_AT = {1: 0, 2: 5, 3: 9, 4: 12}
FINE_CORNER_LINES = (FIELDS + 1) * 32

LAYER_LINES = (FIELDS + 1) * 6 * CY
BAND_LINES = (FIELDS + 1) * 4 * CX
KIN_LINES = FIELDS * GROUPS * 8
COARSE_LINES = 3 * (HX + 1) * HY
FACE_LINES = COARSE_LINES + FIELDS * CY
STRIP_LINES = 272
STRIP_AT = {1: 0, 2: WX, 3: 2 * WX - 2}
SIDE_LINES = STRIP_LINES + FIELDS * (3 * WX - 6)
KNOT_LINES = 6 * CORNER_LINES


def coefficients():
    rho = DELTA / THETA
    pairs = []
    for _ in range(SWEEPS - 1):
        following = 1.0 / (2.0 * THETA / DELTA - rho)
        pairs.append((following * rho, 2.0 * following / DELTA))
        rho = following
    return pairs


def every(low, high, step):
    for i in range(low, high):
        step(i)


def lanes():
    return lax.broadcasted_iota(jnp.int32, (1, CZ), 1)


def beside(ref, f, x, low, count, width):
    here = ref[f, x, low : low + count, :]
    lane = lanes()
    total = ref[f, x + 1, low : low + count, :] + ref[f, x - 1, low : low + count, :]
    total = total + ref[f, x, low + 1 : low + 1 + count, :]
    total = total + ref[f, x, low - 1 : low - 1 + count, :]
    total = total + jnp.where(lane < CZ - width, pltpu.roll(here, CZ - width, 1), 0.0)
    total = total + jnp.where(lane >= width, pltpu.roll(here, width, 1), 0.0)
    return here, total


def diagonal_values(reaction, f):
    low = reaction[2 * f : 2 * f + 1, :]
    jump = reaction[2 * f + 1 : 2 * f + 2, :] - low
    return 6.0 + low, 6.0 + low + jump


def inverse_of(code, reaction, f):
    fluid, solid = diagonal_values(reaction, f)
    fluid, solid = 1.0 / fluid, 1.0 / solid
    return jnp.where(code == 0.0, fluid, jnp.where(code == 1.0, solid, 0.0))


def place():
    return lax.axis_index("row"), lax.axis_index("col")


def by_parity(step, first, second):
    even = lax.rem(lax.axis_index("col"), 2) == 0
    pl.when(even)(functools.partial(step, second, first))
    pl.when(jnp.logical_not(even))(functools.partial(step, first, second))


def pack_layers(
    b, material, inverse, up, down, first, second, own,
    b_here, material_here, inverse_here, solid, first_here, second_here, own_here, sems, out_sems,
):
    copies = [pltpu.make_async_copy(b.at[f], b_here.at[f], sems.at[f]) for f in range(FIELDS)]
    copies.append(pltpu.make_async_copy(material, material_here, sems.at[FIELDS]))
    copies.append(pltpu.make_async_copy(inverse, inverse_here, sems.at[FIELDS + 1]))
    for copy in copies:
        copy.start()
    sent = []

    def send(source, target):
        sent.append(pltpu.make_async_copy(source, target, out_sems.at[len(sent)]))
        sent[-1].start()

    for f in range(FIELDS + 1):
        copies[f].wait()
        layer, band = 6 * CY, 4 * CX
        if f < FIELDS:
            take = lambda start, size, step: b_here[f, pl.ds(start, size, stride=step), :]
            ends = (b_here.at[f, pl.ds((CX - 6) * CY, layer)], b_here.at[f, pl.ds(0, layer)])
        else:
            take = lambda start, size, step: material_here[
                pl.ds(start, size, stride=step), :
            ].astype(jnp.float32)
            solid[0] = take((CX - 6) * CY, layer, 1)
            solid[1] = take(0, layer, 1)
            ends = (solid.at[0], solid.at[1])
        for source, target in zip(ends, (up, down)):
            send(source, target.at[pl.ds(f * layer, layer)])

        def bands(left, right):
            for i in range(4):
                at = f * band + i * CX
                right[at : at + CX, :] = take(CY - 4 + i, CX, CY)
                left[at : at + CX, :] = take(i, CX, CY)

        by_parity(bands, first_here, second_here)
        for source, target in ((first_here, first), (second_here, second)):
            send(source.at[pl.ds(f * band, band)], target.at[pl.ds(f * band, band)])
    copies[FIELDS + 1].wait()
    for f in range(FIELDS):
        for k in range(inverse.shape[2] // CZ):
            at = (f * GROUPS + k) * GROUPS
            own_here[at : at + GROUPS, :] = inverse_here[f, :, k * CZ : (k + 1) * CZ]
    send(own_here, own)
    for copy in sent:
        copy.wait()


def pack_corners(first, second, reaction, up, down, constants):
    for f in range(FIELDS):
        for i in range(2):
            constants[2 * f + i : 2 * f + i + 1, :] = jnp.broadcast_to(
                reaction[i : i + 1, f : f + 1], (1, CZ)
            )

    def pack(low, high):
        for side, ref in enumerate((low, high)):
            for f in range(FIELDS + 1):
                for j, offset in FINE_CORNER_AT.items():
                    size = 6 - j
                    line = (f * 4 + (j - 1 if side else 4 - j)) * CX
                    at = (f * 2 + side) * 16 + offset
                    up[at : at + size, :] = ref[line + CX - size : line + CX, :]
                    down[at : at + size, :] = ref[line : line + size, :]
                at = (f * 2 + side) * 16 + 14
                up[at : at + 2, :] = jnp.zeros((2, CZ), jnp.float32)
                down[at : at + 2, :] = jnp.zeros((2, CZ), jnp.float32)

    by_parity(pack, first, second)


def halo_row(j, is_high):
    return FO + CY - 1 + j if is_high else FO + FN - j


def go_round(ref, f, x, value):
    ref[f, x, ALL, :] = value
    ref[f, x, FO - 1 : FO, :] = value[FN - 1 : FN]
    ref[f, x, FO + FN : FO + FN + 1, :] = value[0:1]


def fine_scale(x, reaction, code, s, inv, p0):
    kind = code[x, ALL, :]
    for f in range(FIELDS):
        inverse = inverse_of(kind, reaction, f)
        inv[f, x, ALL, :] = inverse
        if p0 is not None:
            value = inverse * s[f, x, ALL, :]
            s[f, x, ALL, :] = value
            go_round(p0, f, x, value * (1.0 / THETA))


def fine_sweep(x, k, s, inv, parts):
    keep, gain = coefficients()[k]
    for f in range(FIELDS):
        here, total = beside(parts[k], f, x, FO, FN, 1)
        value = s[f, x, ALL, :] - here + inv[f, x, ALL, :] * total
        s[f, x, ALL, :] = value
        go_round(parts[k + 1], f, x, keep * here + gain * value)


def fine_last(x, reaction, code, s, inv, p3, scaled, line):
    residues = []
    for f in range(FIELDS):
        fluid, solid = diagonal_values(reaction, f)
        here, total = beside(p3, f, x, FO, CY, 1)
        value = s[f, x, OWN, :] - here + inv[f, x, OWN, :] * total
        scaled[f, line : line + CY, :] = value
        residues.append(jnp.where(code[x, OWN, :] == 1.0, solid, fluid) * value)
    return residues


def restrict(x, residues, code, pair, coarse, line):
    parity = lanes() % 2 == 0
    sums = [one + other for one, other in zip(*residues)]
    sums.append(code[x, OWN, :] + code[x + 1, OWN, :])
    halves = []
    for f, value in enumerate(sums):
        here = pair.at[x // 2 % 2, f]
        here[...] = value
        halves.append(here[pl.ds(0, HY, stride=2), :] + here[pl.ds(1, HY, stride=2), :])
    halves.append(halves[4])
    for plane in range(3):
        even, odd = halves[2 * plane], halves[2 * plane + 1]
        merged = jnp.where(
            parity, even + pltpu.roll(even, CZ - 1, 1), odd + pltpu.roll(odd, 1, 1)
        )
        merged = merged * 0.5 if plane < 2 else jnp.where(merged > 8.5, -1.0, merged)
        coarse[plane, line : line + HY, :] = merged


def lay_own(x_at, xs, b, material, s, code):
    zeros = jnp.zeros((8, CZ), jnp.float32)
    for x in xs:
        for f in range(FIELDS):
            s[f, x + x_at, OWN, :] = b[f, x * CY : x * CY + CY, :]
            s[f, x + x_at, FO + CY : FO + FN, :] = zeros
        code[x + x_at, OWN, :] = material[x * CY : x * CY + CY, :].astype(jnp.float32)
        code[x + x_at, FO + CY : FO + FN, :] = zeros + 2.0


def putter(s, code):
    sflat = s.reshape(FIELDS, s.shape[1] * FY, CZ)
    cflat = code.reshape(s.shape[1] * FY, CZ)

    def put(f, x, y_row, size, value):
        to = pl.ds(x * FY + y_row, size, stride=FY)
        if f < FIELDS:
            sflat[f, to, :] = value
        else:
            cflat[to, :] = value

    return put


def lay_bands(x_at, spans, ncol, put, even, odd):
    _, col = place()

    def bands(ref, is_high):
        for f in range(FIELDS + 1):
            for i in range(4):
                at = (f * 4 + i) * CX
                row = halo_row(i + 1 if is_high else 4 - i, is_high)
                for x, size in spans:
                    put(f, x + x_at, row, size, ref[at + x : at + x + size, :])

    def sides(low, high):
        pl.when(col > 0)(functools.partial(bands, low, 0))
        pl.when(col < ncol - 1)(functools.partial(bands, high, 1))

    by_parity(sides, even, odd)


def kept_lines():
    for side in range(2):
        for k in range(1, SWEEPS):
            flip = lambda x: CX - 1 - x if side else x
            yield side, k, (flip(k), flip(k + 1)), flip(k)


def smooth_middle(
    nrow, ncol, reaction, b, material, even, odd,
    first, scaled, coarse, keep_p, keep_s, keep_sum,
    s, inv, p0, p1, p2, p3, code, pair,
):
    parts = (p0, p1, p2, p3)
    lay_own(0, range(CX), b, material, s, code)
    lay_bands(0, ((0, CX),), ncol, putter(s, code), even, odd)
    every(0, CX, lambda x: fine_scale(x, reaction, code, s, inv, p0))
    for k in range(SWEEPS - 1):
        every(k + 1, CX - k - 1, lambda x: fine_sweep(x, k, s, inv, parts))
        for side, step, lines, line in kept_lines():
            if step == k + 1:
                for f in range(FIELDS):
                    for i, x in enumerate(lines):
                        keep_p[side, k, i, f] = parts[step][f, x]
                    keep_s[side, k, f] = s[f, line, ALL, :]
    for x in range(*MID, 2):
        residues = []
        for h in range(2):
            line = (x + h - MID[0]) * CY
            residues.append(fine_last(x + h, reaction, code, s, inv, p3, scaled, line))
            for f in range(FIELDS):
                first[f, line : line + CY, :] = sum(p[f, x + h, OWN, :] for p in parts)
        restrict(x, residues, code, pair, coarse, (x - MID[0]) // 2 * HY)
    for side in range(2):
        for i in range(1, SWEEPS):
            x = CX - 1 - i if side else i
            for f in range(FIELDS):
                keep_sum[side, i - 1, f] = sum(p[f, x, OWN, :] for p in parts[: i + 1])


def smooth_outer(
    nrow, ncol, reaction, b, material, above, below, even, odd, kabove, kbelow,
    own, kin_even, kin_odd, mid_first, mid_scaled, mid_coarse, keep_p, keep_s, keep_sum,
    first, scaled, code, coarse, up, down, side_even, side_odd, kin,
    s, inv, p0, p1, p2, p3, pair,
):
    row, col = place()
    parts = (p0, p1, p2, p3)
    at_x = 6
    zeros = jnp.zeros((FN, CZ), jnp.float32)
    for x in (*range(6), *range(GX - 6, GX)):
        for f in range(FIELDS):
            s[f, x, ALL, :] = zeros
        code[x, ALL, :] = zeros + 2.0
    outer = (*range(4), *range(CX - 4, CX))
    lay_own(at_x, outer, b, material, s, code)
    for x in range(4, CX - 4):
        code[x + at_x, OWN, :] = material[x * CY : x * CY + CY, :].astype(jnp.float32)
        code[x + at_x, FO + CY : FO + FN, :] = zeros[:8] + 2.0
    put = putter(s, code)

    def rows(first_x, ref):
        for i in range(6):
            for f in range(FIELDS):
                at = (f * 6 + i) * CY
                s[f, first_x + i, OWN, :] = ref[at : at + CY, :]
            at = (FIELDS * 6 + i) * CY
            code[first_x + i, OWN, :] = ref[at : at + CY, :]

    pl.when(row > 0)(functools.partial(rows, 0, above))
    pl.when(row < nrow - 1)(functools.partial(rows, GX - 6, below))
    lay_bands(at_x, ((0, CX),), ncol, put, even, odd)

    def corners(ref, is_above, is_high):
        for f in range(FIELDS + 1):
            for j, offset in FINE_CORNER_AT.items():
                size = 6 - j
                at = (f * 2 + is_high) * 16 + offset
                x = 6 - size if is_above else 6 + CX
                put(f, x, halo_row(j, is_high), size, ref[at : at + size, :])

    for ref, is_above, in_x in ((kabove, 1, row > 0), (kbelow, 0, row < nrow - 1)):
        for is_high, in_y in ((0, col > 0), (1, col < ncol - 1)):
            pl.when(in_x & in_y)(functools.partial(corners, ref, is_above, is_high))

    def both(low, high, step):
        for x in range(low, high):
            step(x + at_x)
            step(CX - 1 - x + at_x)

    both(-6, 2, lambda x: fine_scale(x, reaction, code, s, inv, p0))
    both(2, 4, lambda x: fine_scale(x, reaction, code, s, inv, None))
    for side, k, lines, line in kept_lines():
        for f in range(FIELDS):
            for i, x in enumerate(lines):
                parts[k][f, x + at_x] = keep_p[side, k - 1, i, f]
    for k in range(SWEEPS - 1):
        if k > 0:
            for side, step, lines, line in kept_lines():
                if step == k:
                    for f in range(FIELDS):
                        s[f, line + at_x, ALL, :] = keep_s[side, k - 1, f]
        both(k - 5, k + 1, lambda x: fine_sweep(x, k, s, inv, parts))
    for side, step, lines, line in kept_lines():
        if step == SWEEPS - 1:
            for f in range(FIELDS):
                s[f, line + at_x, ALL, :] = keep_s[side, step - 1, f]
    for x in (*range(-2, 4, 2), *range(CX - 4, CX + 2, 2)):
        residues = []
        for h in range(2):
            line = (x + h + 2) * CY
            residues.append(
                fine_last(x + h + at_x, reaction, code, s, inv, p3, scaled, line)
            )
        restrict(x + at_x, residues, code, pair, coarse, (x // 2 + 1) * HY)
    for f in range(FIELDS):
        for x in range(CX):
            out = slice(x * CY, x * CY + CY)
            side = x >= CX // 2
            i = CX - 1 - x if side else x
            if i < 4:
                some = [p[f, x + at_x, OWN, :] for p in (parts if i == 0 else parts[i + 1 :])]
                if i > 0:
                    some.append(keep_sum[int(side), i - 1, f])
                first[f, out, :] = sum(some)
            else:
                mid = slice((x - MID[0]) * CY, (x - MID[0] + 1) * CY)
                first[f, out, :] = mid_first[f, mid, :]
                scaled[f, (x + 2) * CY : (x + 3) * CY, :] = mid_scaled[f, mid, :]
    for plane in range(3):
        size = (MID[1] - MID[0]) // 2 * HY
        at = (MID[0] // 2 + 1) * HY
        coarse[plane, at : at + size, :] = mid_coarse[plane]

    for f in range(FIELDS):
        at = COARSE_LINES + f * CY
        up[at : at + CY, :] = scaled[f, (CX - 1) * CY : CX * CY, :]
        down[at : at + CY, :] = scaled[f, 4 * CY : 5 * CY, :]
    for plane in range(3):
        at, size = plane * (HX + 1) * HY, (HX + 1) * HY
        up[at : at + size, :] = coarse[plane, 0:size, :]
        down[at : at + size, :] = coarse[plane, HY : HY + size, :]

    kin[0] = own[...]

    def gather(low, high):
        kin[1] = low[...]
        kin[2] = high[...]

    by_parity(gather, kin_even, kin_odd)

    def strips(left, right):
        for plane in range(3):
            for i in range(9):
                at = (plane * 9 + i) * VX
                right[at : at + VX, :] = coarse[plane, pl.ds(HY - 9 + i, VX, stride=HY), :]
                left[at : at + VX, :] = coarse[plane, pl.ds(i, VX, stride=HY), :]
        for f in range(FIELDS):
            for j, offset in STRIP_AT.items():
                size = WX + 2 - 2 * j
                at = STRIP_LINES + f * (3 * WX - 6) + offset
                x = (j - 1) * CY
                right[at : at + size, :] = scaled[f, pl.ds(x + CY - j, size, stride=CY), :]
                left[at : at + size, :] = scaled[f, pl.ds(x + j - 1, size, stride=CY), :]

    by_parity(strips, side_even, side_odd)


def pack_knots(first, second, up, down):
    def pack(low, high):
        for plane in range(3):
            for side, ref in enumerate((low, high)):
                base = (plane * 2 + side) * CORNER_LINES
                up[base + 40 : base + 48, :] = jnp.zeros((8, CZ), jnp.float32)
                down[base + 40 : base + 48, :] = jnp.zeros((8, CZ), jnp.float32)
                for j, offset in CORNER_AT.items():
                    size = 10 - j
                    line = (plane * 9 + (j - 1 if side else 9 - j)) * VX
                    at = base + offset
                    up[at : at + size, :] = ref[line + VX - 1 - size : line + VX - 1, :]
                    down[at : at + size, :] = ref[line + 1 : line + 1 + size, :]

    by_parity(pack, first, second)


def coarse_constants(reaction, plane):
    parity = lanes() % 2 == 0
    even, odd = (
        [reaction[2 * f + i : 2 * f + i + 1, :] for i in range(2)]
        for f in (2 * plane, 2 * plane + 1)
    )
    low = jnp.where(parity, even[0], odd[0])
    return 8.0 * low, jnp.where(parity, even[1] - even[0], odd[1] - odd[0])


def smooth_coarse(
    nrow, ncol, reaction, coarse, above, below, even, odd, kabove, kbelow,
    start, scaled, inverse_out, sums,
    s, inv, count, p0, p1, p2, p3,
):
    row, col = place()
    parts = (p0, p1, p2, p3)
    zeros = jnp.zeros((QY, CZ), jnp.float32)

    def clear(x):
        for plane in range(2):
            s[plane, x] = zeros
        count[x] = zeros - 1.0

    every(0, QX, clear)
    sflat = s.reshape(2, QX * QY, CZ)
    cflat = count.reshape(QX * QY, CZ)

    def put(plane, start_row, size, value):
        if plane < 2:
            sflat[plane, pl.ds(start_row, size, stride=QY), :] = value
        else:
            cflat[pl.ds(start_row, size, stride=QY), :] = value

    def block(plane, x, value):
        if plane < 2:
            s[plane, x, QO : QO + HY, :] = value
        else:
            count[x, QO : QO + HY, :] = value

    def rows(first_x, ref):
        for plane in range(3):
            for i in range(HX + 1):
                at = (plane * (HX + 1) + i) * HY
                block(plane, first_x + i, ref[at : at + HY, :])

    for plane in range(3):
        for i in range(HX):
            block(plane, 9 + i, coarse[plane, (i + 1) * HY : (i + 2) * HY, :])
    pl.when(row > 0)(functools.partial(rows, 0, above))
    pl.when(row < nrow - 1)(functools.partial(rows, 9 + HX, below))

    def strips(ref, first_y):
        for plane in range(3):
            for i in range(9):
                line = (plane * 9 + i) * VX
                put(plane, 9 * QY + first_y + i, HX, ref[line + 1 : line + 1 + HX, :])

    def sides(low, high):
        pl.when(col > 0)(functools.partial(strips, low, QO - 9))
        pl.when(col < ncol - 1)(functools.partial(strips, high, QO + HY))

    by_parity(sides, even, odd)

    def corners(ref, is_above, is_high):
        for plane in range(3):
            base = (plane * 2 + is_high) * CORNER_LINES
            for j, at in CORNER_AT.items():
                size = 10 - j
                x = 9 - size if is_above else 9 + HX
                y = QO + HY - 1 + j if is_high else QO - j
                put(plane, x * QY + y, size, ref[base + at : base + at + size, :])

    for ref, is_above, in_x in ((kabove, 1, row > 0), (kbelow, 0, row < nrow - 1)):
        for is_high, in_y in ((0, col > 0), (1, col < ncol - 1)):
            pl.when(in_x & in_y)(functools.partial(corners, ref, is_above, is_high))

    def scale(x):
        number = count[x]
        for plane in range(2):
            low8, jump = coarse_constants(reaction, plane)
            inverse = jnp.where(number < 0.0, 0.0, 1.0 / (6.0 + 0.5 * (low8 + jump * number)))
            value = inverse * s[plane, x]
            inv[plane, x] = inverse
            s[plane, x] = value
            p0[plane, x] = value * (1.0 / THETA)

    every(0, QX, scale)

    for k, (keep, gain) in enumerate(coefficients()):
        def sweep(x):
            for plane in range(2):
                here, total = beside(parts[k], plane, x, 8, 32, 2)
                value = s[plane, x, 8:40, :] - here + inv[plane, x, 8:40, :] * total
                s[plane, x, 8:40, :] = value
                parts[k + 1][plane, x, 8:40, :] = keep * here + gain * value

        every(k + 1, QX - k - 1, sweep)

    def finish(x):
        for plane in range(2):
            here, total = beside(p3, plane, x, 8, 32, 2)
            value = s[plane, x, 8:40, :] - here + inv[plane, x, 8:40, :] * total
            scaled[plane, x - 4] = value
            inverse_out[plane, x - 4] = inv[plane, x, 8:40, :]

    every(4, QX - 4, finish)

    def add(x):
        for plane in range(2):
            start[plane, x - 7] = (
                p0[plane, x, 8:40, :] + p1[plane, x, 8:40, :]
                + p2[plane, x, 8:40, :] + p3[plane, x, 8:40, :]
            )

    every(7, QX - 7, add)

    lane = lanes()
    message = jnp.zeros((8, CZ), jnp.float32)
    for plane in range(2):
        low8, jump = coarse_constants(reaction, plane)
        total = jnp.zeros((HY, CZ), jnp.float32)
        for x in range(9, 9 + HX):
            diagonal = 6.0 + 0.5 * (low8 + jump * count[x, QO : QO + HY, :])
            total = total + diagonal * scaled[plane, x - 4, 8 : 8 + HY, :]
        total = total[:8] + total[8:]
        for shift in (4, 2, 1):
            total = total + pltpu.roll(total, shift, 0)
        for shift in (2, 4, 8):
            total = total + pltpu.roll(total, CZ - shift, 1)
        for odd in range(2):
            for g in range(GROUPS):
                to = (2 * plane + odd) * GROUPS + g
                moved = pltpu.roll(total, (to - 16 * g - odd) % CZ, 1)
                message = jnp.where(lane == to, moved, message)
    sums[...] = jnp.broadcast_to(message[:1], sums.shape)


def smooth_second(
    nrow, ncol, reaction, gathered, kin, kin_above, kin_below,
    start, qscaled, qinverse, first, scaled, code, above, below, even, odd,
    out,
    wide, spread, e, q0, q1, q2, q3, qs, fs, inv, f0, p0, p1, p2,
):
    row, col = place()
    lane = lanes()
    width = ncol * GROUPS
    fields = [jnp.zeros((nrow, CZ), jnp.float32) for _ in range(FIELDS)]
    for c in range(ncol):
        some = gathered[pl.ds(c, nrow, stride=ncol), :]
        for f in range(FIELDS):
            moved = pltpu.roll(some, (c * GROUPS - f * GROUPS) % CZ, 1)
            here = (lane >= c * GROUPS) & (lane < (c + 1) * GROUPS)
            fields[f] = jnp.where(here, moved, fields[f])
    for f in range(FIELDS):
        wide[f] = fields[f]

    group = lax.broadcasted_iota(jnp.int32, (GROUPS, CZ), 0)
    spot = lax.broadcasted_iota(jnp.int32, (GROUPS, CZ), 1)
    mask = [(spot // 16 == group) & (spot % 2 == odd) for odd in range(2)]
    e[...] = jnp.zeros_like(e)

    def product(rows_of, f):
        total = jnp.zeros((GROUPS, width), jnp.float32)
        for k in range(nrow):
            total = total + rows_of(f, k) * wide[f, k : k + 1, 0:width]
        return jnp.sum(total, axis=1, keepdims=True)

    def neighbour(rows_of, dx, dy, inside):
        for plane in range(2):
            even = product(rows_of, 2 * plane)
            odd = product(rows_of, 2 * plane + 1)
            full = jnp.where(mask[0], even, jnp.where(mask[1], odd, 0.0))
            line = jnp.sum(full, axis=0, keepdims=True)
            if inside is not None:
                line = jnp.where(inside, line, 0.0)
            x_from, x_to = {-1: (0, 6), 0: (6, 6 + HX), 1: (6 + HX, EX)}[dx]
            y_from, y_to = {-1: (8, QO), 0: (QO, QO + HY), 1: (QO + HY, QO + HY + 8)}[dy]
            for x in range(x_from, x_to):
                e[plane, x, y_from:y_to, :] = jnp.broadcast_to(line, (y_to - y_from, CZ))

    def slab(ref, part):
        def rows_of(f, k):
            at = (f * GROUPS + k) * GROUPS
            return ref[part, at : at + GROUPS, :]

        return rows_of

    in_x = {-1: row > 0, 0: True, 1: row < nrow - 1}
    in_y = {-1: col > 0, 0: True, 1: col < ncol - 1}
    for dx, ref in ((0, kin), (-1, kin_above), (1, kin_below)):
        for part, dy in enumerate((0, -1, 1)):
            inside = in_x[dx] & in_y[dy] if (dx, dy) != (0, 0) else None
            neighbour(slab(ref, part), dx, dy, inside)

    parts = (q0, q1, q2, q3)

    def begin(x):
        for plane in range(2):
            here, total = beside(e, plane, x, 8, 32, 2)
            value = qscaled[plane, x - 1] - here + qinverse[plane, x - 1] * total
            qs[plane, x] = value
            q0[plane, x, 8:40, :] = value * (1.0 / THETA)

    every(1, EX - 1, begin)
    for k, (keep, gain) in enumerate(coefficients()):
        def sweep(x):
            for plane in range(2):
                here, total = beside(parts[k], plane, x, 8, 32, 2)
                value = qs[plane, x] - here + qinverse[plane, x - 1] * total
                qs[plane, x] = value
                parts[k + 1][plane, x, 8:40, :] = keep * here + gain * value

        every(k + 2, EX - k - 2, sweep)

    parity = lane % 2 == 0

    def lift(i):
        for plane in range(2):
            total = start[plane, i] + e[plane, i + 4, 8:40, :]
            total = total + q0[plane, i + 4, 8:40, :] + q1[plane, i + 4, 8:40, :]
            total = total + q2[plane, i + 4, 8:40, :] + q3[plane, i + 4, 8:40, :]
            for odd in range(2):
                if odd:
                    value = jnp.where(parity, pltpu.roll(total, CZ - 1, 1), total)
                else:
                    value = jnp.where(parity, total, pltpu.roll(total, 1, 1))
                spread[...] = value
                high, low = spread[8:26, :], spread[6:8, :]
                for h in range(2):
                    to = f0.at[2 * plane + odd, i * 2 + h]
                    for y in range(2):
                        to[pl.ds(FO + y, 18, stride=2), :] = high
                        to[pl.ds(FO + FN - 4 + y, 2, stride=2), :] = low
                    to[FO - 1 : FO, :] = low[1:2]
                    to[FO + FN : FO + FN + 1, :] = high[0:1]

    every(0, HX + 4, lift)

    zeros = jnp.zeros((FN, CZ), jnp.float32)
    for f in range(FIELDS):
        for x in (1, FX - 2):
            fs[f, x, ALL, :] = zeros
        for x in range(2, FX - 2):
            fs[f, x, OWN, :] = scaled[f, (x - 2) * CY : (x - 1) * CY, :]
            fs[f, x, FO + CY : FO + FN, :] = zeros[:8]
    sflat = fs.reshape(FIELDS, FX * FY, CZ)

    def face(x, ref):
        for f in range(FIELDS):
            at = COARSE_LINES + f * CY
            fs[f, x, OWN, :] = ref[at : at + CY, :]

    pl.when(in_x[-1])(functools.partial(face, 1, above))
    pl.when(in_x[1])(functools.partial(face, FX - 2, below))

    def strips(ref, is_high):
        for f in range(FIELDS):
            for j, offset in STRIP_AT.items():
                size = WX + 2 - 2 * j
                at = STRIP_LINES + f * (3 * WX - 6) + offset
                start = (1 + j) * FY + halo_row(j, is_high)
                sflat[f, pl.ds(start, size, stride=FY), :] = ref[at : at + size, :]

    def sides(low, high):
        pl.when(in_y[-1])(functools.partial(strips, low, 0))
        pl.when(in_y[1])(functools.partial(strips, high, 1))

    by_parity(sides, even, odd)

    parts = (p0, p1, p2)

    def open_fine(x):
        kind = code[x + 2, ALL, :]
        for f in range(FIELDS):
            here, total = beside(f0, f, x, FO, FN, 1)
            inverse = inverse_of(kind, reaction, f)
            inv[f, x, ALL, :] = inverse
            value = fs[f, x, ALL, :] - here + inverse * total
            fs[f, x, ALL, :] = value
            go_round(p0, f, x, value * (1.0 / THETA))

    every(1, FX - 1, open_fine)
    for k in range(2):
        every(k + 2, FX - k - 2, lambda x: fine_sweep(x, k, fs, inv, parts))

    keep, gain = coefficients()[2]

    def close(i):
        x = i + 4
        at = pl.ds(i * CY, CY)
        for f in range(FIELDS):
            here, total = beside(p2, f, x, FO, CY, 1)
            value = fs[f, x, OWN, :] - here + inv[f, x, OWN, :] * total
            result = first[f, at, :] + f0[f, x, OWN, :] + p0[f, x, OWN, :]
            result = result + p1[f, x, OWN, :] + here
            out[f, at, :] = result + (keep * here + gain * value)

    every(0, CX, close)


def call(kernel, out_shapes, scratch, *args, limit=16, in_hbm=False, microseconds=0.1):
    vmem = pl.BlockSpec(memory_space=pltpu.VMEM)
    given = pl.BlockSpec(memory_space=pltpu.HBM) if in_hbm else vmem
    return pl.pallas_call(
        kernel,
        out_shape=[jax.ShapeDtypeStruct(shape, jnp.float32) for shape in out_shapes],
        in_specs=[given] * len(args),
        out_specs=[given] * len(out_shapes),
        scratch_shapes=[
            pltpu.VMEM(shape, jnp.float32) if isinstance(shape, tuple) else shape
            for shape in scratch
        ],
        cost_estimate=pl.CostEstimate(
            flops=int(microseconds * 1e6), bytes_accessed=int(microseconds * 3.5e6), transcendentals=0
        ),
        compiler_params=pltpu.CompilerParams(vmem_limit_bytes=int(limit * 1024 * 1024)),
    )(*args)


def ahead(value):
    count = lax.axis_size("row")
    return lax.ppermute(value, "row", [(i, (i + 1) % count) for i in range(count)])


def back(value):
    count = lax.axis_size("row")
    return lax.ppermute(value, "row", [((i + 1) % count, i) for i in range(count)])


def pairs(value, odd):
    nrow, ncol = lax.axis_size("row"), lax.axis_size("col")
    moves = []
    for r in range(nrow):
        for c in range(ncol):
            if not odd:
                to = (r, c ^ 1)
            elif c in (0, ncol - 1):
                to = (r ^ 1, c)
            else:
                to = (r, c + 1 if c % 2 else c - 1)
            moves.append((r * ncol + c, to[0] * ncol + to[1]))
    return lax.ppermute(value, ("row", "col"), moves)


def body(right_side, material, reaction, coarse_inverse):
    nrow, ncol = lax.axis_size("row"), lax.axis_size("col")
    b = right_side.reshape(FIELDS, CX * CY, CZ)
    material = material.reshape(CX * CY, CZ)

    fine = (FIELDS, CX * CY, CZ)
    up, down, even, odd, own = call(
        pack_layers,
        [(LAYER_LINES, CZ)] * 2 + [(BAND_LINES, CZ)] * 2 + [(KIN_LINES, CZ)],
        [fine, pltpu.VMEM(fine[1:], jnp.int32), coarse_inverse.shape,
         (2, 6 * CY, CZ), (BAND_LINES, CZ), (BAND_LINES, CZ), (KIN_LINES, CZ),
         pltpu.SemaphoreType.DMA((FIELDS + 2,)), pltpu.SemaphoreType.DMA((4 * FIELDS + 5,))],
        b, material, coarse_inverse,
        in_hbm=True, limit=59.27,
    )
    odd, even = pairs(odd, True), pairs(even, False)
    above, below = ahead(up), back(down)
    even, odd, above, below = lax.optimization_barrier((even, odd, above, below))
    up, down, reaction = call(
        pack_corners, [(FINE_CORNER_LINES, CZ)] * 2 + [(2 * FIELDS, CZ)], [],
        even, odd, reaction.T,
    )
    kabove, kbelow = ahead(up), back(down)
    kin_odd, kin_even = pairs(own, True), pairs(own, False)

    wide = (FIELDS, WX * CY, CZ)
    middle = MID[1] - MID[0]
    padded = (FIELDS, CX, FY, CZ)
    mids = call(
        functools.partial(smooth_middle, nrow, ncol),
        [(FIELDS, middle * CY, CZ)] * 2 + [(3, middle // 2 * HY, CZ),
         (2, 3, 2, FIELDS, FY, CZ), (2, 3, FIELDS, FN, CZ), (2, 3, FIELDS, CY, CZ)],
        [padded] * 6 + [padded[1:], (2, FIELDS + 1, CY, CZ)],
        reaction, b, material, even, odd,
        limit=16, microseconds=100,
    )
    padded = (FIELDS, GX, FY, CZ)
    first, scaled, code, coarse, up, down, side_even, side_odd, kin = call(
        functools.partial(smooth_outer, nrow, ncol),
        [fine, wide, padded[1:], (3, VX * HY, CZ)]
        + [(FACE_LINES, CZ)] * 2 + [(SIDE_LINES, CZ)] * 2 + [(3, KIN_LINES, CZ)],
        [padded] * 6 + [(2, FIELDS + 1, CY, CZ)],
        reaction, b, material, above, below, even, odd, kabove, kbelow, own, kin_even, kin_odd, *mids,
        limit=26,
    )
    odd, even = pairs(side_odd, True), pairs(side_even, False)
    above, below = ahead(up), back(down)
    kin_above, kin_below = ahead(kin), back(kin)
    up, down = call(pack_knots, [(KNOT_LINES, CZ)] * 2, [], even, odd, microseconds=100)
    kabove, kbelow = ahead(up), back(down)

    qpadded = (2, QX, QY, CZ)
    start, qscaled, qinverse, sums = call(
        functools.partial(smooth_coarse, nrow, ncol),
        [(2, HX + 4, 32, CZ), (2, HX + 10, 32, CZ), (2, HX + 10, 32, CZ), (nrow * ncol, CZ)],
        [qpadded, qpadded, qpadded[1:]] + [qpadded] * 4,
        reaction, coarse, above, below, even, odd, kabove, kbelow,
        limit=14, microseconds=2.5,
    )

    sums, kin_above, kin_below = lax.optimization_barrier((sums, kin_above, kin_below))
    gathered = lax.all_to_all(sums, ("row", "col"), 0, 0)

    epadded = (2, EX, QY, CZ)
    padded = (FIELDS, FX, FY, CZ)
    (out,) = call(
        functools.partial(smooth_second, nrow, ncol),
        [fine],
        [(FIELDS, nrow, CZ), (32, CZ)] + [epadded] * 5 + [(2, EX, 32, CZ)] + [padded] * 6,
        reaction, gathered, kin, kin_above, kin_below,
        start, qscaled, qinverse, first, scaled, code, above, below, even, odd,
        limit=32, microseconds=7,
    )
    return out.reshape(right_side.shape)


def solution(mesh):
    placed = (
        P(None, "row", "col", None),
        P("row", "col", None),
        P(),
        P(None, ("row", "col"), None),
    )
    return jax.shard_map(
        body, mesh=mesh, in_specs=placed, out_specs=P(None, "row", "col", None), check_vma=False
    )
```

```python
import functools

import jax
import jax.numpy as jnp
from jax import lax
from jax.experimental import pallas as pl
from jax.experimental.pallas import tpu as pltpu
from jax.sharding import PartitionSpec as P

FIELDS = 4
CX, CY, CZ = 16, 32, 128
HX, HY = CX // 2, CY // 2
GROUPS = 8
SWEEPS = 4
LOW_BOUND = 0.25
HIGH_BOUND = 2.0
THETA = (HIGH_BOUND + LOW_BOUND) / 2.0
DELTA = (HIGH_BOUND - LOW_BOUND) / 2.0

WX = CX + 4
GX, FY, FO, FN = CX + 12, CY + 24, 8, CY + 8
OWN = slice(FO, FO + CY)
ALL = slice(FO, FO + FN)
FX = CX + 8
MID = (4, CX - 4)
VX = HX + 2
QX, QY, QO = HX + 18, HY + 32, 16
EX = HX + 12
CORNER_AT = {1: 0, 2: 9, 3: 17, 4: 24, 5: 30, 6: 35, 7: 39, 8: 42, 9: 44}
CORNER_LINES = 48
FINE_CORNER_AT = {1: 0, 2: 5, 3: 9, 4: 12}
FINE_CORNER_LINES = (FIELDS + 1) * 32

LAYER_LINES = (FIELDS + 1) * 6 * CY
BAND_LINES = (FIELDS + 1) * 4 * CX
KIN_LINES = FIELDS * GROUPS * 8
COARSE_LINES = 3 * (HX + 1) * HY
FACE_LINES = COARSE_LINES + FIELDS * CY
STRIP_LINES = 272
STRIP_AT = {1: 0, 2: WX, 3: 2 * WX - 2}
SIDE_LINES = STRIP_LINES + FIELDS * (3 * WX - 6)
KNOT_LINES = 6 * CORNER_LINES


def coefficients():
    rho = DELTA / THETA
    pairs = []
    for _ in range(SWEEPS - 1):
        following = 1.0 / (2.0 * THETA / DELTA - rho)
        pairs.append((following * rho, 2.0 * following / DELTA))
        rho = following
    return pairs


def every(low, high, step):
    for i in range(low, high):
        step(i)


def lanes():
    return lax.broadcasted_iota(jnp.int32, (1, CZ), 1)


def beside(ref, f, x, low, count, width, share=1):
    after, before, x = (x + 1) // share, (x - 1) // share, x // share
    here = ref[f, x, low : low + count, :]
    lane = lanes()
    total = ref[f, after, low : low + count, :] + ref[f, before, low : low + count, :]
    total = total + ref[f, x, low + 1 : low + 1 + count, :]
    total = total + ref[f, x, low - 1 : low - 1 + count, :]
    total = total + jnp.where(lane < CZ - width, pltpu.roll(here, CZ - width, 1), 0.0)
    total = total + jnp.where(lane >= width, pltpu.roll(here, width, 1), 0.0)
    return here, total


def diagonal_values(reaction, f):
    low = reaction[2 * f : 2 * f + 1, :]
    jump = reaction[2 * f + 1 : 2 * f + 2, :] - low
    return 6.0 + low, 6.0 + low + jump


def inverse_of(code, reaction, f):
    fluid, solid = diagonal_values(reaction, f)
    fluid, solid = 1.0 / fluid, 1.0 / solid
    return jnp.where(code == 0.0, fluid, jnp.where(code == 1.0, solid, 0.0))


def place():
    return lax.axis_index("row"), lax.axis_index("col")


def by_parity(step, first, second):
    even = lax.rem(lax.axis_index("col"), 2) == 0
    pl.when(even)(functools.partial(step, second, first))
    pl.when(jnp.logical_not(even))(functools.partial(step, first, second))


def pack_layers(
    b, material, inverse, up, down, first, second, own,
    b_here, material_here, inverse_here, solid, first_here, second_here, own_here, sems, out_sems,
):
    copies = [pltpu.make_async_copy(b.at[f], b_here.at[f], sems.at[f]) for f in range(FIELDS)]
    copies.append(pltpu.make_async_copy(material, material_here, sems.at[FIELDS]))
    copies.append(pltpu.make_async_copy(inverse, inverse_here, sems.at[FIELDS + 1]))
    for copy in copies:
        copy.start()
    sent = []

    def send(source, target):
        sent.append(pltpu.make_async_copy(source, target, out_sems.at[len(sent)]))
        sent[-1].start()

    for f in range(FIELDS + 1):
        copies[f].wait()
        layer, band = 6 * CY, 4 * CX
        if f < FIELDS:
            take = lambda start, size, step: b_here[f, pl.ds(start, size, stride=step), :]
            ends = (b_here.at[f, pl.ds((CX - 6) * CY, layer)], b_here.at[f, pl.ds(0, layer)])
        else:
            take = lambda start, size, step: material_here[
                pl.ds(start, size, stride=step), :
            ].astype(jnp.float32)
            solid[0] = take((CX - 6) * CY, layer, 1)
            solid[1] = take(0, layer, 1)
            ends = (solid.at[0], solid.at[1])
        for source, target in zip(ends, (up, down)):
            send(source, target.at[pl.ds(f * layer, layer)])

        def bands(left, right):
            for i in range(4):
                at = f * band + i * CX
                right[at : at + CX, :] = take(CY - 4 + i, CX, CY)
                left[at : at + CX, :] = take(i, CX, CY)

        by_parity(bands, first_here, second_here)
        for source, target in ((first_here, first), (second_here, second)):
            send(source.at[pl.ds(f * band, band)], target.at[pl.ds(f * band, band)])
    copies[FIELDS + 1].wait()
    for f in range(FIELDS):
        for k in range(inverse.shape[2] // CZ):
            at = (f * GROUPS + k) * GROUPS
            own_here[at : at + GROUPS, :] = inverse_here[f, :, k * CZ : (k + 1) * CZ]
    send(own_here, own)
    for copy in sent:
        copy.wait()


def pack_corners(first, second, reaction, up, down, constants):
    for f in range(FIELDS):
        for i in range(2):
            constants[2 * f + i : 2 * f + i + 1, :] = jnp.broadcast_to(
                reaction[i : i + 1, f : f + 1], (1, CZ)
            )

    def pack(low, high):
        for side, ref in enumerate((low, high)):
            for f in range(FIELDS + 1):
                for j, offset in FINE_CORNER_AT.items():
                    size = 6 - j
                    line = (f * 4 + (j - 1 if side else 4 - j)) * CX
                    at = (f * 2 + side) * 16 + offset
                    up[at : at + size, :] = ref[line + CX - size : line + CX, :]
                    down[at : at + size, :] = ref[line : line + size, :]
                at = (f * 2 + side) * 16 + 14
                up[at : at + 2, :] = jnp.zeros((2, CZ), jnp.float32)
                down[at : at + 2, :] = jnp.zeros((2, CZ), jnp.float32)

    by_parity(pack, first, second)


def halo_row(j, is_high):
    return FO + CY - 1 + j if is_high else FO + FN - j


def go_round(ref, f, x, value):
    ref[f, x, ALL, :] = value
    ref[f, x, FO - 1 : FO, :] = value[FN - 1 : FN]
    ref[f, x, FO + FN : FO + FN + 1, :] = value[0:1]


def fine_scale(x, reaction, code, s, inv, p0):
    kind = code[x, ALL, :]
    for f in range(FIELDS):
        inverse = inverse_of(kind, reaction, f)
        inv[f, x, ALL, :] = inverse
        if p0 is not None:
            value = inverse * s[f, x, ALL, :]
            s[f, x, ALL, :] = value
            go_round(p0, f, x, value * (1.0 / THETA))


def fine_sweep(x, k, s, inv, parts):
    keep, gain = coefficients()[k]
    for f in range(FIELDS):
        here, total = beside(parts[k], f, x, FO, FN, 1)
        value = s[f, x, ALL, :] - here + inv[f, x, ALL, :] * total
        s[f, x, ALL, :] = value
        go_round(parts[k + 1], f, x, keep * here + gain * value)


def fine_last(x, reaction, code, s, inv, p3, scaled, line):
    residues = []
    for f in range(FIELDS):
        fluid, solid = diagonal_values(reaction, f)
        here, total = beside(p3, f, x, FO, CY, 1)
        value = s[f, x, OWN, :] - here + inv[f, x, OWN, :] * total
        scaled[f, line : line + CY, :] = value
        residues.append(jnp.where(code[x, OWN, :] == 1.0, solid, fluid) * value)
    return residues


def restrict(x, residues, code, pair, coarse, line):
    parity = lanes() % 2 == 0
    sums = [one + other for one, other in zip(*residues)]
    sums.append(code[x, OWN, :] + code[x + 1, OWN, :])
    halves = []
    for f, value in enumerate(sums):
        here = pair.at[x // 2 % 2, f]
        here[...] = value
        halves.append(here[pl.ds(0, HY, stride=2), :] + here[pl.ds(1, HY, stride=2), :])
    halves.append(halves[4])
    for plane in range(3):
        even, odd = halves[2 * plane], halves[2 * plane + 1]
        merged = jnp.where(
            parity, even + pltpu.roll(even, CZ - 1, 1), odd + pltpu.roll(odd, 1, 1)
        )
        merged = merged * 0.5 if plane < 2 else jnp.where(merged > 8.5, -1.0, merged)
        coarse[plane, line : line + HY, :] = merged


def lay_own(x_at, xs, b, material, s, code):
    zeros = jnp.zeros((8, CZ), jnp.float32)
    for x in xs:
        for f in range(FIELDS):
            s[f, x + x_at, OWN, :] = b[f, x * CY : x * CY + CY, :]
            s[f, x + x_at, FO + CY : FO + FN, :] = zeros
        code[x + x_at, OWN, :] = material[x * CY : x * CY + CY, :].astype(jnp.float32)
        code[x + x_at, FO + CY : FO + FN, :] = zeros + 2.0


def putter(s, code):
    sflat = s.reshape(FIELDS, s.shape[1] * FY, CZ)
    cflat = code.reshape(s.shape[1] * FY, CZ)

    def put(f, x, y_row, size, value):
        to = pl.ds(x * FY + y_row, size, stride=FY)
        if f < FIELDS:
            sflat[f, to, :] = value
        else:
            cflat[to, :] = value

    return put


def lay_bands(x_at, spans, ncol, put, even, odd):
    _, col = place()

    def bands(ref, is_high):
        for f in range(FIELDS + 1):
            for i in range(4):
                at = (f * 4 + i) * CX
                row = halo_row(i + 1 if is_high else 4 - i, is_high)
                for x, size in spans:
                    put(f, x + x_at, row, size, ref[at + x : at + x + size, :])

    def sides(low, high):
        pl.when(col > 0)(functools.partial(bands, low, 0))
        pl.when(col < ncol - 1)(functools.partial(bands, high, 1))

    by_parity(sides, even, odd)


def kept_lines():
    for side in range(2):
        for k in range(1, SWEEPS):
            flip = lambda x: CX - 1 - x if side else x
            yield side, k, (flip(k), flip(k + 1)), flip(k)


def smooth_middle(
    nrow, ncol, reaction, b, material, even, odd,
    first, scaled, coarse, keep_p, keep_s, keep_sum,
    s, inv, p0, p1, p2, p3, code, pair,
):
    parts = (p0, p1, p2, p3)
    lay_own(0, range(CX), b, material, s, code)
    lay_bands(0, ((0, CX),), ncol, putter(s, code), even, odd)
    every(0, CX, lambda x: fine_scale(x, reaction, code, s, inv, p0))
    for k in range(SWEEPS - 1):
        every(k + 1, CX - k - 1, lambda x: fine_sweep(x, k, s, inv, parts))
        for side, step, lines, line in kept_lines():
            if step == k + 1:
                for f in range(FIELDS):
                    for i, x in enumerate(lines):
                        keep_p[side, k, i, f] = parts[step][f, x]
                    keep_s[side, k, f] = s[f, line, ALL, :]
    for x in range(*MID, 2):
        residues = []
        for h in range(2):
            line = (x + h - MID[0]) * CY
            residues.append(fine_last(x + h, reaction, code, s, inv, p3, scaled, line))
            for f in range(FIELDS):
                first[f, line : line + CY, :] = sum(p[f, x + h, OWN, :] for p in parts)
        restrict(x, residues, code, pair, coarse, (x - MID[0]) // 2 * HY)
    for side in range(2):
        for i in range(1, SWEEPS):
            x = CX - 1 - i if side else i
            for f in range(FIELDS):
                keep_sum[side, i - 1, f] = sum(p[f, x, OWN, :] for p in parts[: i + 1])


def smooth_outer(
    nrow, ncol, reaction, b, material, above, below, even, odd, kabove, kbelow,
    own, kin_even, kin_odd, mid_first, mid_scaled, mid_coarse, keep_p, keep_s, keep_sum,
    first, scaled, code, coarse, up, down, side_even, side_odd, kin,
    s, inv, p0, p1, p2, p3, pair,
):
    row, col = place()
    parts = (p0, p1, p2, p3)
    at_x = 6
    zeros = jnp.zeros((FN, CZ), jnp.float32)
    for x in (*range(6), *range(GX - 6, GX)):
        for f in range(FIELDS):
            s[f, x, ALL, :] = zeros
        code[x, ALL, :] = zeros + 2.0
    outer = (*range(4), *range(CX - 4, CX))
    lay_own(at_x, outer, b, material, s, code)
    for x in range(4, CX - 4):
        code[x + at_x, OWN, :] = material[x * CY : x * CY + CY, :].astype(jnp.float32)
        code[x + at_x, FO + CY : FO + FN, :] = zeros[:8] + 2.0
    put = putter(s, code)

    def rows(first_x, ref):
        for i in range(6):
            for f in range(FIELDS):
                at = (f * 6 + i) * CY
                s[f, first_x + i, OWN, :] = ref[at : at + CY, :]
            at = (FIELDS * 6 + i) * CY
            code[first_x + i, OWN, :] = ref[at : at + CY, :]

    pl.when(row > 0)(functools.partial(rows, 0, above))
    pl.when(row < nrow - 1)(functools.partial(rows, GX - 6, below))
    lay_bands(at_x, ((0, CX),), ncol, put, even, odd)

    def corners(ref, is_above, is_high):
        for f in range(FIELDS + 1):
            for j, offset in FINE_CORNER_AT.items():
                size = 6 - j
                at = (f * 2 + is_high) * 16 + offset
                x = 6 - size if is_above else 6 + CX
                put(f, x, halo_row(j, is_high), size, ref[at : at + size, :])

    for ref, is_above, in_x in ((kabove, 1, row > 0), (kbelow, 0, row < nrow - 1)):
        for is_high, in_y in ((0, col > 0), (1, col < ncol - 1)):
            pl.when(in_x & in_y)(functools.partial(corners, ref, is_above, is_high))

    def both(low, high, step):
        for x in range(low, high):
            step(x + at_x)
            step(CX - 1 - x + at_x)

    both(-6, 2, lambda x: fine_scale(x, reaction, code, s, inv, p0))
    both(2, 4, lambda x: fine_scale(x, reaction, code, s, inv, None))
    for side, k, lines, line in kept_lines():
        for f in range(FIELDS):
            for i, x in enumerate(lines):
                parts[k][f, x + at_x] = keep_p[side, k - 1, i, f]
    for k in range(SWEEPS - 1):
        if k > 0:
            for side, step, lines, line in kept_lines():
                if step == k:
                    for f in range(FIELDS):
                        s[f, line + at_x, ALL, :] = keep_s[side, k - 1, f]
        both(k - 5, k + 1, lambda x: fine_sweep(x, k, s, inv, parts))
    for side, step, lines, line in kept_lines():
        if step == SWEEPS - 1:
            for f in range(FIELDS):
                s[f, line + at_x, ALL, :] = keep_s[side, step - 1, f]
    for x in (*range(-2, 4, 2), *range(CX - 4, CX + 2, 2)):
        residues = []
        for h in range(2):
            line = (x + h + 2) * CY
            residues.append(
                fine_last(x + h + at_x, reaction, code, s, inv, p3, scaled, line)
            )
        restrict(x + at_x, residues, code, pair, coarse, (x // 2 + 1) * HY)
    for f in range(FIELDS):
        for x in range(CX):
            out = slice(x * CY, x * CY + CY)
            side = x >= CX // 2
            i = CX - 1 - x if side else x
            if i < 4:
                some = [p[f, x + at_x, OWN, :] for p in (parts if i == 0 else parts[i + 1 :])]
                if i > 0:
                    some.append(keep_sum[int(side), i - 1, f])
                first[f, out, :] = sum(some)
            else:
                mid = slice((x - MID[0]) * CY, (x - MID[0] + 1) * CY)
                first[f, out, :] = mid_first[f, mid, :]
                scaled[f, (x + 2) * CY : (x + 3) * CY, :] = mid_scaled[f, mid, :]
    for plane in range(3):
        size = (MID[1] - MID[0]) // 2 * HY
        at = (MID[0] // 2 + 1) * HY
        coarse[plane, at : at + size, :] = mid_coarse[plane]

    for f in range(FIELDS):
        at = COARSE_LINES + f * CY
        up[at : at + CY, :] = scaled[f, (CX - 1) * CY : CX * CY, :]
        down[at : at + CY, :] = scaled[f, 4 * CY : 5 * CY, :]
    for plane in range(3):
        at, size = plane * (HX + 1) * HY, (HX + 1) * HY
        up[at : at + size, :] = coarse[plane, 0:size, :]
        down[at : at + size, :] = coarse[plane, HY : HY + size, :]

    kin[0] = own[...]

    def gather(low, high):
        kin[1] = low[...]
        kin[2] = high[...]

    by_parity(gather, kin_even, kin_odd)

    def strips(left, right):
        for plane in range(3):
            for i in range(9):
                at = (plane * 9 + i) * VX
                right[at : at + VX, :] = coarse[plane, pl.ds(HY - 9 + i, VX, stride=HY), :]
                left[at : at + VX, :] = coarse[plane, pl.ds(i, VX, stride=HY), :]
        for f in range(FIELDS):
            for j, offset in STRIP_AT.items():
                size = WX + 2 - 2 * j
                at = STRIP_LINES + f * (3 * WX - 6) + offset
                x = (j - 1) * CY
                right[at : at + size, :] = scaled[f, pl.ds(x + CY - j, size, stride=CY), :]
                left[at : at + size, :] = scaled[f, pl.ds(x + j - 1, size, stride=CY), :]

    by_parity(strips, side_even, side_odd)


def pack_knots(first, second, up, down):
    def pack(low, high):
        for plane in range(3):
            for side, ref in enumerate((low, high)):
                base = (plane * 2 + side) * CORNER_LINES
                up[base + 40 : base + 48, :] = jnp.zeros((8, CZ), jnp.float32)
                down[base + 40 : base + 48, :] = jnp.zeros((8, CZ), jnp.float32)
                for j, offset in CORNER_AT.items():
                    size = 10 - j
                    line = (plane * 9 + (j - 1 if side else 9 - j)) * VX
                    at = base + offset
                    up[at : at + size, :] = ref[line + VX - 1 - size : line + VX - 1, :]
                    down[at : at + size, :] = ref[line + 1 : line + 1 + size, :]

    by_parity(pack, first, second)


def coarse_constants(reaction, plane):
    parity = lanes() % 2 == 0
    even, odd = (
        [reaction[2 * f + i : 2 * f + i + 1, :] for i in range(2)]
        for f in (2 * plane, 2 * plane + 1)
    )
    low = jnp.where(parity, even[0], odd[0])
    return 8.0 * low, jnp.where(parity, even[1] - even[0], odd[1] - odd[0])


def smooth_coarse(
    nrow, ncol, reaction, coarse, above, below, even, odd, kabove, kbelow,
    start, scaled, inverse_out, sums,
    s, inv, count, p0, p1, p2, p3,
):
    row, col = place()
    parts = (p0, p1, p2, p3)
    zeros = jnp.zeros((QY, CZ), jnp.float32)

    def clear(x):
        for plane in range(2):
            s[plane, x] = zeros
        count[x] = zeros - 1.0

    every(0, QX, clear)
    sflat = s.reshape(2, QX * QY, CZ)
    cflat = count.reshape(QX * QY, CZ)

    def put(plane, start_row, size, value):
        if plane < 2:
            sflat[plane, pl.ds(start_row, size, stride=QY), :] = value
        else:
            cflat[pl.ds(start_row, size, stride=QY), :] = value

    def block(plane, x, value):
        if plane < 2:
            s[plane, x, QO : QO + HY, :] = value
        else:
            count[x, QO : QO + HY, :] = value

    def rows(first_x, ref):
        for plane in range(3):
            for i in range(HX + 1):
                at = (plane * (HX + 1) + i) * HY
                block(plane, first_x + i, ref[at : at + HY, :])

    for plane in range(3):
        for i in range(HX):
            block(plane, 9 + i, coarse[plane, (i + 1) * HY : (i + 2) * HY, :])
    pl.when(row > 0)(functools.partial(rows, 0, above))
    pl.when(row < nrow - 1)(functools.partial(rows, 9 + HX, below))

    def strips(ref, first_y):
        for plane in range(3):
            for i in range(9):
                line = (plane * 9 + i) * VX
                put(plane, 9 * QY + first_y + i, HX, ref[line + 1 : line + 1 + HX, :])

    def sides(low, high):
        pl.when(col > 0)(functools.partial(strips, low, QO - 9))
        pl.when(col < ncol - 1)(functools.partial(strips, high, QO + HY))

    by_parity(sides, even, odd)

    def corners(ref, is_above, is_high):
        for plane in range(3):
            base = (plane * 2 + is_high) * CORNER_LINES
            for j, at in CORNER_AT.items():
                size = 10 - j
                x = 9 - size if is_above else 9 + HX
                y = QO + HY - 1 + j if is_high else QO - j
                put(plane, x * QY + y, size, ref[base + at : base + at + size, :])

    for ref, is_above, in_x in ((kabove, 1, row > 0), (kbelow, 0, row < nrow - 1)):
        for is_high, in_y in ((0, col > 0), (1, col < ncol - 1)):
            pl.when(in_x & in_y)(functools.partial(corners, ref, is_above, is_high))

    def scale(x):
        number = count[x]
        for plane in range(2):
            low8, jump = coarse_constants(reaction, plane)
            inverse = jnp.where(number < 0.0, 0.0, 1.0 / (6.0 + 0.5 * (low8 + jump * number)))
            value = inverse * s[plane, x]
            inv[plane, x] = inverse
            s[plane, x] = value
            p0[plane, x] = value * (1.0 / THETA)

    every(0, QX, scale)

    for k, (keep, gain) in enumerate(coefficients()):
        def sweep(x):
            for plane in range(2):
                here, total = beside(parts[k], plane, x, 8, 32, 2)
                value = s[plane, x, 8:40, :] - here + inv[plane, x, 8:40, :] * total
                s[plane, x, 8:40, :] = value
                parts[k + 1][plane, x, 8:40, :] = keep * here + gain * value

        every(k + 1, QX - k - 1, sweep)

    def finish(x):
        for plane in range(2):
            here, total = beside(p3, plane, x, 8, 32, 2)
            value = s[plane, x, 8:40, :] - here + inv[plane, x, 8:40, :] * total
            scaled[plane, x - 4] = value
            inverse_out[plane, x - 4] = inv[plane, x, 8:40, :]

    every(4, QX - 4, finish)

    def add(x):
        for plane in range(2):
            start[plane, x - 7] = (
                p0[plane, x, 8:40, :] + p1[plane, x, 8:40, :]
                + p2[plane, x, 8:40, :] + p3[plane, x, 8:40, :]
            )

    every(7, QX - 7, add)

    lane = lanes()
    message = jnp.zeros((8, CZ), jnp.float32)
    for plane in range(2):
        low8, jump = coarse_constants(reaction, plane)
        total = jnp.zeros((HY, CZ), jnp.float32)
        for x in range(9, 9 + HX):
            diagonal = 6.0 + 0.5 * (low8 + jump * count[x, QO : QO + HY, :])
            total = total + diagonal * scaled[plane, x - 4, 8 : 8 + HY, :]
        total = total[:8] + total[8:]
        for shift in (4, 2, 1):
            total = total + pltpu.roll(total, shift, 0)
        for shift in (2, 4, 8):
            total = total + pltpu.roll(total, CZ - shift, 1)
        for odd in range(2):
            for g in range(GROUPS):
                to = (2 * plane + odd) * GROUPS + g
                moved = pltpu.roll(total, (to - 16 * g - odd) % CZ, 1)
                message = jnp.where(lane == to, moved, message)
    sums[...] = jnp.broadcast_to(message[:1], sums.shape)


def smooth_second(
    nrow, ncol, reaction, gathered, kin, kin_above, kin_below,
    start, qscaled, qinverse, first, scaled, code, above, below, even, odd,
    out,
    wide, spread, e, q0, q1, q2, q3, qs, fs, inv, f0, p0, p1, p2, out_here, sems,
):
    row, col = place()
    lane = lanes()
    width = ncol * GROUPS
    fields = [jnp.zeros((nrow, CZ), jnp.float32) for _ in range(FIELDS)]
    for c in range(ncol):
        some = gathered[pl.ds(c, nrow, stride=ncol), :]
        for f in range(FIELDS):
            moved = pltpu.roll(some, (c * GROUPS - f * GROUPS) % CZ, 1)
            here = (lane >= c * GROUPS) & (lane < (c + 1) * GROUPS)
            fields[f] = jnp.where(here, moved, fields[f])
    for f in range(FIELDS):
        wide[f] = fields[f]

    group = lax.broadcasted_iota(jnp.int32, (GROUPS, CZ), 0)
    spot = lax.broadcasted_iota(jnp.int32, (GROUPS, CZ), 1)
    mask = [(spot // 16 == group) & (spot % 2 == odd) for odd in range(2)]
    e[...] = jnp.zeros_like(e)

    def product(rows_of, f):
        total = jnp.zeros((GROUPS, width), jnp.float32)
        for k in range(nrow):
            total = total + rows_of(f, k) * wide[f, k : k + 1, 0:width]
        return jnp.sum(total, axis=1, keepdims=True)

    def neighbour(rows_of, dx, dy, inside):
        for plane in range(2):
            even = product(rows_of, 2 * plane)
            odd = product(rows_of, 2 * plane + 1)
            full = jnp.where(mask[0], even, jnp.where(mask[1], odd, 0.0))
            line = jnp.sum(full, axis=0, keepdims=True)
            if inside is not None:
                line = jnp.where(inside, line, 0.0)
            x_from, x_to = {-1: (0, 6), 0: (6, 6 + HX), 1: (6 + HX, EX)}[dx]
            y_from, y_to = {-1: (8, QO), 0: (QO, QO + HY), 1: (QO + HY, QO + HY + 8)}[dy]
            for x in range(x_from, x_to):
                e[plane, x, y_from:y_to, :] = jnp.broadcast_to(line, (y_to - y_from, CZ))

    def slab(ref, part):
        def rows_of(f, k):
            at = (f * GROUPS + k) * GROUPS
            return ref[part, at : at + GROUPS, :]

        return rows_of

    in_x = {-1: row > 0, 0: True, 1: row < nrow - 1}
    in_y = {-1: col > 0, 0: True, 1: col < ncol - 1}
    for dx, ref in ((0, kin), (-1, kin_above), (1, kin_below)):
        for part, dy in enumerate((0, -1, 1)):
            inside = in_x[dx] & in_y[dy] if (dx, dy) != (0, 0) else None
            neighbour(slab(ref, part), dx, dy, inside)

    parts = (q0, q1, q2, q3)

    def begin(x):
        for plane in range(2):
            here, total = beside(e, plane, x, 8, 32, 2)
            value = qscaled[plane, x - 1] - here + qinverse[plane, x - 1] * total
            qs[plane, x] = value
            q0[plane, x, 8:40, :] = value * (1.0 / THETA)

    every(1, EX - 1, begin)
    for k, (keep, gain) in enumerate(coefficients()):
        def sweep(x):
            for plane in range(2):
                here, total = beside(parts[k], plane, x, 8, 32, 2)
                value = qs[plane, x] - here + qinverse[plane, x - 1] * total
                qs[plane, x] = value
                parts[k + 1][plane, x, 8:40, :] = keep * here + gain * value

        every(k + 2, EX - k - 2, sweep)

    parity = lane % 2 == 0

    def lift(i):
        for plane in range(2):
            total = start[plane, i] + e[plane, i + 4, 8:40, :]
            total = total + q0[plane, i + 4, 8:40, :] + q1[plane, i + 4, 8:40, :]
            total = total + q2[plane, i + 4, 8:40, :] + q3[plane, i + 4, 8:40, :]
            for odd in range(2):
                if odd:
                    value = jnp.where(parity, pltpu.roll(total, CZ - 1, 1), total)
                else:
                    value = jnp.where(parity, total, pltpu.roll(total, 1, 1))
                some = spread.at[i % 2, 2 * plane + odd]
                some[...] = value
                high, low = some[8:26, :], some[6:8, :]
                to = f0.at[2 * plane + odd, i]
                for y in range(2):
                    to[pl.ds(FO + y, 18, stride=2), :] = high
                    to[pl.ds(FO + FN - 4 + y, 2, stride=2), :] = low
                to[FO - 1 : FO, :] = low[1:2]
                to[FO + FN : FO + FN + 1, :] = high[0:1]

    every(0, HX + 4, lift)

    zeros = jnp.zeros((FN, CZ), jnp.float32)
    for f in range(FIELDS):
        for x in (1, FX - 2):
            fs[f, x, ALL, :] = zeros
        for x in range(2, FX - 2):
            fs[f, x, OWN, :] = scaled[f, (x - 2) * CY : (x - 1) * CY, :]
            fs[f, x, FO + CY : FO + FN, :] = zeros[:8]
    sflat = fs.reshape(FIELDS, FX * FY, CZ)

    def face(x, ref):
        for f in range(FIELDS):
            at = COARSE_LINES + f * CY
            fs[f, x, OWN, :] = ref[at : at + CY, :]

    pl.when(in_x[-1])(functools.partial(face, 1, above))
    pl.when(in_x[1])(functools.partial(face, FX - 2, below))

    def strips(ref, is_high):
        for f in range(FIELDS):
            for j, offset in STRIP_AT.items():
                size = WX + 2 - 2 * j
                at = STRIP_LINES + f * (3 * WX - 6) + offset
                start = (1 + j) * FY + halo_row(j, is_high)
                sflat[f, pl.ds(start, size, stride=FY), :] = ref[at : at + size, :]

    def sides(low, high):
        pl.when(in_y[-1])(functools.partial(strips, low, 0))
        pl.when(in_y[1])(functools.partial(strips, high, 1))

    by_parity(sides, even, odd)

    parts = (p0, p1, p2)

    def open_fine(x):
        kind = code[x + 2, ALL, :]
        for f in range(FIELDS):
            here, total = beside(f0, f, x, FO, FN, 1, 2)
            inverse = inverse_of(kind, reaction, f)
            inv[f, x, ALL, :] = inverse
            value = fs[f, x, ALL, :] - here + inverse * total
            fs[f, x, ALL, :] = value
            go_round(p0, f, x, value * (1.0 / THETA))

    every(1, FX - 1, open_fine)
    for k in range(2):
        every(k + 2, FX - k - 2, lambda x: fine_sweep(x, k, fs, inv, parts))

    keep, gain = coefficients()[2]

    sent = []
    part = CX // 2
    for f in range(FIELDS):
        for i in range(CX):
            x = i + 4
            at = slice(i * CY, i * CY + CY)
            here, total = beside(p2, f, x, FO, CY, 1)
            value = fs[f, x, OWN, :] - here + inv[f, x, OWN, :] * total
            result = first[f, at, :] + f0[f, x // 2, OWN, :] + p0[f, x, OWN, :]
            result = result + p1[f, x, OWN, :] + here
            out_here[f, at, :] = result + (keep * here + gain * value)
            if i % part == part - 1:
                lines = pl.ds((i + 1 - part) * CY, part * CY)
                copy = pltpu.make_async_copy(
                    out_here.at[f, lines], out.at[f, lines], sems.at[len(sent)]
                )
                copy.start()
                sent.append(copy)
    for copy in sent:
        copy.wait()


def call(kernel, out_shapes, scratch, *args, limit=16, in_hbm=False, out_hbm=False, microseconds=0.1):
    vmem = pl.BlockSpec(memory_space=pltpu.VMEM)
    hbm = pl.BlockSpec(memory_space=pltpu.HBM)
    given, taken = hbm if in_hbm else vmem, hbm if out_hbm else vmem
    return pl.pallas_call(
        kernel,
        out_shape=[jax.ShapeDtypeStruct(shape, jnp.float32) for shape in out_shapes],
        in_specs=[given] * len(args),
        out_specs=[taken] * len(out_shapes),
        scratch_shapes=[
            pltpu.VMEM(shape, jnp.float32) if isinstance(shape, tuple) else shape
            for shape in scratch
        ],
        cost_estimate=pl.CostEstimate(
            flops=int(microseconds * 1e6), bytes_accessed=int(microseconds * 3.5e6), transcendentals=0
        ),
        compiler_params=pltpu.CompilerParams(vmem_limit_bytes=int(limit * 1024 * 1024)),
    )(*args)


def ahead(value):
    count = lax.axis_size("row")
    return lax.ppermute(value, "row", [(i, (i + 1) % count) for i in range(count)])


def back(value):
    count = lax.axis_size("row")
    return lax.ppermute(value, "row", [((i + 1) % count, i) for i in range(count)])


def pairs(value, odd):
    nrow, ncol = lax.axis_size("row"), lax.axis_size("col")
    moves = []
    for r in range(nrow):
        for c in range(ncol):
            if not odd:
                to = (r, c ^ 1)
            elif c in (0, ncol - 1):
                to = (r ^ 1, c)
            else:
                to = (r, c + 1 if c % 2 else c - 1)
            moves.append((r * ncol + c, to[0] * ncol + to[1]))
    return lax.ppermute(value, ("row", "col"), moves)


def body(right_side, material, reaction, coarse_inverse):
    nrow, ncol = lax.axis_size("row"), lax.axis_size("col")
    b = right_side.reshape(FIELDS, CX * CY, CZ)
    material = material.reshape(CX * CY, CZ)

    fine = (FIELDS, CX * CY, CZ)
    up, down, even, odd, own = call(
        pack_layers,
        [(LAYER_LINES, CZ)] * 2 + [(BAND_LINES, CZ)] * 2 + [(KIN_LINES, CZ)],
        [fine, pltpu.VMEM(fine[1:], jnp.int32), coarse_inverse.shape,
         (2, 6 * CY, CZ), (BAND_LINES, CZ), (BAND_LINES, CZ), (KIN_LINES, CZ),
         pltpu.SemaphoreType.DMA((FIELDS + 2,)), pltpu.SemaphoreType.DMA((4 * FIELDS + 5,))],
        b, material, coarse_inverse,
        in_hbm=True, out_hbm=True, limit=59.27,
    )
    odd, even = pairs(odd, True), pairs(even, False)
    above, below = ahead(up), back(down)
    even, odd, above, below = lax.optimization_barrier((even, odd, above, below))
    up, down, reaction = call(
        pack_corners, [(FINE_CORNER_LINES, CZ)] * 2 + [(2 * FIELDS, CZ)], [],
        even, odd, reaction.T,
    )
    kabove, kbelow = ahead(up), back(down)
    kin_odd, kin_even = pairs(own, True), pairs(own, False)

    wide = (FIELDS, WX * CY, CZ)
    middle = MID[1] - MID[0]
    padded = (FIELDS, CX, FY, CZ)
    mids = call(
        functools.partial(smooth_middle, nrow, ncol),
        [(FIELDS, middle * CY, CZ)] * 2 + [(3, middle // 2 * HY, CZ),
         (2, 3, 2, FIELDS, FY, CZ), (2, 3, FIELDS, FN, CZ), (2, 3, FIELDS, CY, CZ)],
        [padded] * 6 + [padded[1:], (2, FIELDS + 1, CY, CZ)],
        reaction, b, material, even, odd,
        limit=16, microseconds=100,
    )
    padded = (FIELDS, GX, FY, CZ)
    first, scaled, code, coarse, up, down, side_even, side_odd, kin = call(
        functools.partial(smooth_outer, nrow, ncol),
        [fine, wide, padded[1:], (3, VX * HY, CZ)]
        + [(FACE_LINES, CZ)] * 2 + [(SIDE_LINES, CZ)] * 2 + [(3, KIN_LINES, CZ)],
        [padded] * 6 + [(2, FIELDS + 1, CY, CZ)],
        reaction, b, material, above, below, even, odd, kabove, kbelow, own, kin_even, kin_odd, *mids,
        limit=26,
    )
    odd, even = pairs(side_odd, True), pairs(side_even, False)
    above, below = ahead(up), back(down)
    kin_above, kin_below = ahead(kin), back(kin)
    up, down = call(pack_knots, [(KNOT_LINES, CZ)] * 2, [], even, odd, microseconds=100)
    kabove, kbelow = ahead(up), back(down)

    qpadded = (2, QX, QY, CZ)
    start, qscaled, qinverse, sums = call(
        functools.partial(smooth_coarse, nrow, ncol),
        [(2, HX + 4, 32, CZ), (2, HX + 10, 32, CZ), (2, HX + 10, 32, CZ), (nrow * ncol, CZ)],
        [qpadded, qpadded, qpadded[1:]] + [qpadded] * 4,
        reaction, coarse, above, below, even, odd, kabove, kbelow,
        limit=14, microseconds=2.5,
    )

    sums, kin_above, kin_below = lax.optimization_barrier((sums, kin_above, kin_below))
    gathered = lax.all_to_all(sums, ("row", "col"), 0, 0)

    epadded = (2, EX, QY, CZ)
    padded = (FIELDS, FX, FY, CZ)
    (out,) = call(
        functools.partial(smooth_second, nrow, ncol),
        [fine],
        [(FIELDS, nrow, CZ), (2, FIELDS, 32, CZ)] + [epadded] * 5 + [(2, EX, 32, CZ)] + [padded] * 2
        + [(FIELDS, FX // 2, FY, CZ)] + [padded] * 3 + [fine, pltpu.SemaphoreType.DMA((2 * FIELDS,))],
        reaction, gathered, kin, kin_above, kin_below,
        start, qscaled, qinverse, first, scaled, code, above, below, even, odd,
        limit=30, microseconds=7, out_hbm=True,
    )
    return out.reshape(right_side.shape)


def solution(mesh):
    placed = (
        P(None, "row", "col", None),
        P("row", "col", None),
        P(),
        P(None, ("row", "col"), None),
    )
    return jax.shard_map(
        body, mesh=mesh, in_specs=placed, out_specs=P(None, "row", "col", None), check_vma=False
    )
```

```python
import functools

import jax
import jax.numpy as jnp
from jax import lax
from jax.experimental import pallas as pl
from jax.experimental.pallas import tpu as pltpu
from jax.sharding import PartitionSpec as P

FIELDS = 4
CX, CY, CZ = 16, 32, 128
HX, HY = CX // 2, CY // 2
GROUPS = 8
SWEEPS = 4
LOW_BOUND = 0.25
HIGH_BOUND = 2.0
THETA = (HIGH_BOUND + LOW_BOUND) / 2.0
DELTA = (HIGH_BOUND - LOW_BOUND) / 2.0

WX = CX + 4
GX, FY, FO, FN = CX + 12, CY + 24, 8, CY + 8
OWN = slice(FO, FO + CY)
ALL = slice(FO, FO + FN)
FX = CX + 8
MID = (4, CX - 4)
VX = HX + 2
QX, QY, QO = HX + 18, HY + 32, 16
EX = HX + 12
CORNER_AT = {1: 0, 2: 9, 3: 17, 4: 24, 5: 30, 6: 35, 7: 39, 8: 42, 9: 44}
CORNER_LINES = 48
FINE_CORNER_AT = {1: 0, 2: 5, 3: 9, 4: 12}
FINE_CORNER_LINES = (FIELDS + 1) * 32

LAYER_LINES = (FIELDS + 1) * 6 * CY
BAND_LINES = (FIELDS + 1) * 4 * CX
KIN_LINES = FIELDS * GROUPS * 8
COARSE_LINES = 3 * (HX + 1) * HY
FACE_LINES = COARSE_LINES + FIELDS * CY
STRIP_LINES = 272
STRIP_AT = {1: 0, 2: WX, 3: 2 * WX - 2}
SIDE_LINES = STRIP_LINES + FIELDS * (3 * WX - 6)
KNOT_LINES = 6 * CORNER_LINES


def coefficients():
    rho = DELTA / THETA
    pairs = []
    for _ in range(SWEEPS - 1):
        following = 1.0 / (2.0 * THETA / DELTA - rho)
        pairs.append((following * rho, 2.0 * following / DELTA))
        rho = following
    return pairs


def every(low, high, step):
    for i in range(low, high):
        step(i)


def lanes():
    return lax.broadcasted_iota(jnp.int32, (1, CZ), 1)


def beside(ref, f, x, low, count, width, share=1):
    after, before, x = (x + 1) // share, (x - 1) // share, x // share
    here = ref[f, x, low : low + count, :]
    lane = lanes()
    total = ref[f, after, low : low + count, :] + ref[f, before, low : low + count, :]
    total = total + ref[f, x, low + 1 : low + 1 + count, :]
    total = total + ref[f, x, low - 1 : low - 1 + count, :]
    total = total + jnp.where(lane < CZ - width, pltpu.roll(here, CZ - width, 1), 0.0)
    total = total + jnp.where(lane >= width, pltpu.roll(here, width, 1), 0.0)
    return here, total


def diagonal_values(reaction, f):
    low = reaction[2 * f : 2 * f + 1, :]
    jump = reaction[2 * f + 1 : 2 * f + 2, :] - low
    return 6.0 + low, 6.0 + low + jump


def inverse_of(code, reaction, f):
    fluid, solid = diagonal_values(reaction, f)
    fluid, solid = 1.0 / fluid, 1.0 / solid
    return jnp.where(code == 0.0, fluid, jnp.where(code == 1.0, solid, 0.0))


def place():
    return lax.axis_index("row"), lax.axis_index("col")


def by_parity(step, first, second):
    even = lax.rem(lax.axis_index("col"), 2) == 0
    pl.when(even)(functools.partial(step, second, first))
    pl.when(jnp.logical_not(even))(functools.partial(step, first, second))


def pack_layers(
    b, material, inverse, up, down, first, second, own,
    b_here, material_here, inverse_here, solid, first_here, second_here, own_here, sems, out_sems,
):
    copies = [pltpu.make_async_copy(b.at[f], b_here.at[f], sems.at[f]) for f in range(FIELDS)]
    copies.append(pltpu.make_async_copy(material, material_here, sems.at[FIELDS]))
    copies.append(pltpu.make_async_copy(inverse, inverse_here, sems.at[FIELDS + 1]))
    for copy in copies:
        copy.start()
    sent = []

    def send(source, target):
        sent.append(pltpu.make_async_copy(source, target, out_sems.at[len(sent)]))
        sent[-1].start()

    for f in range(FIELDS + 1):
        copies[f].wait()
        layer, band = 6 * CY, 4 * CX
        if f < FIELDS:
            take = lambda start, size, step: b_here[f, pl.ds(start, size, stride=step), :]
            ends = (b_here.at[f, pl.ds((CX - 6) * CY, layer)], b_here.at[f, pl.ds(0, layer)])
        else:
            take = lambda start, size, step: material_here[
                pl.ds(start, size, stride=step), :
            ].astype(jnp.float32)
            solid[0] = take((CX - 6) * CY, layer, 1)
            solid[1] = take(0, layer, 1)
            ends = (solid.at[0], solid.at[1])
        for source, target in zip(ends, (up, down)):
            send(source, target.at[pl.ds(f * layer, layer)])

        def bands(left, right):
            for i in range(4):
                at = f * band + i * CX
                right[at : at + CX, :] = take(CY - 4 + i, CX, CY)
                left[at : at + CX, :] = take(i, CX, CY)

        by_parity(bands, first_here, second_here)
        for source, target in ((first_here, first), (second_here, second)):
            send(source.at[pl.ds(f * band, band)], target.at[pl.ds(f * band, band)])
    copies[FIELDS + 1].wait()
    for f in range(FIELDS):
        for k in range(inverse.shape[2] // CZ):
            at = (f * GROUPS + k) * GROUPS
            own_here[at : at + GROUPS, :] = inverse_here[f, :, k * CZ : (k + 1) * CZ]
    send(own_here, own)
    for copy in sent:
        copy.wait()


def pack_corners(first, second, reaction, up, down, constants):
    for f in range(FIELDS):
        for i in range(2):
            constants[2 * f + i : 2 * f + i + 1, :] = jnp.broadcast_to(
                reaction[i : i + 1, f : f + 1], (1, CZ)
            )

    def pack(low, high):
        for side, ref in enumerate((low, high)):
            for f in range(FIELDS + 1):
                for j, offset in FINE_CORNER_AT.items():
                    size = 6 - j
                    line = (f * 4 + (j - 1 if side else 4 - j)) * CX
                    at = (f * 2 + side) * 16 + offset
                    up[at : at + size, :] = ref[line + CX - size : line + CX, :]
                    down[at : at + size, :] = ref[line : line + size, :]
                at = (f * 2 + side) * 16 + 14
                up[at : at + 2, :] = jnp.zeros((2, CZ), jnp.float32)
                down[at : at + 2, :] = jnp.zeros((2, CZ), jnp.float32)

    by_parity(pack, first, second)


def halo_row(j, is_high):
    return FO + CY - 1 + j if is_high else FO + FN - j


def go_round(ref, f, x, value):
    ref[f, x, ALL, :] = value
    ref[f, x, FO - 1 : FO, :] = value[FN - 1 : FN]
    ref[f, x, FO + FN : FO + FN + 1, :] = value[0:1]


def fine_scale(x, reaction, code, s, inv, p0):
    kind = code[x, ALL, :]
    for f in range(FIELDS):
        inverse = inverse_of(kind, reaction, f)
        inv[f, x, ALL, :] = inverse
        if p0 is not None:
            value = inverse * s[f, x, ALL, :]
            s[f, x, ALL, :] = value
            go_round(p0, f, x, value * (1.0 / THETA))


def fine_sweep(x, k, s, inv, parts):
    keep, gain = coefficients()[k]
    for f in range(FIELDS):
        here, total = beside(parts[k], f, x, FO, FN, 1)
        value = s[f, x, ALL, :] - here + inv[f, x, ALL, :] * total
        s[f, x, ALL, :] = value
        go_round(parts[k + 1], f, x, keep * here + gain * value)


def fine_last(x, reaction, code, s, inv, p3, scaled, line):
    residues = []
    for f in range(FIELDS):
        fluid, solid = diagonal_values(reaction, f)
        here, total = beside(p3, f, x, FO, CY, 1)
        value = s[f, x, OWN, :] - here + inv[f, x, OWN, :] * total
        scaled[f, line : line + CY, :] = value
        residues.append(jnp.where(code[x, OWN, :] == 1.0, solid, fluid) * value)
    return residues


def restrict(x, residues, code, pair, coarse, line):
    parity = lanes() % 2 == 0
    sums = [one + other for one, other in zip(*residues)]
    sums.append(code[x, OWN, :] + code[x + 1, OWN, :])
    halves = []
    for f, value in enumerate(sums):
        here = pair.at[x // 2 % 2, f]
        here[...] = value
        halves.append(here[pl.ds(0, HY, stride=2), :] + here[pl.ds(1, HY, stride=2), :])
    halves.append(halves[4])
    for plane in range(3):
        even, odd = halves[2 * plane], halves[2 * plane + 1]
        merged = jnp.where(
            parity, even + pltpu.roll(even, CZ - 1, 1), odd + pltpu.roll(odd, 1, 1)
        )
        merged = merged * 0.5 if plane < 2 else jnp.where(merged > 8.5, -1.0, merged)
        coarse[plane, line : line + HY, :] = merged


def lay_own(x_at, xs, b, material, s, code):
    zeros = jnp.zeros((8, CZ), jnp.float32)
    for x in xs:
        for f in range(FIELDS):
            s[f, x + x_at, OWN, :] = b[f, x * CY : x * CY + CY, :]
            s[f, x + x_at, FO + CY : FO + FN, :] = zeros
        code[x + x_at, OWN, :] = material[x * CY : x * CY + CY, :].astype(jnp.float32)
        code[x + x_at, FO + CY : FO + FN, :] = zeros + 2.0


def putter(s, code):
    sflat = s.reshape(FIELDS, s.shape[1] * FY, CZ)
    cflat = code.reshape(s.shape[1] * FY, CZ)

    def put(f, x, y_row, size, value):
        to = pl.ds(x * FY + y_row, size, stride=FY)
        if f < FIELDS:
            sflat[f, to, :] = value
        else:
            cflat[to, :] = value

    return put


def lay_bands(x_at, spans, ncol, put, even, odd):
    _, col = place()

    def bands(ref, is_high):
        for f in range(FIELDS + 1):
            for i in range(4):
                at = (f * 4 + i) * CX
                row = halo_row(i + 1 if is_high else 4 - i, is_high)
                for x, size in spans if f < FIELDS else ((0, CX),):
                    put(f, x + x_at, row, size, ref[at + x : at + x + size, :])

    def sides(low, high):
        pl.when(col > 0)(functools.partial(bands, low, 0))
        pl.when(col < ncol - 1)(functools.partial(bands, high, 1))

    by_parity(sides, even, odd)


def kept_lines():
    for side in range(2):
        for k in range(1, SWEEPS):
            flip = lambda x: CX - 1 - x if side else x
            yield side, k, (flip(k), flip(k + 1)), flip(k)


def smooth_middle(
    nrow, ncol, reaction, b, material, even, odd,
    first, scaled, coarse, keep_p, keep_s, keep_sum,
    s, inv, p0, p1, p2, p3, code, pair,
):
    parts = (p0, p1, p2, p3)
    lay_own(0, range(CX), b, material, s, code)
    lay_bands(0, ((0, CX),), ncol, putter(s, code), even, odd)
    every(0, CX, lambda x: fine_scale(x, reaction, code, s, inv, p0))
    for k in range(SWEEPS - 1):
        every(k + 1, CX - k - 1, lambda x: fine_sweep(x, k, s, inv, parts))
        for side, step, lines, line in kept_lines():
            if step == k + 1:
                for f in range(FIELDS):
                    for i, x in enumerate(lines):
                        keep_p[side, k, i, f] = parts[step][f, x]
                    keep_s[side, k, f] = s[f, line, ALL, :]
    for x in range(*MID, 2):
        residues = []
        for h in range(2):
            line = (x + h - MID[0]) * CY
            residues.append(fine_last(x + h, reaction, code, s, inv, p3, scaled, line))
            for f in range(FIELDS):
                first[f, line : line + CY, :] = sum(p[f, x + h, OWN, :] for p in parts)
        restrict(x, residues, code, pair, coarse, (x - MID[0]) // 2 * HY)
    for side in range(2):
        for i in range(1, SWEEPS):
            x = CX - 1 - i if side else i
            for f in range(FIELDS):
                keep_sum[side, i - 1, f] = sum(p[f, x, OWN, :] for p in parts[: i + 1])


def smooth_outer(
    nrow, ncol, reaction, b, material, above, below, even, odd, kabove, kbelow,
    own, kin_even, kin_odd, mid_first, mid_scaled, mid_coarse, keep_p, keep_s, keep_sum,
    first, scaled, code, coarse, up, down, side_even, side_odd, kin,
    s, inv, p0, p1, p2, p3, pair,
):
    row, col = place()
    parts = (p0, p1, p2, p3)
    at_x = 6
    zeros = jnp.zeros((FN, CZ), jnp.float32)
    for x in (*range(6), *range(GX - 6, GX)):
        for f in range(FIELDS):
            s[f, x, ALL, :] = zeros
        code[x, ALL, :] = zeros + 2.0
    outer = (*range(4), *range(CX - 4, CX))
    lay_own(at_x, outer, b, material, s, code)
    for x in range(4, CX - 4):
        code[x + at_x, OWN, :] = material[x * CY : x * CY + CY, :].astype(jnp.float32)
        code[x + at_x, FO + CY : FO + FN, :] = zeros[:8] + 2.0
    put = putter(s, code)

    def rows(first_x, ref):
        for i in range(6):
            for f in range(FIELDS):
                at = (f * 6 + i) * CY
                s[f, first_x + i, OWN, :] = ref[at : at + CY, :]
            at = (FIELDS * 6 + i) * CY
            code[first_x + i, OWN, :] = ref[at : at + CY, :]

    pl.when(row > 0)(functools.partial(rows, 0, above))
    pl.when(row < nrow - 1)(functools.partial(rows, GX - 6, below))
    lay_bands(at_x, ((0, 4), (CX - 4, 4)), ncol, put, even, odd)

    def corners(ref, is_above, is_high):
        for f in range(FIELDS + 1):
            for j, offset in FINE_CORNER_AT.items():
                size = 6 - j
                at = (f * 2 + is_high) * 16 + offset
                x = 6 - size if is_above else 6 + CX
                put(f, x, halo_row(j, is_high), size, ref[at : at + size, :])

    for ref, is_above, in_x in ((kabove, 1, row > 0), (kbelow, 0, row < nrow - 1)):
        for is_high, in_y in ((0, col > 0), (1, col < ncol - 1)):
            pl.when(in_x & in_y)(functools.partial(corners, ref, is_above, is_high))

    def both(low, high, step):
        for x in range(low, high):
            step(x + at_x)
            step(CX - 1 - x + at_x)

    both(-6, 2, lambda x: fine_scale(x, reaction, code, s, inv, p0))
    both(2, 4, lambda x: fine_scale(x, reaction, code, s, inv, None))
    for side, k, lines, line in kept_lines():
        for f in range(FIELDS):
            for i, x in enumerate(lines):
                parts[k][f, x + at_x] = keep_p[side, k - 1, i, f]
    for k in range(SWEEPS - 1):
        if k > 0:
            for side, step, lines, line in kept_lines():
                if step == k:
                    for f in range(FIELDS):
                        s[f, line + at_x, ALL, :] = keep_s[side, k - 1, f]
        both(k - 5, k + 1, lambda x: fine_sweep(x, k, s, inv, parts))
    for side, step, lines, line in kept_lines():
        if step == SWEEPS - 1:
            for f in range(FIELDS):
                s[f, line + at_x, ALL, :] = keep_s[side, step - 1, f]
    for x in (*range(-2, 4, 2), *range(CX - 4, CX + 2, 2)):
        residues = []
        for h in range(2):
            line = (x + h + 2) * CY
            residues.append(
                fine_last(x + h + at_x, reaction, code, s, inv, p3, scaled, line)
            )
        restrict(x + at_x, residues, code, pair, coarse, (x // 2 + 1) * HY)
    for f in range(FIELDS):
        for x in range(CX):
            out = slice(x * CY, x * CY + CY)
            side = x >= CX // 2
            i = CX - 1 - x if side else x
            if i < 4:
                some = [p[f, x + at_x, OWN, :] for p in (parts if i == 0 else parts[i + 1 :])]
                if i > 0:
                    some.append(keep_sum[int(side), i - 1, f])
                first[f, out, :] = sum(some)
            else:
                mid = slice((x - MID[0]) * CY, (x - MID[0] + 1) * CY)
                first[f, out, :] = mid_first[f, mid, :]
                scaled[f, (x + 2) * CY : (x + 3) * CY, :] = mid_scaled[f, mid, :]
    for plane in range(3):
        size = (MID[1] - MID[0]) // 2 * HY
        at = (MID[0] // 2 + 1) * HY
        coarse[plane, at : at + size, :] = mid_coarse[plane]

    for f in range(FIELDS):
        at = COARSE_LINES + f * CY
        up[at : at + CY, :] = scaled[f, (CX - 1) * CY : CX * CY, :]
        down[at : at + CY, :] = scaled[f, 4 * CY : 5 * CY, :]
    for plane in range(3):
        at, size = plane * (HX + 1) * HY, (HX + 1) * HY
        up[at : at + size, :] = coarse[plane, 0:size, :]
        down[at : at + size, :] = coarse[plane, HY : HY + size, :]

    kin[0] = own[...]

    def gather(low, high):
        kin[1] = low[...]
        kin[2] = high[...]

    by_parity(gather, kin_even, kin_odd)

    def strips(left, right):
        for plane in range(3):
            for i in range(9):
                at = (plane * 9 + i) * VX
                right[at : at + VX, :] = coarse[plane, pl.ds(HY - 9 + i, VX, stride=HY), :]
                left[at : at + VX, :] = coarse[plane, pl.ds(i, VX, stride=HY), :]
        for f in range(FIELDS):
            for j, offset in STRIP_AT.items():
                size = WX + 2 - 2 * j
                at = STRIP_LINES + f * (3 * WX - 6) + offset
                x = (j - 1) * CY
                right[at : at + size, :] = scaled[f, pl.ds(x + CY - j, size, stride=CY), :]
                left[at : at + size, :] = scaled[f, pl.ds(x + j - 1, size, stride=CY), :]

    by_parity(strips, side_even, side_odd)


def pack_knots(first, second, up, down):
    def pack(low, high):
        for plane in range(3):
            for side, ref in enumerate((low, high)):
                base = (plane * 2 + side) * CORNER_LINES
                up[base + 40 : base + 48, :] = jnp.zeros((8, CZ), jnp.float32)
                down[base + 40 : base + 48, :] = jnp.zeros((8, CZ), jnp.float32)
                for j, offset in CORNER_AT.items():
                    size = 10 - j
                    line = (plane * 9 + (j - 1 if side else 9 - j)) * VX
                    at = base + offset
                    up[at : at + size, :] = ref[line + VX - 1 - size : line + VX - 1, :]
                    down[at : at + size, :] = ref[line + 1 : line + 1 + size, :]

    by_parity(pack, first, second)


def coarse_constants(reaction, plane):
    parity = lanes() % 2 == 0
    even, odd = (
        [reaction[2 * f + i : 2 * f + i + 1, :] for i in range(2)]
        for f in (2 * plane, 2 * plane + 1)
    )
    low = jnp.where(parity, even[0], odd[0])
    return 8.0 * low, jnp.where(parity, even[1] - even[0], odd[1] - odd[0])


def smooth_coarse(
    nrow, ncol, reaction, coarse, above, below, even, odd, kabove, kbelow,
    start, scaled, inverse_out, sums,
    s, inv, count, p0, p1, p2, p3,
):
    row, col = place()
    parts = (p0, p1, p2, p3)
    zeros = jnp.zeros((QY, CZ), jnp.float32)

    def clear(x):
        for plane in range(2):
            s[plane, x] = zeros
        count[x] = zeros - 1.0

    every(0, QX, clear)
    sflat = s.reshape(2, QX * QY, CZ)
    cflat = count.reshape(QX * QY, CZ)

    def put(plane, start_row, size, value):
        if plane < 2:
            sflat[plane, pl.ds(start_row, size, stride=QY), :] = value
        else:
            cflat[pl.ds(start_row, size, stride=QY), :] = value

    def block(plane, x, value):
        if plane < 2:
            s[plane, x, QO : QO + HY, :] = value
        else:
            count[x, QO : QO + HY, :] = value

    def rows(first_x, ref):
        for plane in range(3):
            for i in range(HX + 1):
                at = (plane * (HX + 1) + i) * HY
                block(plane, first_x + i, ref[at : at + HY, :])

    for plane in range(3):
        for i in range(HX):
            block(plane, 9 + i, coarse[plane, (i + 1) * HY : (i + 2) * HY, :])
    pl.when(row > 0)(functools.partial(rows, 0, above))
    pl.when(row < nrow - 1)(functools.partial(rows, 9 + HX, below))

    def strips(ref, first_y):
        for plane in range(3):
            for i in range(9):
                line = (plane * 9 + i) * VX
                put(plane, 9 * QY + first_y + i, HX, ref[line + 1 : line + 1 + HX, :])

    def sides(low, high):
        pl.when(col > 0)(functools.partial(strips, low, QO - 9))
        pl.when(col < ncol - 1)(functools.partial(strips, high, QO + HY))

    by_parity(sides, even, odd)

    def corners(ref, is_above, is_high):
        for plane in range(3):
            base = (plane * 2 + is_high) * CORNER_LINES
            for j, at in CORNER_AT.items():
                size = 10 - j
                x = 9 - size if is_above else 9 + HX
                y = QO + HY - 1 + j if is_high else QO - j
                put(plane, x * QY + y, size, ref[base + at : base + at + size, :])

    for ref, is_above, in_x in ((kabove, 1, row > 0), (kbelow, 0, row < nrow - 1)):
        for is_high, in_y in ((0, col > 0), (1, col < ncol - 1)):
            pl.when(in_x & in_y)(functools.partial(corners, ref, is_above, is_high))

    def scale(x):
        number = count[x]
        for plane in range(2):
            low8, jump = coarse_constants(reaction, plane)
            inverse = jnp.where(number < 0.0, 0.0, 1.0 / (6.0 + 0.5 * (low8 + jump * number)))
            value = inverse * s[plane, x]
            inv[plane, x] = inverse
            s[plane, x] = value
            p0[plane, x] = value * (1.0 / THETA)

    every(0, QX, scale)

    for k, (keep, gain) in enumerate(coefficients()):
        def sweep(x):
            for plane in range(2):
                here, total = beside(parts[k], plane, x, 8, 32, 2)
                value = s[plane, x, 8:40, :] - here + inv[plane, x, 8:40, :] * total
                s[plane, x, 8:40, :] = value
                parts[k + 1][plane, x, 8:40, :] = keep * here + gain * value

        every(k + 1, QX - k - 1, sweep)

    def finish(x):
        for plane in range(2):
            here, total = beside(p3, plane, x, 8, 32, 2)
            value = s[plane, x, 8:40, :] - here + inv[plane, x, 8:40, :] * total
            scaled[plane, x - 4] = value
            inverse_out[plane, x - 4] = inv[plane, x, 8:40, :]

    every(4, QX - 4, finish)

    def add(x):
        for plane in range(2):
            start[plane, x - 7] = (
                p0[plane, x, 8:40, :] + p1[plane, x, 8:40, :]
                + p2[plane, x, 8:40, :] + p3[plane, x, 8:40, :]
            )

    every(7, QX - 7, add)

    lane = lanes()
    message = jnp.zeros((8, CZ), jnp.float32)
    for plane in range(2):
        low8, jump = coarse_constants(reaction, plane)
        total = jnp.zeros((HY, CZ), jnp.float32)
        for x in range(9, 9 + HX):
            diagonal = 6.0 + 0.5 * (low8 + jump * count[x, QO : QO + HY, :])
            total = total + diagonal * scaled[plane, x - 4, 8 : 8 + HY, :]
        total = total[:8] + total[8:]
        for shift in (4, 2, 1):
            total = total + pltpu.roll(total, shift, 0)
        for shift in (2, 4, 8):
            total = total + pltpu.roll(total, CZ - shift, 1)
        for odd in range(2):
            for g in range(GROUPS):
                to = (2 * plane + odd) * GROUPS + g
                moved = pltpu.roll(total, (to - 16 * g - odd) % CZ, 1)
                message = jnp.where(lane == to, moved, message)
    sums[...] = jnp.broadcast_to(message[:1], sums.shape)


def smooth_second(
    nrow, ncol, reaction, gathered, kin, kin_above, kin_below,
    start, qscaled, qinverse, first, scaled, code, above, below, even, odd,
    out,
    wide, spread, e, q0, q1, q2, q3, qs, fs, inv, f0, p0, p1, p2, out_here, sems,
):
    row, col = place()
    lane = lanes()
    width = ncol * GROUPS
    fields = [jnp.zeros((nrow, CZ), jnp.float32) for _ in range(FIELDS)]
    for c in range(ncol):
        some = gathered[pl.ds(c, nrow, stride=ncol), :]
        for f in range(FIELDS):
            moved = pltpu.roll(some, (c * GROUPS - f * GROUPS) % CZ, 1)
            here = (lane >= c * GROUPS) & (lane < (c + 1) * GROUPS)
            fields[f] = jnp.where(here, moved, fields[f])
    for f in range(FIELDS):
        wide[f] = fields[f]

    group = lax.broadcasted_iota(jnp.int32, (GROUPS, CZ), 0)
    spot = lax.broadcasted_iota(jnp.int32, (GROUPS, CZ), 1)
    mask = [(spot // 16 == group) & (spot % 2 == odd) for odd in range(2)]
    e[...] = jnp.zeros_like(e)

    def product(rows_of, f):
        total = jnp.zeros((GROUPS, width), jnp.float32)
        for k in range(nrow):
            total = total + rows_of(f, k) * wide[f, k : k + 1, 0:width]
        return jnp.sum(total, axis=1, keepdims=True)

    def neighbour(rows_of, dx, dy, inside):
        for plane in range(2):
            even = product(rows_of, 2 * plane)
            odd = product(rows_of, 2 * plane + 1)
            full = jnp.where(mask[0], even, jnp.where(mask[1], odd, 0.0))
            line = jnp.sum(full, axis=0, keepdims=True)
            if inside is not None:
                line = jnp.where(inside, line, 0.0)
            x_from, x_to = {-1: (0, 6), 0: (6, 6 + HX), 1: (6 + HX, EX)}[dx]
            y_from, y_to = {-1: (8, QO), 0: (QO, QO + HY), 1: (QO + HY, QO + HY + 8)}[dy]
            for x in range(x_from, x_to):
                e[plane, x, y_from:y_to, :] = jnp.broadcast_to(line, (y_to - y_from, CZ))

    def slab(ref, part):
        def rows_of(f, k):
            at = (f * GROUPS + k) * GROUPS
            return ref[part, at : at + GROUPS, :]

        return rows_of

    in_x = {-1: row > 0, 0: True, 1: row < nrow - 1}
    in_y = {-1: col > 0, 0: True, 1: col < ncol - 1}
    for dx, ref in ((0, kin), (-1, kin_above), (1, kin_below)):
        for part, dy in enumerate((0, -1, 1)):
            inside = in_x[dx] & in_y[dy] if (dx, dy) != (0, 0) else None
            neighbour(slab(ref, part), dx, dy, inside)

    parts = (q0, q1, q2, q3)

    def begin(x):
        for plane in range(2):
            here, total = beside(e, plane, x, 8, 32, 2)
            value = qscaled[plane, x - 1] - here + qinverse[plane, x - 1] * total
            qs[plane, x] = value
            q0[plane, x, 8:40, :] = value * (1.0 / THETA)

    every(1, EX - 1, begin)
    for k, (keep, gain) in enumerate(coefficients()):
        def sweep(x):
            for plane in range(2):
                here, total = beside(parts[k], plane, x, 8, 32, 2)
                value = qs[plane, x] - here + qinverse[plane, x - 1] * total
                qs[plane, x] = value
                parts[k + 1][plane, x, 8:40, :] = keep * here + gain * value

        every(k + 2, EX - k - 2, sweep)

    parity = lane % 2 == 0

    def lift(i):
        for plane in range(2):
            total = start[plane, i] + e[plane, i + 4, 8:40, :]
            total = total + q0[plane, i + 4, 8:40, :] + q1[plane, i + 4, 8:40, :]
            total = total + q2[plane, i + 4, 8:40, :] + q3[plane, i + 4, 8:40, :]
            for odd in range(2):
                if odd:
                    value = jnp.where(parity, pltpu.roll(total, CZ - 1, 1), total)
                else:
                    value = jnp.where(parity, total, pltpu.roll(total, 1, 1))
                some = spread.at[i % 2, 2 * plane + odd]
                some[...] = value
                high, low = some[8:26, :], some[6:8, :]
                to = f0.at[2 * plane + odd, i]
                for y in range(2):
                    to[pl.ds(FO + y, 18, stride=2), :] = high
                    to[pl.ds(FO + FN - 4 + y, 2, stride=2), :] = low
                to[FO - 1 : FO, :] = low[1:2]
                to[FO + FN : FO + FN + 1, :] = high[0:1]

    every(0, HX + 4, lift)

    zeros = jnp.zeros((FN, CZ), jnp.float32)
    for f in range(FIELDS):
        for x in (1, FX - 2):
            fs[f, x, ALL, :] = zeros
        for x in range(2, FX - 2):
            fs[f, x, OWN, :] = scaled[f, (x - 2) * CY : (x - 1) * CY, :]
            fs[f, x, FO + CY : FO + FN, :] = zeros[:8]
    sflat = fs.reshape(FIELDS, FX * FY, CZ)

    def face(x, ref):
        for f in range(FIELDS):
            at = COARSE_LINES + f * CY
            fs[f, x, OWN, :] = ref[at : at + CY, :]

    pl.when(in_x[-1])(functools.partial(face, 1, above))
    pl.when(in_x[1])(functools.partial(face, FX - 2, below))

    def strips(ref, is_high):
        for f in range(FIELDS):
            for j, offset in STRIP_AT.items():
                size = WX + 2 - 2 * j
                at = STRIP_LINES + f * (3 * WX - 6) + offset
                start = (1 + j) * FY + halo_row(j, is_high)
                sflat[f, pl.ds(start, size, stride=FY), :] = ref[at : at + size, :]

    def sides(low, high):
        pl.when(in_y[-1])(functools.partial(strips, low, 0))
        pl.when(in_y[1])(functools.partial(strips, high, 1))

    by_parity(sides, even, odd)

    parts = (p0, p1, p2)

    def open_fine(x):
        kind = code[x + 2, ALL, :]
        for f in range(FIELDS):
            here, total = beside(f0, f, x, FO, FN, 1, 2)
            inverse = inverse_of(kind, reaction, f)
            inv[f, x, ALL, :] = inverse
            value = fs[f, x, ALL, :] - here + inverse * total
            fs[f, x, ALL, :] = value
            go_round(p0, f, x, value * (1.0 / THETA))

    every(1, FX - 1, open_fine)
    for k in range(2):
        every(k + 2, FX - k - 2, lambda x: fine_sweep(x, k, fs, inv, parts))

    keep, gain = coefficients()[2]

    sent = []
    part = CX // 2
    for f in range(FIELDS):
        for i in range(CX):
            x = i + 4
            at = slice(i * CY, i * CY + CY)
            here, total = beside(p2, f, x, FO, CY, 1)
            value = fs[f, x, OWN, :] - here + inv[f, x, OWN, :] * total
            result = first[f, at, :] + f0[f, x // 2, OWN, :] + p0[f, x, OWN, :]
            result = result + p1[f, x, OWN, :] + here
            out_here[f, at, :] = result + (keep * here + gain * value)
            if i % part == part - 1:
                lines = pl.ds((i + 1 - part) * CY, part * CY)
                copy = pltpu.make_async_copy(
                    out_here.at[f, lines], out.at[f, lines], sems.at[len(sent)]
                )
                copy.start()
                sent.append(copy)
    for copy in sent:
        copy.wait()


def call(kernel, out_shapes, scratch, *args, limit=16, in_hbm=False, out_hbm=False, microseconds=0.1):
    vmem = pl.BlockSpec(memory_space=pltpu.VMEM)
    hbm = pl.BlockSpec(memory_space=pltpu.HBM)
    given, taken = hbm if in_hbm else vmem, hbm if out_hbm else vmem
    return pl.pallas_call(
        kernel,
        out_shape=[jax.ShapeDtypeStruct(shape, jnp.float32) for shape in out_shapes],
        in_specs=[given] * len(args),
        out_specs=[taken] * len(out_shapes),
        scratch_shapes=[
            pltpu.VMEM(shape, jnp.float32) if isinstance(shape, tuple) else shape
            for shape in scratch
        ],
        cost_estimate=pl.CostEstimate(
            flops=int(microseconds * 1e6), bytes_accessed=int(microseconds * 3.5e6), transcendentals=0
        ),
        compiler_params=pltpu.CompilerParams(vmem_limit_bytes=int(limit * 1024 * 1024)),
    )(*args)


def ahead(value):
    count = lax.axis_size("row")
    return lax.ppermute(value, "row", [(i, (i + 1) % count) for i in range(count)])


def back(value):
    count = lax.axis_size("row")
    return lax.ppermute(value, "row", [((i + 1) % count, i) for i in range(count)])


def pairs(value, odd):
    nrow, ncol = lax.axis_size("row"), lax.axis_size("col")
    moves = []
    for r in range(nrow):
        for c in range(ncol):
            if not odd:
                to = (r, c ^ 1)
            elif c in (0, ncol - 1):
                to = (r ^ 1, c)
            else:
                to = (r, c + 1 if c % 2 else c - 1)
            moves.append((r * ncol + c, to[0] * ncol + to[1]))
    return lax.ppermute(value, ("row", "col"), moves)


def body(right_side, material, reaction, coarse_inverse):
    nrow, ncol = lax.axis_size("row"), lax.axis_size("col")
    b = right_side.reshape(FIELDS, CX * CY, CZ)
    material = material.reshape(CX * CY, CZ)

    fine = (FIELDS, CX * CY, CZ)
    up, down, even, odd, own = call(
        pack_layers,
        [(LAYER_LINES, CZ)] * 2 + [(BAND_LINES, CZ)] * 2 + [(KIN_LINES, CZ)],
        [fine, pltpu.VMEM(fine[1:], jnp.int32), coarse_inverse.shape,
         (2, 6 * CY, CZ), (BAND_LINES, CZ), (BAND_LINES, CZ), (KIN_LINES, CZ),
         pltpu.SemaphoreType.DMA((FIELDS + 2,)), pltpu.SemaphoreType.DMA((4 * FIELDS + 5,))],
        b, material, coarse_inverse,
        in_hbm=True, out_hbm=True, limit=59.27,
    )
    odd, even = pairs(odd, True), pairs(even, False)
    above, below = ahead(up), back(down)
    even, odd, above, below = lax.optimization_barrier((even, odd, above, below))
    up, down, reaction = call(
        pack_corners, [(FINE_CORNER_LINES, CZ)] * 2 + [(2 * FIELDS, CZ)], [],
        even, odd, reaction.T,
    )
    kabove, kbelow = ahead(up), back(down)
    kin_odd, kin_even = pairs(own, True), pairs(own, False)

    wide = (FIELDS, WX * CY, CZ)
    middle = MID[1] - MID[0]
    padded = (FIELDS, CX, FY, CZ)
    mids = call(
        functools.partial(smooth_middle, nrow, ncol),
        [(FIELDS, middle * CY, CZ)] * 2 + [(3, middle // 2 * HY, CZ),
         (2, 3, 2, FIELDS, FY, CZ), (2, 3, FIELDS, FN, CZ), (2, 3, FIELDS, CY, CZ)],
        [padded] * 6 + [padded[1:], (2, FIELDS + 1, CY, CZ)],
        reaction, b, material, even, odd,
        limit=16, microseconds=100,
    )
    padded = (FIELDS, GX, FY, CZ)
    first, scaled, code, coarse, up, down, side_even, side_odd, kin = call(
        functools.partial(smooth_outer, nrow, ncol),
        [fine, wide, padded[1:], (3, VX * HY, CZ)]
        + [(FACE_LINES, CZ)] * 2 + [(SIDE_LINES, CZ)] * 2 + [(3, KIN_LINES, CZ)],
        [padded] * 6 + [(2, FIELDS + 1, CY, CZ)],
        reaction, b, material, above, below, even, odd, kabove, kbelow, own, kin_even, kin_odd, *mids,
        limit=26,
    )
    odd, even = pairs(side_odd, True), pairs(side_even, False)
    above, below = ahead(up), back(down)
    kin_above, kin_below = ahead(kin), back(kin)
    up, down = call(pack_knots, [(KNOT_LINES, CZ)] * 2, [], even, odd, microseconds=100)
    kabove, kbelow = ahead(up), back(down)

    qpadded = (2, QX, QY, CZ)
    start, qscaled, qinverse, sums = call(
        functools.partial(smooth_coarse, nrow, ncol),
        [(2, HX + 4, 32, CZ), (2, HX + 10, 32, CZ), (2, HX + 10, 32, CZ), (nrow * ncol, CZ)],
        [qpadded, qpadded, qpadded[1:]] + [qpadded] * 4,
        reaction, coarse, above, below, even, odd, kabove, kbelow,
        limit=14, microseconds=2.5,
    )

    sums, kin_above, kin_below = lax.optimization_barrier((sums, kin_above, kin_below))
    gathered = lax.all_to_all(sums, ("row", "col"), 0, 0)

    epadded = (2, EX, QY, CZ)
    padded = (FIELDS, FX, FY, CZ)
    (out,) = call(
        functools.partial(smooth_second, nrow, ncol),
        [fine],
        [(FIELDS, nrow, CZ), (2, FIELDS, 32, CZ)] + [epadded] * 5 + [(2, EX, 32, CZ)] + [padded] * 2
        + [(FIELDS, FX // 2, FY, CZ)] + [padded] * 3 + [fine, pltpu.SemaphoreType.DMA((2 * FIELDS,))],
        reaction, gathered, kin, kin_above, kin_below,
        start, qscaled, qinverse, first, scaled, code, above, below, even, odd,
        limit=30, microseconds=7, out_hbm=True,
    )
    return out.reshape(right_side.shape)


def solution(mesh):
    placed = (
        P(None, "row", "col", None),
        P("row", "col", None),
        P(),
        P(None, ("row", "col"), None),
    )
    return jax.shard_map(
        body, mesh=mesh, in_specs=placed, out_specs=P(None, "row", "col", None), check_vma=False
    )
```

```python
import functools

import jax
import jax.numpy as jnp
from jax import lax
from jax.experimental import pallas as pl
from jax.experimental.pallas import tpu as pltpu
from jax.sharding import PartitionSpec as P

FIELDS = 4
CX, CY, CZ = 16, 32, 128
HX, HY = CX // 2, CY // 2
GROUPS = 8
SWEEPS = 4
LOW_BOUND = 0.25
HIGH_BOUND = 2.0
THETA = (HIGH_BOUND + LOW_BOUND) / 2.0
DELTA = (HIGH_BOUND - LOW_BOUND) / 2.0

WX = CX + 4
GX, FY, FO, FN = CX + 12, CY + 24, 8, CY + 8
OWN = slice(FO, FO + CY)
ALL = slice(FO, FO + FN)
FX = CX + 8
MID = (4, CX - 4)
VX = HX + 2
QX, QY, QO = HX + 18, HY + 32, 16
EX = HX + 12
CORNER_AT = {1: 0, 2: 9, 3: 17, 4: 24, 5: 30, 6: 35, 7: 39, 8: 42, 9: 44}
CORNER_LINES = 48
FINE_CORNER_AT = {1: 0, 2: 5, 3: 9, 4: 12}
FINE_CORNER_LINES = (FIELDS + 1) * 32

LAYER_LINES = (FIELDS + 1) * 6 * CY
BAND_LINES = (FIELDS + 1) * 4 * CX
KIN_LINES = FIELDS * GROUPS * 8
COARSE_LINES = 3 * (HX + 1) * HY
FACE_LINES = COARSE_LINES + FIELDS * CY
STRIP_LINES = 272
STRIP_AT = {1: 0, 2: WX, 3: 2 * WX - 2}
SIDE_LINES = STRIP_LINES + FIELDS * (3 * WX - 6)
KNOT_LINES = 6 * CORNER_LINES


def coefficients():
    rho = DELTA / THETA
    pairs = []
    for _ in range(SWEEPS - 1):
        following = 1.0 / (2.0 * THETA / DELTA - rho)
        pairs.append((following * rho, 2.0 * following / DELTA))
        rho = following
    return pairs


def every(low, high, step):
    for i in range(low, high):
        step(i)


def lanes():
    return lax.broadcasted_iota(jnp.int32, (1, CZ), 1)


def beside(ref, f, x, low, count, width, share=1):
    after, before, x = (x + 1) // share, (x - 1) // share, x // share
    here = ref[f, x, low : low + count, :]
    lane = lanes()
    total = ref[f, after, low : low + count, :] + ref[f, before, low : low + count, :]
    total = total + ref[f, x, low + 1 : low + 1 + count, :]
    total = total + ref[f, x, low - 1 : low - 1 + count, :]
    total = total + jnp.where(lane < CZ - width, pltpu.roll(here, CZ - width, 1), 0.0)
    total = total + jnp.where(lane >= width, pltpu.roll(here, width, 1), 0.0)
    return here, total


def diagonal_values(reaction, f):
    low = reaction[2 * f : 2 * f + 1, :]
    jump = reaction[2 * f + 1 : 2 * f + 2, :] - low
    return 6.0 + low, 6.0 + low + jump


def inverse_of(code, reaction, f):
    fluid, solid = diagonal_values(reaction, f)
    fluid, solid = 1.0 / fluid, 1.0 / solid
    return jnp.where(code == 0.0, fluid, jnp.where(code == 1.0, solid, 0.0))


def place():
    return lax.axis_index("row"), lax.axis_index("col")


def by_parity(step, first, second):
    even = lax.rem(lax.axis_index("col"), 2) == 0
    pl.when(even)(functools.partial(step, second, first))
    pl.when(jnp.logical_not(even))(functools.partial(step, first, second))


def pack_layers(
    b, material, inverse, up, down, first, second, own,
    b_here, material_here, inverse_here, solid, first_here, second_here, own_here, sems, out_sems,
):
    copies = [pltpu.make_async_copy(b.at[f], b_here.at[f], sems.at[f]) for f in range(FIELDS)]
    copies.append(pltpu.make_async_copy(material, material_here, sems.at[FIELDS]))
    copies.append(pltpu.make_async_copy(inverse, inverse_here, sems.at[FIELDS + 1]))
    for copy in copies:
        copy.start()
    sent = []

    def send(source, target):
        sent.append(pltpu.make_async_copy(source, target, out_sems.at[len(sent)]))
        sent[-1].start()

    for f in range(FIELDS + 1):
        copies[f].wait()
        layer, band = 6 * CY, 4 * CX
        if f < FIELDS:
            take = lambda start, size, step: b_here[f, pl.ds(start, size, stride=step), :]
            ends = (b_here.at[f, pl.ds((CX - 6) * CY, layer)], b_here.at[f, pl.ds(0, layer)])
        else:
            take = lambda start, size, step: material_here[
                pl.ds(start, size, stride=step), :
            ].astype(jnp.float32)
            solid[0] = take((CX - 6) * CY, layer, 1)
            solid[1] = take(0, layer, 1)
            ends = (solid.at[0], solid.at[1])
        for source, target in zip(ends, (up, down)):
            send(source, target.at[pl.ds(f * layer, layer)])

        def bands(left, right):
            for i in range(4):
                at = f * band + i * CX
                right[at : at + CX, :] = take(CY - 4 + i, CX, CY)
                left[at : at + CX, :] = take(i, CX, CY)

        by_parity(bands, first_here, second_here)
        for source, target in ((first_here, first), (second_here, second)):
            send(source.at[pl.ds(f * band, band)], target.at[pl.ds(f * band, band)])
    copies[FIELDS + 1].wait()
    for f in range(FIELDS):
        for k in range(inverse.shape[2] // CZ):
            at = (f * GROUPS + k) * GROUPS
            own_here[at : at + GROUPS, :] = inverse_here[f, :, k * CZ : (k + 1) * CZ]
    send(own_here, own)
    for copy in sent:
        copy.wait()


def pack_corners(first, second, reaction, up, down, constants):
    for f in range(FIELDS):
        for i in range(2):
            constants[2 * f + i : 2 * f + i + 1, :] = jnp.broadcast_to(
                reaction[i : i + 1, f : f + 1], (1, CZ)
            )

    def pack(low, high):
        for side, ref in enumerate((low, high)):
            for f in range(FIELDS + 1):
                for j, offset in FINE_CORNER_AT.items():
                    size = 6 - j
                    line = (f * 4 + (j - 1 if side else 4 - j)) * CX
                    at = (f * 2 + side) * 16 + offset
                    up[at : at + size, :] = ref[line + CX - size : line + CX, :]
                    down[at : at + size, :] = ref[line : line + size, :]
                at = (f * 2 + side) * 16 + 14
                up[at : at + 2, :] = jnp.zeros((2, CZ), jnp.float32)
                down[at : at + 2, :] = jnp.zeros((2, CZ), jnp.float32)

    by_parity(pack, first, second)


def halo_row(j, is_high):
    return FO + CY - 1 + j if is_high else FO + FN - j


def go_round(ref, f, x, value):
    ref[f, x, ALL, :] = value
    ref[f, x, FO - 1 : FO, :] = value[FN - 1 : FN]
    ref[f, x, FO + FN : FO + FN + 1, :] = value[0:1]


def fine_scale(x, reaction, code, s, inv, p0):
    kind = code[x, ALL, :]
    for f in range(FIELDS):
        inverse = inverse_of(kind, reaction, f)
        inv[f, x, ALL, :] = inverse
        if p0 is not None:
            value = inverse * s[f, x, ALL, :]
            s[f, x, ALL, :] = value
            go_round(p0, f, x, value * (1.0 / THETA))


def fine_sweep(x, k, s, inv, parts):
    keep, gain = coefficients()[k]
    for f in range(FIELDS):
        here, total = beside(parts[k], f, x, FO, FN, 1)
        value = s[f, x, ALL, :] - here + inv[f, x, ALL, :] * total
        s[f, x, ALL, :] = value
        go_round(parts[k + 1], f, x, keep * here + gain * value)


def fine_last(x, reaction, code, s, inv, p3, scaled, line):
    residues = []
    for f in range(FIELDS):
        fluid, solid = diagonal_values(reaction, f)
        here, total = beside(p3, f, x, FO, CY, 1)
        value = s[f, x, OWN, :] - here + inv[f, x, OWN, :] * total
        scaled[f, line : line + CY, :] = value
        residues.append(jnp.where(code[x, OWN, :] == 1.0, solid, fluid) * value)
    return residues


def restrict(x, residues, code, pair, coarse, line):
    parity = lanes() % 2 == 0
    sums = [one + other for one, other in zip(*residues)]
    sums.append(code[x, OWN, :] + code[x + 1, OWN, :])
    halves = []
    for f, value in enumerate(sums):
        here = pair.at[x // 2 % 2, f]
        here[...] = value
        halves.append(here[pl.ds(0, HY, stride=2), :] + here[pl.ds(1, HY, stride=2), :])
    halves.append(halves[4])
    for plane in range(3):
        even, odd = halves[2 * plane], halves[2 * plane + 1]
        merged = jnp.where(
            parity, even + pltpu.roll(even, CZ - 1, 1), odd + pltpu.roll(odd, 1, 1)
        )
        merged = merged * 0.5 if plane < 2 else jnp.where(merged > 8.5, -1.0, merged)
        coarse[plane, line : line + HY, :] = merged


def lay_own(x_at, xs, b, material, s, code):
    zeros = jnp.zeros((8, CZ), jnp.float32)
    for x in xs:
        for f in range(FIELDS):
            s[f, x + x_at, OWN, :] = b[f, x * CY : x * CY + CY, :]
            s[f, x + x_at, FO + CY : FO + FN, :] = zeros
        code[x + x_at, OWN, :] = material[x * CY : x * CY + CY, :].astype(jnp.float32)
        code[x + x_at, FO + CY : FO + FN, :] = zeros + 2.0


def putter(s, code):
    sflat = s.reshape(FIELDS, s.shape[1] * FY, CZ)
    cflat = code.reshape(s.shape[1] * FY, CZ)

    def put(f, x, y_row, size, value):
        to = pl.ds(x * FY + y_row, size, stride=FY)
        if f < FIELDS:
            sflat[f, to, :] = value
        else:
            cflat[to, :] = value

    return put


def lay_bands(x_at, spans, ncol, put, even, odd):
    _, col = place()

    def bands(ref, is_high):
        for f in range(FIELDS + 1):
            for i in range(4):
                at = (f * 4 + i) * CX
                row = halo_row(i + 1 if is_high else 4 - i, is_high)
                for x, size in spans if f < FIELDS else ((0, CX),):
                    put(f, x + x_at, row, size, ref[at + x : at + x + size, :])

    def sides(low, high):
        pl.when(col > 0)(functools.partial(bands, low, 0))
        pl.when(col < ncol - 1)(functools.partial(bands, high, 1))

    by_parity(sides, even, odd)


def kept_lines():
    for side in range(2):
        for k in range(1, SWEEPS):
            flip = lambda x: CX - 1 - x if side else x
            yield side, k, (flip(k), flip(k + 1)), flip(k)


def smooth_middle(
    nrow, ncol, reaction, b, material, even, odd,
    first, scaled, coarse, keep_p, keep_s, keep_sum,
    s, inv, p0, p1, p2, p3, code, pair,
):
    parts = (p0, p1, p2, p3)
    lay_own(0, range(CX), b, material, s, code)
    lay_bands(0, ((0, CX),), ncol, putter(s, code), even, odd)
    every(0, CX, lambda x: fine_scale(x, reaction, code, s, inv, p0))
    for k in range(SWEEPS - 1):
        every(k + 1, CX - k - 1, lambda x: fine_sweep(x, k, s, inv, parts))
        for side, step, lines, line in kept_lines():
            if step == k + 1:
                for f in range(FIELDS):
                    for i, x in enumerate(lines):
                        keep_p[side, k, i, f] = parts[step][f, x]
                    keep_s[side, k, f] = s[f, line, ALL, :]
    for x in range(*MID, 2):
        residues = []
        for h in range(2):
            line = (x + h - MID[0]) * CY
            residues.append(fine_last(x + h, reaction, code, s, inv, p3, scaled, line))
            for f in range(FIELDS):
                first[f, line : line + CY, :] = sum(p[f, x + h, OWN, :] for p in parts)
        restrict(x, residues, code, pair, coarse, (x - MID[0]) // 2 * HY)
    for side in range(2):
        for i in range(1, SWEEPS):
            x = CX - 1 - i if side else i
            for f in range(FIELDS):
                keep_sum[side, i - 1, f] = sum(p[f, x, OWN, :] for p in parts[: i + 1])


def smooth_outer(
    nrow, ncol, reaction, b, material, above, below, even, odd, kabove, kbelow,
    own, kin_even, kin_odd, mid_first, mid_scaled, mid_coarse, keep_p, keep_s, keep_sum,
    first, scaled, code, coarse, up, down, side_even, side_odd, kin,
    s, inv, p0, p1, p2, p3, pair,
):
    row, col = place()
    parts = (p0, p1, p2, p3)
    at_x = 6
    zeros = jnp.zeros((FN, CZ), jnp.float32)
    for x in (*range(6), *range(GX - 6, GX)):
        for f in range(FIELDS):
            s[f, x, ALL, :] = zeros
        code[x, ALL, :] = zeros + 2.0
    outer = (*range(4), *range(CX - 4, CX))
    lay_own(at_x, outer, b, material, s, code)
    for x in range(4, CX - 4):
        code[x + at_x, OWN, :] = material[x * CY : x * CY + CY, :].astype(jnp.float32)
        code[x + at_x, FO + CY : FO + FN, :] = zeros[:8] + 2.0
    put = putter(s, code)

    def rows(first_x, ref):
        for i in range(6):
            for f in range(FIELDS):
                at = (f * 6 + i) * CY
                s[f, first_x + i, OWN, :] = ref[at : at + CY, :]
            at = (FIELDS * 6 + i) * CY
            code[first_x + i, OWN, :] = ref[at : at + CY, :]

    pl.when(row > 0)(functools.partial(rows, 0, above))
    pl.when(row < nrow - 1)(functools.partial(rows, GX - 6, below))
    lay_bands(at_x, ((0, 4), (CX - 4, 4)), ncol, put, even, odd)

    def corners(ref, is_above, is_high):
        for f in range(FIELDS + 1):
            for j, offset in FINE_CORNER_AT.items():
                size = 6 - j
                at = (f * 2 + is_high) * 16 + offset
                x = 6 - size if is_above else 6 + CX
                put(f, x, halo_row(j, is_high), size, ref[at : at + size, :])

    for ref, is_above, in_x in ((kabove, 1, row > 0), (kbelow, 0, row < nrow - 1)):
        for is_high, in_y in ((0, col > 0), (1, col < ncol - 1)):
            pl.when(in_x & in_y)(functools.partial(corners, ref, is_above, is_high))

    def both(low, high, step):
        for x in range(low, high):
            step(x + at_x)
            step(CX - 1 - x + at_x)

    both(-6, 2, lambda x: fine_scale(x, reaction, code, s, inv, p0))
    both(2, 4, lambda x: fine_scale(x, reaction, code, s, inv, None))
    for side, k, lines, line in kept_lines():
        for f in range(FIELDS):
            for i, x in enumerate(lines):
                parts[k][f, x + at_x] = keep_p[side, k - 1, i, f]
    for k in range(SWEEPS - 1):
        if k > 0:
            for side, step, lines, line in kept_lines():
                if step == k:
                    for f in range(FIELDS):
                        s[f, line + at_x, ALL, :] = keep_s[side, k - 1, f]
        both(k - 5, k + 1, lambda x: fine_sweep(x, k, s, inv, parts))
    for side, step, lines, line in kept_lines():
        if step == SWEEPS - 1:
            for f in range(FIELDS):
                s[f, line + at_x, ALL, :] = keep_s[side, step - 1, f]
    for x in (*range(-2, 4, 2), *range(CX - 4, CX + 2, 2)):
        residues = []
        for h in range(2):
            line = (x + h + 2) * CY
            residues.append(
                fine_last(x + h + at_x, reaction, code, s, inv, p3, scaled, line)
            )
        restrict(x + at_x, residues, code, pair, coarse, (x // 2 + 1) * HY)
    for f in range(FIELDS):
        for x in range(CX):
            out = slice(x * CY, x * CY + CY)
            side = x >= CX // 2
            i = CX - 1 - x if side else x
            if i < 4:
                some = [p[f, x + at_x, OWN, :] for p in (parts if i == 0 else parts[i + 1 :])]
                if i > 0:
                    some.append(keep_sum[int(side), i - 1, f])
                first[f, out, :] = sum(some)
            else:
                mid = slice((x - MID[0]) * CY, (x - MID[0] + 1) * CY)
                first[f, out, :] = mid_first[f, mid, :]
                scaled[f, (x + 2) * CY : (x + 3) * CY, :] = mid_scaled[f, mid, :]
    for plane in range(3):
        size = (MID[1] - MID[0]) // 2 * HY
        at = (MID[0] // 2 + 1) * HY
        coarse[plane, at : at + size, :] = mid_coarse[plane]

    for f in range(FIELDS):
        at = COARSE_LINES + f * CY
        up[at : at + CY, :] = scaled[f, (CX - 1) * CY : CX * CY, :]
        down[at : at + CY, :] = scaled[f, 4 * CY : 5 * CY, :]
    for plane in range(3):
        at, size = plane * (HX + 1) * HY, (HX + 1) * HY
        up[at : at + size, :] = coarse[plane, 0:size, :]
        down[at : at + size, :] = coarse[plane, HY : HY + size, :]

    kin[0] = own[...]

    def gather(low, high):
        kin[1] = low[...]
        kin[2] = high[...]

    by_parity(gather, kin_even, kin_odd)

    def strips(left, right):
        for plane in range(3):
            for i in range(9):
                at = (plane * 9 + i) * VX
                right[at : at + VX, :] = coarse[plane, pl.ds(HY - 9 + i, VX, stride=HY), :]
                left[at : at + VX, :] = coarse[plane, pl.ds(i, VX, stride=HY), :]
        for f in range(FIELDS):
            for j, offset in STRIP_AT.items():
                size = WX + 2 - 2 * j
                at = STRIP_LINES + f * (3 * WX - 6) + offset
                x = (j - 1) * CY
                right[at : at + size, :] = scaled[f, pl.ds(x + CY - j, size, stride=CY), :]
                left[at : at + size, :] = scaled[f, pl.ds(x + j - 1, size, stride=CY), :]

    by_parity(strips, side_even, side_odd)


def pack_knots(first, second, up, down):
    def pack(low, high):
        for plane in range(3):
            for side, ref in enumerate((low, high)):
                base = (plane * 2 + side) * CORNER_LINES
                up[base + 40 : base + 48, :] = jnp.zeros((8, CZ), jnp.float32)
                down[base + 40 : base + 48, :] = jnp.zeros((8, CZ), jnp.float32)
                for j, offset in CORNER_AT.items():
                    size = 10 - j
                    line = (plane * 9 + (j - 1 if side else 9 - j)) * VX
                    at = base + offset
                    up[at : at + size, :] = ref[line + VX - 1 - size : line + VX - 1, :]
                    down[at : at + size, :] = ref[line + 1 : line + 1 + size, :]

    by_parity(pack, first, second)


def coarse_constants(reaction, plane):
    parity = lanes() % 2 == 0
    even, odd = (
        [reaction[2 * f + i : 2 * f + i + 1, :] for i in range(2)]
        for f in (2 * plane, 2 * plane + 1)
    )
    low = jnp.where(parity, even[0], odd[0])
    return 8.0 * low, jnp.where(parity, even[1] - even[0], odd[1] - odd[0])


def smooth_coarse(
    nrow, ncol, reaction, coarse, above, below, even, odd, kabove, kbelow,
    start, scaled, inverse_out, sums,
    s, inv, count, p0, p1, p2, p3,
):
    row, col = place()
    parts = (p0, p1, p2, p3)
    zeros = jnp.zeros((QY, CZ), jnp.float32)

    def clear(x):
        for plane in range(2):
            s[plane, x] = zeros
        count[x] = zeros - 1.0

    every(0, QX, clear)
    sflat = s.reshape(2, QX * QY, CZ)
    cflat = count.reshape(QX * QY, CZ)

    def put(plane, start_row, size, value):
        if plane < 2:
            sflat[plane, pl.ds(start_row, size, stride=QY), :] = value
        else:
            cflat[pl.ds(start_row, size, stride=QY), :] = value

    def block(plane, x, value):
        if plane < 2:
            s[plane, x, QO : QO + HY, :] = value
        else:
            count[x, QO : QO + HY, :] = value

    def rows(first_x, ref):
        for plane in range(3):
            for i in range(HX + 1):
                at = (plane * (HX + 1) + i) * HY
                block(plane, first_x + i, ref[at : at + HY, :])

    for plane in range(3):
        for i in range(HX):
            block(plane, 9 + i, coarse[plane, (i + 1) * HY : (i + 2) * HY, :])
    pl.when(row > 0)(functools.partial(rows, 0, above))
    pl.when(row < nrow - 1)(functools.partial(rows, 9 + HX, below))

    def strips(ref, first_y):
        for plane in range(3):
            for i in range(9):
                line = (plane * 9 + i) * VX
                put(plane, 9 * QY + first_y + i, HX, ref[line + 1 : line + 1 + HX, :])

    def sides(low, high):
        pl.when(col > 0)(functools.partial(strips, low, QO - 9))
        pl.when(col < ncol - 1)(functools.partial(strips, high, QO + HY))

    by_parity(sides, even, odd)

    def corners(ref, is_above, is_high):
        for plane in range(3):
            base = (plane * 2 + is_high) * CORNER_LINES
            for j, at in CORNER_AT.items():
                size = 10 - j
                x = 9 - size if is_above else 9 + HX
                y = QO + HY - 1 + j if is_high else QO - j
                put(plane, x * QY + y, size, ref[base + at : base + at + size, :])

    for ref, is_above, in_x in ((kabove, 1, row > 0), (kbelow, 0, row < nrow - 1)):
        for is_high, in_y in ((0, col > 0), (1, col < ncol - 1)):
            pl.when(in_x & in_y)(functools.partial(corners, ref, is_above, is_high))

    def scale(x):
        number = count[x]
        for plane in range(2):
            low8, jump = coarse_constants(reaction, plane)
            inverse = jnp.where(number < 0.0, 0.0, 1.0 / (6.0 + 0.5 * (low8 + jump * number)))
            value = inverse * s[plane, x]
            inv[plane, x] = inverse
            s[plane, x] = value
            p0[plane, x] = value * (1.0 / THETA)

    every(0, QX, scale)

    for k, (keep, gain) in enumerate(coefficients()):
        def sweep(x):
            for plane in range(2):
                here, total = beside(parts[k], plane, x, 8, 32, 2)
                value = s[plane, x, 8:40, :] - here + inv[plane, x, 8:40, :] * total
                s[plane, x, 8:40, :] = value
                parts[k + 1][plane, x, 8:40, :] = keep * here + gain * value

        every(k + 1, QX - k - 1, sweep)

    def finish(x):
        for plane in range(2):
            here, total = beside(p3, plane, x, 8, 32, 2)
            value = s[plane, x, 8:40, :] - here + inv[plane, x, 8:40, :] * total
            scaled[plane, x - 4] = value
            inverse_out[plane, x - 4] = inv[plane, x, 8:40, :]

    every(4, QX - 4, finish)

    def add(x):
        for plane in range(2):
            start[plane, x - 7] = (
                p0[plane, x, 8:40, :] + p1[plane, x, 8:40, :]
                + p2[plane, x, 8:40, :] + p3[plane, x, 8:40, :]
            )

    every(7, QX - 7, add)

    lane = lanes()
    message = jnp.zeros((8, CZ), jnp.float32)
    for plane in range(2):
        low8, jump = coarse_constants(reaction, plane)
        total = jnp.zeros((HY, CZ), jnp.float32)
        for x in range(9, 9 + HX):
            diagonal = 6.0 + 0.5 * (low8 + jump * count[x, QO : QO + HY, :])
            total = total + diagonal * scaled[plane, x - 4, 8 : 8 + HY, :]
        total = total[:8] + total[8:]
        for shift in (4, 2, 1):
            total = total + pltpu.roll(total, shift, 0)
        for shift in (2, 4, 8):
            total = total + pltpu.roll(total, CZ - shift, 1)
        for odd in range(2):
            for g in range(GROUPS):
                to = (2 * plane + odd) * GROUPS + g
                moved = pltpu.roll(total, (to - 16 * g - odd) % CZ, 1)
                message = jnp.where(lane == to, moved, message)
    sums[...] = jnp.broadcast_to(message[:1], sums.shape)


def smooth_second(
    nrow, ncol, reaction, gathered, kin, kin_above, kin_below,
    start, qscaled, qinverse, first, scaled, code, above, below, even, odd,
    out,
    wide, spread, e, q0, q1, q2, q3, qs, fs, inv, f0, p0, p1, p2, out_here, sems,
):
    row, col = place()
    lane = lanes()
    width = ncol * GROUPS
    fields = [jnp.zeros((nrow, CZ), jnp.float32) for _ in range(FIELDS)]
    for c in range(ncol):
        some = gathered[pl.ds(c, nrow, stride=ncol), :]
        for f in range(FIELDS):
            moved = pltpu.roll(some, (c * GROUPS - f * GROUPS) % CZ, 1)
            here = (lane >= c * GROUPS) & (lane < (c + 1) * GROUPS)
            fields[f] = jnp.where(here, moved, fields[f])
    for f in range(FIELDS):
        wide[f] = fields[f]

    group = lax.broadcasted_iota(jnp.int32, (GROUPS, CZ), 0)
    spot = lax.broadcasted_iota(jnp.int32, (GROUPS, CZ), 1)
    mask = [(spot // 16 == group) & (spot % 2 == odd) for odd in range(2)]

    def product(rows_of, f):
        total = jnp.zeros((GROUPS, width), jnp.float32)
        for k in range(nrow):
            total = total + rows_of(f, k) * wide[f, k : k + 1, 0:width]
        return jnp.sum(total, axis=1, keepdims=True)

    def neighbour(rows_of, dx, dy, inside):
        for plane in range(2):
            even = product(rows_of, 2 * plane)
            odd = product(rows_of, 2 * plane + 1)
            full = jnp.where(mask[0], even, jnp.where(mask[1], odd, 0.0))
            line = jnp.sum(full, axis=0, keepdims=True)
            if inside is not None:
                line = jnp.where(inside, line, 0.0)
            x_from, x_to = {-1: (0, 6), 0: (6, 6 + HX), 1: (6 + HX, EX)}[dx]
            y_from, y_to = {-1: (8, QO), 0: (QO, QO + HY), 1: (QO + HY, QO + HY + 8)}[dy]
            for x in range(x_from, x_to):
                e[plane, x, y_from:y_to, :] = jnp.broadcast_to(line, (y_to - y_from, CZ))

    def slab(ref, part):
        def rows_of(f, k):
            at = (f * GROUPS + k) * GROUPS
            return ref[part, at : at + GROUPS, :]

        return rows_of

    in_x = {-1: row > 0, 0: True, 1: row < nrow - 1}
    in_y = {-1: col > 0, 0: True, 1: col < ncol - 1}
    for dx, ref in ((0, kin), (-1, kin_above), (1, kin_below)):
        for part, dy in enumerate((0, -1, 1)):
            inside = in_x[dx] & in_y[dy] if (dx, dy) != (0, 0) else None
            neighbour(slab(ref, part), dx, dy, inside)

    parts = (q0, q1, q2, q3)

    def begin(x):
        for plane in range(2):
            here, total = beside(e, plane, x, 8, 32, 2)
            value = qscaled[plane, x - 1] - here + qinverse[plane, x - 1] * total
            qs[plane, x] = value
            q0[plane, x, 8:40, :] = value * (1.0 / THETA)

    every(1, EX - 1, begin)
    for k, (keep, gain) in enumerate(coefficients()):
        def sweep(x):
            for plane in range(2):
                here, total = beside(parts[k], plane, x, 8, 32, 2)
                value = qs[plane, x] - here + qinverse[plane, x - 1] * total
                qs[plane, x] = value
                parts[k + 1][plane, x, 8:40, :] = keep * here + gain * value

        every(k + 2, EX - k - 2, sweep)

    parity = lane % 2 == 0

    def lift(i):
        for plane in range(2):
            total = start[plane, i] + e[plane, i + 4, 8:40, :]
            total = total + q0[plane, i + 4, 8:40, :] + q1[plane, i + 4, 8:40, :]
            total = total + q2[plane, i + 4, 8:40, :] + q3[plane, i + 4, 8:40, :]
            for odd in range(2):
                if odd:
                    value = jnp.where(parity, pltpu.roll(total, CZ - 1, 1), total)
                else:
                    value = jnp.where(parity, total, pltpu.roll(total, 1, 1))
                some = spread.at[i % 2, 2 * plane + odd]
                some[...] = value
                high, low = some[8:26, :], some[6:8, :]
                to = f0.at[2 * plane + odd, i]
                for y in range(2):
                    to[pl.ds(FO + y, 18, stride=2), :] = high
                    to[pl.ds(FO + FN - 4 + y, 2, stride=2), :] = low
                to[FO - 1 : FO, :] = low[1:2]
                to[FO + FN : FO + FN + 1, :] = high[0:1]

    every(0, HX + 4, lift)

    zeros = jnp.zeros((FN, CZ), jnp.float32)
    for f in range(FIELDS):
        for x in (1, FX - 2):
            fs[f, x, ALL, :] = zeros
        for x in range(2, FX - 2):
            fs[f, x, OWN, :] = scaled[f, (x - 2) * CY : (x - 1) * CY, :]
            fs[f, x, FO + CY : FO + FN, :] = zeros[:8]
    sflat = fs.reshape(FIELDS, FX * FY, CZ)

    def face(x, ref):
        for f in range(FIELDS):
            at = COARSE_LINES + f * CY
            fs[f, x, OWN, :] = ref[at : at + CY, :]

    pl.when(in_x[-1])(functools.partial(face, 1, above))
    pl.when(in_x[1])(functools.partial(face, FX - 2, below))

    def strips(ref, is_high):
        for f in range(FIELDS):
            for j, offset in STRIP_AT.items():
                size = WX + 2 - 2 * j
                at = STRIP_LINES + f * (3 * WX - 6) + offset
                start = (1 + j) * FY + halo_row(j, is_high)
                sflat[f, pl.ds(start, size, stride=FY), :] = ref[at : at + size, :]

    def sides(low, high):
        pl.when(in_y[-1])(functools.partial(strips, low, 0))
        pl.when(in_y[1])(functools.partial(strips, high, 1))

    by_parity(sides, even, odd)

    parts = (p0, p1, p2)

    def open_fine(x):
        kind = code[x + 2, ALL, :]
        for f in range(FIELDS):
            here, total = beside(f0, f, x, FO, FN, 1, 2)
            inverse = inverse_of(kind, reaction, f)
            inv[f, x, ALL, :] = inverse
            value = fs[f, x, ALL, :] - here + inverse * total
            fs[f, x, ALL, :] = value
            go_round(p0, f, x, value * (1.0 / THETA))

    every(1, FX - 1, open_fine)
    for k in range(2):
        every(k + 2, FX - k - 2, lambda x: fine_sweep(x, k, fs, inv, parts))

    keep, gain = coefficients()[2]

    sent = []
    part = CX // 2
    for f in range(FIELDS):
        for i in range(CX):
            x = i + 4
            at = slice(i * CY, i * CY + CY)
            here, total = beside(p2, f, x, FO, CY, 1)
            value = fs[f, x, OWN, :] - here + inv[f, x, OWN, :] * total
            result = first[f, at, :] + f0[f, x // 2, OWN, :] + p0[f, x, OWN, :]
            result = result + p1[f, x, OWN, :] + here
            out_here[f, at, :] = result + (keep * here + gain * value)
            if i % part == part - 1:
                lines = pl.ds((i + 1 - part) * CY, part * CY)
                copy = pltpu.make_async_copy(
                    out_here.at[f, lines], out.at[f, lines], sems.at[len(sent)]
                )
                copy.start()
                sent.append(copy)
    for copy in sent:
        copy.wait()


def call(kernel, out_shapes, scratch, *args, limit=16, in_hbm=False, out_hbm=False, microseconds=0.1):
    vmem = pl.BlockSpec(memory_space=pltpu.VMEM)
    hbm = pl.BlockSpec(memory_space=pltpu.HBM)
    given, taken = hbm if in_hbm else vmem, hbm if out_hbm else vmem
    return pl.pallas_call(
        kernel,
        out_shape=[jax.ShapeDtypeStruct(shape, jnp.float32) for shape in out_shapes],
        in_specs=[given] * len(args),
        out_specs=[taken] * len(out_shapes),
        scratch_shapes=[
            pltpu.VMEM(shape, jnp.float32) if isinstance(shape, tuple) else shape
            for shape in scratch
        ],
        cost_estimate=pl.CostEstimate(
            flops=int(microseconds * 1e6), bytes_accessed=int(microseconds * 3.5e6), transcendentals=0
        ),
        compiler_params=pltpu.CompilerParams(vmem_limit_bytes=int(limit * 1024 * 1024)),
    )(*args)


def ahead(value):
    count = lax.axis_size("row")
    return lax.ppermute(value, "row", [(i, (i + 1) % count) for i in range(count)])


def back(value):
    count = lax.axis_size("row")
    return lax.ppermute(value, "row", [((i + 1) % count, i) for i in range(count)])


def pairs(value, odd):
    nrow, ncol = lax.axis_size("row"), lax.axis_size("col")
    moves = []
    for r in range(nrow):
        for c in range(ncol):
            if not odd:
                to = (r, c ^ 1)
            elif c in (0, ncol - 1):
                to = (r ^ 1, c)
            else:
                to = (r, c + 1 if c % 2 else c - 1)
            moves.append((r * ncol + c, to[0] * ncol + to[1]))
    return lax.ppermute(value, ("row", "col"), moves)


def body(right_side, material, reaction, coarse_inverse):
    nrow, ncol = lax.axis_size("row"), lax.axis_size("col")
    b = right_side.reshape(FIELDS, CX * CY, CZ)
    material = material.reshape(CX * CY, CZ)

    fine = (FIELDS, CX * CY, CZ)
    up, down, even, odd, own = call(
        pack_layers,
        [(LAYER_LINES, CZ)] * 2 + [(BAND_LINES, CZ)] * 2 + [(KIN_LINES, CZ)],
        [fine, pltpu.VMEM(fine[1:], jnp.int32), coarse_inverse.shape,
         (2, 6 * CY, CZ), (BAND_LINES, CZ), (BAND_LINES, CZ), (KIN_LINES, CZ),
         pltpu.SemaphoreType.DMA((FIELDS + 2,)), pltpu.SemaphoreType.DMA((4 * FIELDS + 5,))],
        b, material, coarse_inverse,
        in_hbm=True, out_hbm=True, limit=59.27,
    )
    odd, even = pairs(odd, True), pairs(even, False)
    above, below = ahead(up), back(down)
    even, odd, above = lax.optimization_barrier((even, odd, above))
    up, down, reaction = call(
        pack_corners, [(FINE_CORNER_LINES, CZ)] * 2 + [(2 * FIELDS, CZ)], [],
        even, odd, reaction.T,
    )
    kabove, kbelow = ahead(up), back(down)
    kin_odd, kin_even = pairs(own, True), pairs(own, False)

    wide = (FIELDS, WX * CY, CZ)
    middle = MID[1] - MID[0]
    padded = (FIELDS, CX, FY, CZ)
    mids = call(
        functools.partial(smooth_middle, nrow, ncol),
        [(FIELDS, middle * CY, CZ)] * 2 + [(3, middle // 2 * HY, CZ),
         (2, 3, 2, FIELDS, FY, CZ), (2, 3, FIELDS, FN, CZ), (2, 3, FIELDS, CY, CZ)],
        [padded] * 6 + [padded[1:], (2, FIELDS + 1, CY, CZ)],
        reaction, b, material, even, odd,
        limit=16, microseconds=100,
    )
    padded = (FIELDS, GX, FY, CZ)
    first, scaled, code, coarse, up, down, side_even, side_odd, kin = call(
        functools.partial(smooth_outer, nrow, ncol),
        [fine, wide, padded[1:], (3, VX * HY, CZ)]
        + [(FACE_LINES, CZ)] * 2 + [(SIDE_LINES, CZ)] * 2 + [(3, KIN_LINES, CZ)],
        [padded] * 6 + [(2, FIELDS + 1, CY, CZ)],
        reaction, b, material, above, below, even, odd, kabove, kbelow, own, kin_even, kin_odd, *mids,
        limit=26,
    )
    odd, even = pairs(side_odd, True), pairs(side_even, False)
    above, below = ahead(up), back(down)
    kin_above, kin_below = ahead(kin), back(kin)
    up, down = call(pack_knots, [(KNOT_LINES, CZ)] * 2, [], even, odd, microseconds=100)
    kabove, kbelow = ahead(up), back(down)

    qpadded = (2, QX, QY, CZ)
    start, qscaled, qinverse, sums = call(
        functools.partial(smooth_coarse, nrow, ncol),
        [(2, HX + 4, 32, CZ), (2, HX + 10, 32, CZ), (2, HX + 10, 32, CZ), (nrow * ncol, CZ)],
        [qpadded, qpadded, qpadded[1:]] + [qpadded] * 4,
        reaction, coarse, above, below, even, odd, kabove, kbelow,
        limit=14, microseconds=2.5,
    )

    sums, kin_above, kin_below = lax.optimization_barrier((sums, kin_above, kin_below))
    gathered = lax.all_to_all(sums, ("row", "col"), 0, 0)

    epadded = (2, EX, QY, CZ)
    padded = (FIELDS, FX, FY, CZ)
    (out,) = call(
        functools.partial(smooth_second, nrow, ncol),
        [fine],
        [(FIELDS, nrow, CZ), (2, FIELDS, 32, CZ)] + [epadded] * 5 + [(2, EX, 32, CZ)] + [padded] * 2
        + [(FIELDS, FX // 2, FY, CZ)] + [padded] * 3 + [fine, pltpu.SemaphoreType.DMA((2 * FIELDS,))],
        reaction, gathered, kin, kin_above, kin_below,
        start, qscaled, qinverse, first, scaled, code, above, below, even, odd,
        limit=30, microseconds=7, out_hbm=True,
    )
    return out.reshape(right_side.shape)


def solution(mesh):
    placed = (
        P(None, "row", "col", None),
        P("row", "col", None),
        P(),
        P(None, ("row", "col"), None),
    )
    return jax.shard_map(
        body, mesh=mesh, in_specs=placed, out_specs=P(None, "row", "col", None), check_vma=False
    )
```
